256 devices in a mesh: gx: 16 (over y, x), gz: 16 (over z, core).
Axes of the slice: x: 4, y: 4, z: 8, core: 2. Of those that a mesh axis runs over, the one named last changes fastest.
Arguments:
- phase: float32 [4, 256, 256, 512], P(None, 'gx', 'gz'), may hold values from 0 to 1
- solute: float32 [256, 256, 512], P('gx', 'gz'), may hold values from -3 to 3
- grain_map: int32 [4, 256, 256, 512], P(None, 'gx', 'gz'), may hold values from 0 to 1023
- frame_steps: int32 [2], replicated, may hold values from 0 to 15
Outputs:
- phase_out: float32 [4, 256, 256, 512], P(None, 'gx', 'gz')
- solute_out: float32 [256, 256, 512], P('gx', 'gz')
The draws below stay inside these ranges and needn't reach their ends.
All inputs are finite; a program needn't handle non-finite values.
Results may differ from the reference program's by a relative error of at most 0.0003.
Values sent between devices are 32-bit elements; how exact they have to be, the bound alone decides.
A program may use at most 128 MiB of HBM per device.

```python
import math
import jax
import jax.numpy as jnp
from jax import lax

ORDERS = 4
STEPS = 2
NGRAIN = 1024
SHIFT_SPAN = 16
CX = 16
NY = 512
NX = 256
NZ = 256
N_GX = 16


def set_ends(drawn, stream_key, low, top_value):
    extent = drawn.shape
    spot = [jax.random.randint(jax.random.fold_in(stream_key, axis), (), 0, extent[axis]) for axis in range(len(extent))]
    drawn = drawn.at[tuple(spot)].set(low)
    longest = extent.index(max(extent))
    spot[longest] = (spot[longest] + 1) % extent[longest]
    return drawn.at[tuple(spot)].set(top_value)


def block_levels(key, shape, shards, least, high):
    level, own = 1.0, jax.random.fold_in(key, 6)
    for position, parts in shards:
        heights = jnp.exp(jax.random.uniform(jax.random.fold_in(own, position), (parts,), jnp.float32, least / len(shards), high / len(shards)))
        level = level * jnp.repeat(heights, shape[position] // parts).reshape([-1 if axis == position else 1 for axis in range(len(shape))])
    return level


def scatter_about(key, dims, deviation, limit, shards=(), kind=jnp.bfloat16):
    result = deviation * jax.random.normal(key, dims, jnp.float32)
    if shards:
        result = result * block_levels(key, dims, shards, -0.22, 0.18)
    return jnp.clip(result, -limit, limit).astype(kind)


def setup_inputs(seed: int = 0) -> dict:
    key_list = jax.random.split(jax.random.key(seed), 5)
    return {
        "phase": jnp.clip(1.0 * jax.random.uniform(key_list[0], (ORDERS, NX, NZ, NY), jnp.float32) ** block_levels(key_list[0], (ORDERS, NX, NZ, NY), ((1, 16), (2, 16)), -0.2, 0.2), 0.0, 1.0),
        "solute": scatter_about(key_list[1], (NX, NZ, NY), 0.5, 3.0, ((0, 16), (1, 16)), jnp.float32),
        "grain_map": set_ends(jax.random.randint(key_list[2], (ORDERS, NX, NZ, NY), 0, NGRAIN), jax.random.fold_in(key_list[2], 1), 0, NGRAIN - 1).astype(jnp.int32),
        "frame_steps": jax.random.randint(key_list[3], (STEPS,), 0, SHIFT_SPAN).astype(jnp.int32),
    }


time_step = 0.08
aniso_strength = 0.5
grad_floor = 0.05
well_height = 8.0
intersection_penalty = 2.0
drive_gain = 1.0
solute_diffusion = 1.0
rejection = 0.5
thermal_length = 8.0


def core(ext, grains, offset, zglob, center_plane):
    center = ext[:, 1:-1, 1:-1]
    x_low = ext[:, :-2, 1:-1]
    x_high = ext[:, 2:, 1:-1]
    z_low = ext[:, 1:-1, :-2]
    z_high = ext[:, 1:-1, 2:]
    y_low = jnp.roll(center, 1, axis=3)
    y_high = jnp.roll(center, -1, axis=3)
    lap = x_low + x_high + z_low + z_high + y_low + y_high - 6.0 * center
    phase = center[:ORDERS]
    solute = center[ORDERS]
    grad_x = 0.5 * (x_high[:ORDERS] - x_low[:ORDERS])
    grad_y = 0.5 * (y_high[:ORDERS] - y_low[:ORDERS])
    grad_z = 0.5 * (z_high[:ORDERS] - z_low[:ORDERS])
    angle = grains.astype(jnp.float32) * (2.0 * math.pi / NGRAIN)
    cosine = jnp.cos(angle)
    sine = jnp.sin(angle)
    rot_x = cosine * grad_x + sine * grad_y
    rot_y = cosine * grad_y - sine * grad_x
    squares = grad_x * grad_x + grad_y * grad_y + grad_z * grad_z
    quartic = rot_x ** 4 + rot_y ** 4 + grad_z ** 4
    aniso = 1.0 + aniso_strength * quartic / (squares + grad_floor) ** 2
    intersection = jnp.sum(phase * phase, axis=0)
    well = phase * (1.0 - phase) * (1.0 - 2.0 * phase)
    shape_fn = 30.0 * phase * phase * (1.0 - phase) * (1.0 - phase)
    height = (center_plane - zglob - offset).astype(jnp.float32)
    drive = jnp.tanh(height / thermal_length)[None, :, None] - solute
    delta = time_step * (aniso * lap[:ORDERS] + well_height * well
                         - intersection_penalty * phase * (intersection - phase * phase)
                         + drive_gain * shape_fn * drive)
    solute_new = solute + time_step * solute_diffusion * lap[ORDERS] + rejection * jnp.sum(delta, axis=0)
    return jnp.concatenate([phase + delta, solute_new[None]], axis=0)


def reference(phase, solute, grain_map, frame_steps):
    state = jnp.concatenate([phase, solute[None]], axis=0)
    zglob = jnp.arange(NZ, dtype=jnp.int32)
    for step in range(STEPS):
        full = jnp.pad(state, ((0, 0), (1, 1), (0, 0), (0, 0)), mode="wrap")
        full = jnp.pad(full, ((0, 0), (0, 0), (1, 1), (0, 0)))

        def block(index):
            start = (index * CX).astype(jnp.int32)
            ext = lax.dynamic_slice_in_dim(full, start, CX + 2, 1)
            grains = lax.dynamic_slice_in_dim(grain_map, start, CX, 1)
            return core(ext, grains, frame_steps[step], zglob, NZ // 2)

        blocks = lax.map(block, jnp.arange(N_GX, dtype=jnp.int32))
        state = jnp.moveaxis(blocks, 0, 1).reshape(ORDERS + 1, NX, NZ, NY)
    shifted = jnp.concatenate([state[:, :, 1:], jnp.zeros_like(state[:, :, :1])], axis=2)
    return shifted[:ORDERS], shifted[ORDERS]
```

```python
import math

import jax
import jax.numpy as jnp
import numpy as np
from jax import lax
from jax.experimental import pallas as pl
from jax.experimental.pallas import tpu as pltpu
from jax.sharding import PartitionSpec as P

ORDERS = 4
FIELDS = 5
STEPS = 2
NGRAIN = 1024
NZ = 256
CX = 16
CZ = 16
NY = 512
LANES = 128
YT = NY // LANES
GROUP = 4
GROUPS = CX // GROUP
MESH = pl.DeviceIdType.MESH

BASE0 = 8


def sine_coefficients():
    nodes = np.cos(np.pi * (np.arange(400) + 0.5) / 400)
    theta = nodes * np.pi / 2
    even = np.polynomial.chebyshev.Chebyshev.fit(nodes, np.cos(theta), 8, domain=[-1, 1])
    odd = np.polynomial.chebyshev.Chebyshev.fit(nodes, np.sin(theta), 9, domain=[-1, 1])
    even = even.convert(kind=np.polynomial.Polynomial).coef
    odd = odd.convert(kind=np.polynomial.Polynomial).coef
    cos_c = [float(even[i] * math.sqrt(0.5) / 128.0**i) for i in (0, 2, 4, 6, 8)]
    sin_c = [float(odd[i] * math.sqrt(2.0) / 128.0**i) for i in (1, 3, 5, 7, 9)]
    return sin_c, cos_c


SIN_C, COS_C = sine_coefficients()


def horner(x, coefficients):
    value = coefficients[-1]
    for c in coefficients[-2::-1]:
        value = value * x + c
    return value


def next_y(rolled, offset):
    if offset > 0:
        return jnp.concatenate([rolled[1:], rolled[:1]], axis=0)
    return jnp.concatenate([rolled[-1:], rolled[:-1]], axis=0)


def neighbours(s, f, xi, row):
    at = pl.ds(row, 8)
    c = s[f, xi, :, at, :]
    xl = s[f, xi - 1, :, at, :]
    xh = s[f, xi + 1, :, at, :]
    zl = s[f, xi, :, pl.ds(row - 1, 8), :]
    zh = s[f, xi, :, pl.ds(row + 1, 8), :]
    lane = lax.broadcasted_iota(jnp.int32, c.shape, 2)
    right = pltpu.roll(c, 1, axis=2)
    left = pltpu.roll(c, LANES - 1, axis=2)
    yl = jnp.where(lane == 0, next_y(right, -1), right)
    yh = jnp.where(lane == LANES - 1, next_y(left, 1), left)
    return c, xl, xh, yl, yh, zl, zh


def advance(s, cs, x, row, cs_row, thermal, put):
    xi = x + 1
    u = s[ORDERS, xi, :, pl.ds(row, 8), :]
    drive = thermal - 2.4 * u
    q = None
    for k in range(ORDERS):
        p = s[k, xi, :, pl.ds(row, 8), :]
        q = p * p if q is None else q + p * p
    well = 0.64 - 0.16 * q
    total = None
    for k in range(ORDERS):
        p, xl, xh, yl, yh, zl, zh = neighbours(s, k, xi, row)
        gx, gy, gz = xh - xl, yh - yl, zh - zl
        lap = (xl + xh) + (yl + yh) + (zl + zh) - 6.0 * p
        x2, y2, z2 = gx * gx, gy * gy, gz * gz
        r = x2 + y2
        at = pl.ds(cs_row, 8)
        t = cs[0, k, x, :, at, :] * (gx * gy) + cs[1, k, x, :, at, :] * (x2 - y2)
        quartic = r * r + z2 * z2 - t * t
        d = (r + z2) + 0.2
        ratio = quartic * pl.reciprocal(d * d, approx=True)
        w = p - p * p
        delta = (
            lap * (0.08 + 0.04 * ratio)
            + p * (well + p * (1.44 * p - 1.92))
            + (w * w) * drive
        )
        put(k, p + delta)
        total = delta if total is None else total + delta
    c, xl, xh, yl, yh, zl, zh = neighbours(s, ORDERS, xi, row)
    near = (xl + xh) + (yl + yh) + (zl + zh)
    put(ORDERS, 0.52 * c + 0.08 * near + 0.5 * total)


def kernel(
    frames, phase, solute, grain, phase_out, solute_out,
    s0, s1, g, cs, o,
    load_sem, out_sem, x_send, x_recv, z_send, z_recv, m_send, m_recv, c_send, c_recv, d_send, d_recv,
):
    gx, gz = lax.axis_index("gx"), lax.axis_index("gz")
    n_gx, n_gz = lax.axis_size("gx"), lax.axis_size("gz")
    right, left = lax.rem(gx + 1, n_gx), lax.rem(gx + n_gx - 1, n_gx)
    has_up, has_down = gz < n_gz - 1, gz > 0

    loads = []
    for k in range(YT):
        lanes = pl.ds(k * LANES, LANES)
        rows = pl.ds(BASE0, CZ)
        loads.append(
            (
                pltpu.make_async_copy(
                    phase.at[:, :, :, lanes], s0.at[pl.ds(0, ORDERS), pl.ds(1, CX), k, rows, :], load_sem.at[0, k]
                ),
                pltpu.make_async_copy(
                    solute.at[:, :, lanes], s0.at[ORDERS, pl.ds(1, CX), k, rows, :], load_sem.at[1, k]
                ),
                pltpu.make_async_copy(grain.at[:, :, :, lanes], g.at[:, :, k, :, :], load_sem.at[2, k]),
            )
        )
    for which in range(3):
        for k in range(YT):
            loads[k][which].start()

    barrier = pltpu.get_barrier_semaphore()

    def greet(ix, iz):
        pl.semaphore_signal(barrier, inc=1, device_id=(ix, iz), device_id_type=MESH)

    greet(left, gz)
    greet(right, gz)

    @pl.when(has_up)
    def _():
        greet(gx, gz + 1)
        greet(left, gz + 1)
        greet(right, gz + 1)

    @pl.when(has_down)
    def _():
        greet(gx, gz - 1)
        greet(left, gz - 1)
        greet(right, gz - 1)

    @pl.when(jnp.logical_not(has_down))
    def _():
        s0[:, :, :, pl.ds(BASE0 - 1, 1), :] = jnp.zeros((FIELDS, CX + 2, YT, 1, LANES), jnp.float32)

    @pl.when(jnp.logical_not(has_up))
    def _():
        s0[:, :, :, pl.ds(BASE0 + CZ, 1), :] = jnp.zeros((FIELDS, CX + 2, YT, 1, LANES), jnp.float32)
        s1[:, :, :, pl.ds(CZ, 2), :] = jnp.zeros((FIELDS, CX + 2, YT, 2, LANES), jnp.float32)
        cs[:, :, :, :, pl.ds(CZ, 1), :] = jnp.zeros((2, ORDERS, CX, YT, 1, LANES), jnp.float32)

    def remote(src, dst, send, recv, ix, iz):
        return pltpu.make_async_remote_copy(
            src_ref=src, dst_ref=dst, send_sem=send, recv_sem=recv, device_id=(ix, iz), device_id_type=MESH
        )

    def x_copy(step, way):
        s, rows = (s0, pl.ds(BASE0, CZ)) if step == 0 else (s1, pl.ds(0, CZ))
        src, dst, to = (CX, 0, right) if way == 0 else (1, CX + 1, left)
        return remote(
            s.at[:, src, :, rows, :], s.at[:, dst, :, rows, :], x_send.at[step, way], x_recv.at[step, way], to, gz
        )

    def z_copy(group, way):
        planes = pl.ds(1 + group * GROUP, GROUP)
        src, dst, to = (BASE0 + CZ - 1, BASE0 - 1, gz + 1) if way == 0 else (BASE0, BASE0 + CZ, gz - 1)
        return remote(
            s0.at[:, planes, :, pl.ds(src, 1), :],
            s0.at[:, planes, :, pl.ds(dst, 1), :],
            z_send.at[way, group],
            z_recv.at[way, group],
            gx,
            to,
        )

    def m_copy(group):
        planes = pl.ds(1 + group * GROUP, GROUP)
        return remote(
            s1.at[:, planes, :, pl.ds(0, 2), :],
            s1.at[:, planes, :, pl.ds(CZ, 2), :],
            m_send.at[group],
            m_recv.at[group],
            gx,
            gz - 1,
        )

    def d_copy(way):
        src, dst, to = (CX, 0, right) if way == 0 else (1, CX + 1, left)
        return remote(
            s1.at[:, src, :, pl.ds(0, 1), :],
            s1.at[:, dst, :, pl.ds(CZ, 1), :],
            d_send.at[way],
            d_recv.at[way],
            to,
            gz - 1,
        )

    def c_copy():
        return remote(
            cs.at[:, :, :, :, pl.ds(0, 1), :], cs.at[:, :, :, :, pl.ds(CZ, 1), :], c_send, c_recv, gx, gz - 1
        )

    for which in range(2):
        for k in range(YT):
            loads[k][which].wait()

    pl.semaphore_wait(barrier, 2 + 3 * (has_up.astype(jnp.int32) + has_down.astype(jnp.int32)))

    x_copy(0, 0).start()
    x_copy(0, 1).start()
    order = (1, 2, 3, 0)
    for group in order:

        @pl.when(has_up)
        def _(group=group):
            z_copy(group, 0).start()

        @pl.when(has_down)
        def _(group=group):
            z_copy(group, 1).start()

    for k in range(YT):
        loads[k][2].wait()

    def trig(x, carry):
        for k in range(ORDERS):
            for half in range(2):
                at = pl.ds(8 * half, 8)
                h = ((g[k, x, :, at, :] & 255) - 128).astype(jnp.float32)
                h2 = h * h
                cs[0, k, x, :, at, :] = h * horner(h2, SIN_C)
                cs[1, k, x, :, at, :] = horner(h2, COS_C)
        return carry

    lax.fori_loop(0, CX, trig, 0)

    @pl.when(has_down)
    def _():
        c_copy().start()

    def thermal(step, first):
        z = gz * CZ + first + lax.broadcasted_iota(jnp.int32, (1, 8, LANES), 1)
        height = (NZ // 2 - z - frames[step]).astype(jnp.float32)
        return 2.4 * jnp.tanh(height * 0.125)

    heat = [thermal(0, 0), thermal(0, 8)]

    def first_step(i, carry):
        x = lax.rem(i + GROUP, CX)

        @pl.when(lax.rem(i, GROUP) == 0)
        def _():
            group = lax.div(x, GROUP)

            @pl.when(has_down)
            def _():
                z_copy(group, 0).wait_recv()

            @pl.when(has_up)
            def _():
                z_copy(group, 1).wait_recv()

        @pl.when(x == CX - 1)
        def _():
            x_copy(0, 1).wait_recv()

        @pl.when(x == 0)
        def _():
            x_copy(0, 0).wait_recv()

        for half in range(2):

            def put(f, value, half=half):
                s1[f, x + 1, :, pl.ds(8 * half, 8), :] = value

            advance(s0, cs, x, BASE0 + 8 * half, 8 * half, heat[half], put)

        @pl.when(x == CX - 1)
        def _():
            x_copy(1, 0).start()

            @pl.when(has_down)
            def _():
                d_copy(0).start()

        @pl.when(x == 0)
        def _():
            x_copy(1, 1).start()

            @pl.when(has_down)
            def _():
                d_copy(1).start()

        @pl.when(jnp.logical_and(lax.rem(i, GROUP) == GROUP - 1, has_down))
        def _():
            m_copy(lax.div(x, GROUP)).start()

        return carry

    lax.fori_loop(0, CX, first_step, 0)

    @pl.when(has_up)
    def _():
        c_copy().wait_recv()
        for group in range(GROUPS):
            m_copy(group).wait_recv()

    heat2 = [thermal(1, 1), thermal(1, 9)]

    def out_copies(x):
        return (
            pltpu.make_async_copy(o.at[pl.ds(0, ORDERS), x], phase_out.at[:, x], out_sem.at[0, x]),
            pltpu.make_async_copy(o.at[ORDERS, x], solute_out.at[x], out_sem.at[1, x]),
        )

    def second_step(i, carry):
        x = lax.rem(i + 1, CX)

        @pl.when(x == CX - 1)
        def _():
            x_copy(1, 1).wait_recv()

            @pl.when(has_up)
            def _():
                d_copy(1).wait_recv()

        @pl.when(x == 0)
        def _():
            x_copy(1, 0).wait_recv()

            @pl.when(has_up)
            def _():
                d_copy(0).wait_recv()

        for half in range(2):

            def put(f, value, half=half):
                for k in range(YT):
                    o[f, x, pl.ds(8 * half, 8), pl.ds(k * LANES, LANES)] = value[k]

            advance(s1, cs, x, 1 + 8 * half, 1 + 8 * half, heat2[half], put)

        @pl.when(jnp.logical_not(has_up))
        def _():
            o[:, x, pl.ds(CZ - 1, 1), :] = jnp.zeros((FIELDS, 1, NY), jnp.float32)

        for copy in out_copies(x):
            copy.start()
        return carry

    lax.fori_loop(0, CX, second_step, 0)

    def finish(x, carry):
        for copy in out_copies(x):
            copy.wait()
        return carry

    lax.fori_loop(0, CX, finish, 0)
    for step in range(STEPS):
        for way in range(2):
            x_copy(step, way).wait_send()

    @pl.when(has_up)
    def _():
        for group in range(GROUPS):
            z_copy(group, 0).wait_send()

    @pl.when(has_down)
    def _():
        for group in range(GROUPS):
            z_copy(group, 1).wait_send()
            m_copy(group).wait_send()
        c_copy().wait_send()
        d_copy(0).wait_send()
        d_copy(1).wait_send()


def local(phase, solute, grain_map, frame_steps):
    anywhere = pl.BlockSpec(memory_space=pl.ANY)
    dma = pltpu.SemaphoreType.DMA
    return pl.pallas_call(
        kernel,
        out_shape=(
            jax.ShapeDtypeStruct(phase.shape, jnp.float32),
            jax.ShapeDtypeStruct(solute.shape, jnp.float32),
        ),
        in_specs=[pl.BlockSpec(memory_space=pltpu.SMEM), anywhere, anywhere, anywhere],
        out_specs=(anywhere, anywhere),
        scratch_shapes=[
            pltpu.VMEM((FIELDS, CX + 2, YT, 32, LANES), jnp.float32),
            pltpu.VMEM((FIELDS, CX + 2, YT, 24, LANES), jnp.float32),
            pltpu.VMEM((ORDERS, CX, YT, CZ, LANES), jnp.int32),
            pltpu.VMEM((2, ORDERS, CX, YT, 24, LANES), jnp.float32),
            pltpu.VMEM((FIELDS, CX, CZ, NY), jnp.float32),
            dma((3, YT)),
            dma((2, CX)),
            dma((STEPS, 2)),
            dma((STEPS, 2)),
            dma((2, GROUPS)),
            dma((2, GROUPS)),
            dma((GROUPS,)),
            dma((GROUPS,)),
            dma,
            dma,
            dma((2,)),
            dma((2,)),
        ],
        compiler_params=pltpu.CompilerParams(
            collective_id=0, has_side_effects=True, vmem_limit_bytes=48 * 1024 * 1024
        ),
        name="grow",
    )(frame_steps, phase, solute, grain_map)


def solution(mesh):
    in_specs = (P(None, "gx", "gz", None), P("gx", "gz", None), P(None, "gx", "gz", None), P())
    out_specs = (P(None, "gx", "gz", None), P("gx", "gz", None))
    return jax.shard_map(local, mesh=mesh, in_specs=in_specs, out_specs=out_specs, check_vma=False)
```

```python
import math

import jax
import jax.numpy as jnp
import numpy as np
from jax import lax
from jax.experimental import pallas as pl
from jax.experimental.pallas import tpu as pltpu
from jax.sharding import PartitionSpec as P

ORDERS = 4
FIELDS = 5
STEPS = 2
NGRAIN = 1024
NZ = 256
CX = 16
CZ = 16
NY = 512
LANES = 128
YT = NY // LANES
GROUP = 4
GROUPS = CX // GROUP
MESH = pl.DeviceIdType.MESH

BASE0 = 8


def sine_coefficients():
    nodes = np.cos(np.pi * (np.arange(400) + 0.5) / 400)
    theta = nodes * np.pi / 2
    even = np.polynomial.chebyshev.Chebyshev.fit(nodes, np.cos(theta), 8, domain=[-1, 1])
    odd = np.polynomial.chebyshev.Chebyshev.fit(nodes, np.sin(theta), 9, domain=[-1, 1])
    even = even.convert(kind=np.polynomial.Polynomial).coef
    odd = odd.convert(kind=np.polynomial.Polynomial).coef
    cos_c = [float(even[i] * math.sqrt(0.5) / 128.0**i) for i in (0, 2, 4, 6, 8)]
    sin_c = [float(odd[i] * math.sqrt(2.0) / 128.0**i) for i in (1, 3, 5, 7, 9)]
    return sin_c, cos_c


SIN_C, COS_C = sine_coefficients()


def horner(x, coefficients):
    value = coefficients[-1]
    for c in coefficients[-2::-1]:
        value = value * x + c
    return value


def next_y(rolled, offset):
    if offset > 0:
        return jnp.concatenate([rolled[1:], rolled[:1]], axis=0)
    return jnp.concatenate([rolled[-1:], rolled[:-1]], axis=0)


def neighbours(s, f, xi, row):
    at = pl.ds(row, 8)
    c = s[f, xi, :, at, :]
    xl = s[f, xi - 1, :, at, :]
    xh = s[f, xi + 1, :, at, :]
    zl = s[f, xi, :, pl.ds(row - 1, 8), :]
    zh = s[f, xi, :, pl.ds(row + 1, 8), :]
    lane = lax.broadcasted_iota(jnp.int32, c.shape, 2)
    right = pltpu.roll(c, 1, axis=2)
    left = pltpu.roll(c, LANES - 1, axis=2)
    yl = jnp.where(lane == 0, next_y(right, -1), right)
    yh = jnp.where(lane == LANES - 1, next_y(left, 1), left)
    return c, xl, xh, yl, yh, zl, zh


def advance(s, cs, x, row, cs_row, thermal, put):
    xi = x + 1
    u = s[ORDERS, xi, :, pl.ds(row, 8), :]
    drive = thermal - 2.4 * u
    q = None
    for k in range(ORDERS):
        p = s[k, xi, :, pl.ds(row, 8), :]
        q = p * p if q is None else q + p * p
    well = 0.64 - 0.16 * q
    total = None
    for k in range(ORDERS):
        p, xl, xh, yl, yh, zl, zh = neighbours(s, k, xi, row)
        gx, gy, gz = xh - xl, yh - yl, zh - zl
        lap = (xl + xh) + (yl + yh) + (zl + zh) - 6.0 * p
        x2, y2, z2 = gx * gx, gy * gy, gz * gz
        r = x2 + y2
        at = pl.ds(cs_row, 8)
        t = cs[0, k, x, :, at, :] * (gx * gy) + cs[1, k, x, :, at, :] * (x2 - y2)
        quartic = r * r + z2 * z2 - t * t
        d = (r + z2) + 0.2
        ratio = quartic * pl.reciprocal(d * d, approx=True)
        w = p - p * p
        delta = (
            lap * (0.08 + 0.04 * ratio)
            + p * (well + p * (1.44 * p - 1.92))
            + (w * w) * drive
        )
        put(k, p + delta)
        total = delta if total is None else total + delta
    c, xl, xh, yl, yh, zl, zh = neighbours(s, ORDERS, xi, row)
    near = (xl + xh) + (yl + yh) + (zl + zh)
    put(ORDERS, 0.52 * c + 0.08 * near + 0.5 * total)


def kernel(
    frames, phase, solute, grain, phase_out, solute_out,
    s0, s1, g, cs, o, heat,
    load_sem, out_sem, x_send, x_recv, z_send, z_recv, m_send, m_recv, c_send, c_recv, d_send, d_recv,
):
    gx, gz = lax.axis_index("gx"), lax.axis_index("gz")
    n_gx, n_gz = lax.axis_size("gx"), lax.axis_size("gz")
    right, left = lax.rem(gx + 1, n_gx), lax.rem(gx + n_gx - 1, n_gx)
    has_up, has_down = gz < n_gz - 1, gz > 0

    loads = []
    for k in range(YT):
        lanes = pl.ds(k * LANES, LANES)
        rows = pl.ds(BASE0, CZ)
        loads.append(
            (
                pltpu.make_async_copy(
                    phase.at[:, :, :, lanes], s0.at[pl.ds(0, ORDERS), pl.ds(1, CX), k, rows, :], load_sem.at[0, k]
                ),
                pltpu.make_async_copy(
                    solute.at[:, :, lanes], s0.at[ORDERS, pl.ds(1, CX), k, rows, :], load_sem.at[1, k]
                ),
                pltpu.make_async_copy(grain.at[:, :, :, lanes], g.at[:, :, k, :, :], load_sem.at[2, k]),
            )
        )
    barrier = pltpu.get_barrier_semaphore()

    def greet(ix, iz):
        pl.semaphore_signal(barrier, inc=1, device_id=(ix, iz), device_id_type=MESH)

    greet(left, gz)
    greet(right, gz)

    @pl.when(has_up)
    def _():
        greet(gx, gz + 1)

    @pl.when(has_down)
    def _():
        greet(gx, gz - 1)

    for which in range(3):
        for k in range(YT):
            loads[k][which].start()

    @pl.when(jnp.logical_not(has_down))
    def _():
        def clear(x, carry):
            s0[:, x, :, pl.ds(BASE0 - 1, 1), :] = jnp.zeros((FIELDS, YT, 1, LANES), jnp.float32)
            return carry

        lax.fori_loop(0, CX + 2, clear, 0)

    @pl.when(jnp.logical_not(has_up))
    def _():
        def clear(x, carry):
            s0[:, x, :, pl.ds(BASE0 + CZ, 1), :] = jnp.zeros((FIELDS, YT, 1, LANES), jnp.float32)
            s1[:, x, :, pl.ds(CZ, 2), :] = jnp.zeros((FIELDS, YT, 2, LANES), jnp.float32)
            return carry

        lax.fori_loop(0, CX + 2, clear, 0)

        def clear_cs(x, carry):
            cs[:, :, x, :, pl.ds(CZ, 1), :] = jnp.zeros((2, ORDERS, YT, 1, LANES), jnp.float32)
            return carry

        lax.fori_loop(0, CX, clear_cs, 0)

    def remote(src, dst, send, recv, ix, iz):
        return pltpu.make_async_remote_copy(
            src_ref=src, dst_ref=dst, send_sem=send, recv_sem=recv, device_id=(ix, iz), device_id_type=MESH
        )

    def x_copy(step, way, half):
        s, base = (s0, BASE0) if step == 0 else (s1, 0)
        rows = pl.ds(base + 8 * half, 8)
        src, dst, to = (CX, 0, right) if way == 0 else (1, CX + 1, left)
        return remote(
            s.at[:, src, :, rows, :],
            s.at[:, dst, :, rows, :],
            x_send.at[step, way, half],
            x_recv.at[step, way, half],
            to,
            gz,
        )

    def z_copy(group, way):
        planes = pl.ds(1 + group * GROUP, GROUP)
        src, dst, to = (BASE0 + CZ - 1, BASE0 - 1, gz + 1) if way == 0 else (BASE0, BASE0 + CZ, gz - 1)
        return remote(
            s0.at[:, planes, :, pl.ds(src, 1), :],
            s0.at[:, planes, :, pl.ds(dst, 1), :],
            z_send.at[way, group],
            z_recv.at[way, group],
            gx,
            to,
        )

    def m_copy(x):
        return remote(
            s1.at[:, x + 1, :, pl.ds(0, 2), :],
            s1.at[:, x + 1, :, pl.ds(CZ, 2), :],
            m_send.at[x],
            m_recv.at[x],
            gx,
            gz - 1,
        )

    def d_copy(way):
        src, dst, to = (CX, 0, right) if way == 0 else (1, CX + 1, left)
        return remote(
            s1.at[:, src, :, pl.ds(0, 1), :],
            s1.at[:, dst, :, pl.ds(CZ, 1), :],
            d_send.at[way],
            d_recv.at[way],
            to,
            gz - 1,
        )

    def c_copy():
        return remote(
            cs.at[:, :, :, :, pl.ds(0, 1), :], cs.at[:, :, :, :, pl.ds(CZ, 1), :], c_send, c_recv, gx, gz - 1
        )

    for which in range(2):
        for k in range(YT):
            loads[k][which].wait()

    pl.semaphore_wait(barrier, 2 + has_up.astype(jnp.int32) + has_down.astype(jnp.int32))

    for half in range(2):
        x_copy(0, 0, half).start()
        x_copy(0, 1, half).start()
    for group in (1, 2, 3, 0):

        @pl.when(has_up)
        def _(group=group):
            z_copy(group, 0).start()

        @pl.when(has_down)
        def _(group=group):
            z_copy(group, 1).start()

    for k in range(YT):
        loads[k][2].wait()

    def trig(x, carry):
        for k in range(ORDERS):
            for half in range(2):
                at = pl.ds(8 * half, 8)
                h = ((g[k, x, :, at, :] & 255) - 128).astype(jnp.float32)
                h2 = h * h
                cs[0, k, x, :, at, :] = h * horner(h2, SIN_C)
                cs[1, k, x, :, at, :] = horner(h2, COS_C)
        return carry

    lax.fori_loop(0, CX, trig, 0)

    @pl.when(has_down)
    def _():
        c_copy().start()

    for step in range(STEPS):
        for half in range(2):
            z = gz * CZ + 8 * half + step + lax.broadcasted_iota(jnp.int32, (1, 8, LANES), 1)
            height = (NZ // 2 - z - frames[step]).astype(jnp.float32)
            heat[step, half] = 2.4 * jnp.tanh(height * 0.125)

    def first_step(i, carry):
        m, half = lax.div(i, 2), lax.rem(i, 2)
        xa = jnp.where(m < 5, 4 + 2 * m, jnp.where(m == 5, 2, 21 - m))
        xb = jnp.where(m < 6, xa + 1, m - 6)

        @pl.when(jnp.logical_or(i == 0, jnp.logical_or(i == 4, jnp.logical_or(i == 8, i == 10))))
        def _():
            group = lax.div(xa, GROUP)

            @pl.when(has_down)
            def _():
                z_copy(group, 0).wait_recv()

            @pl.when(has_up)
            def _():
                z_copy(group, 1).wait_recv()

        @pl.when(m == 6)
        def _():
            x_copy(0, 0, half).wait_recv()
            x_copy(0, 1, half).wait_recv()

        for x in (xa, xb):

            def put(f, value, x=x):
                s1[f, x + 1, :, pl.ds(8 * half, 8), :] = value

            advance(s0, cs, x, BASE0 + 8 * half, 8 * half, heat[0, half], put)

        @pl.when(m == 6)
        def _():
            x_copy(1, 0, half).start()
            x_copy(1, 1, half).start()

        @pl.when(jnp.logical_and(half == 0, has_down))
        def _():
            m_copy(xa).start()
            m_copy(xb).start()

            @pl.when(m == 6)
            def _():
                d_copy(0).start()
                d_copy(1).start()

        return carry

    lax.fori_loop(0, CX, first_step, 0)

    def out_copies(x, half):
        rows = pl.ds(8 * half, 8)
        return (
            pltpu.make_async_copy(o.at[pl.ds(0, ORDERS), x, rows, :], phase_out.at[:, x, rows, :], out_sem.at[0, x, half]),
            pltpu.make_async_copy(o.at[ORDERS, x, rows, :], solute_out.at[x, rows, :], out_sem.at[1, x, half]),
        )

    def second_step(i, carry):
        rim = i >= 14
        half = jnp.where(rim, i - 14, lax.div(i, 7))
        m = lax.rem(i, 7)
        xa = jnp.where(rim, 0, jnp.where(m < 5, 5 + 2 * m, 13 - 2 * m))
        xb = jnp.where(rim, CX - 1, xa + 1)

        @pl.when(jnp.logical_and(has_up, i == 7))
        def _():
            c_copy().wait_recv()
            m_copy(4).wait_recv()
            m_copy(5).wait_recv()

        @pl.when(jnp.logical_and(has_up, jnp.logical_and(i >= 7, i < 14)))
        def _():
            first = jnp.where(m < 5, xa + 1, xa - 1)
            m_copy(first).wait_recv()
            m_copy(first + 1).wait_recv()

        @pl.when(i == 14)
        def _():
            for part in range(2):
                x_copy(1, 0, part).wait_recv()
                x_copy(1, 1, part).wait_recv()

        @pl.when(jnp.logical_and(i == 15, has_up))
        def _():
            d_copy(0).wait_recv()
            d_copy(1).wait_recv()

        for x in (xa, xb):

            def put(f, value, x=x):
                for k in range(YT):
                    o[f, x, pl.ds(pl.multiple_of(8 * half, 8), 8), pl.ds(k * LANES, LANES)] = value[k]

            advance(s1, cs, x, 1 + 8 * half, 1 + 8 * half, heat[1, half], put)

        @pl.when(jnp.logical_and(half == 1, jnp.logical_not(has_up)))
        def _():
            for x in (xa, xb):
                o[:, x, pl.ds(CZ - 1, 1), :] = jnp.zeros((FIELDS, 1, NY), jnp.float32)

        for x in (xa, xb):
            for copy in out_copies(x, half):
                copy.start()
        return carry

    lax.fori_loop(0, CX, second_step, 0)

    def finish(x, carry):
        for half in range(2):
            for copy in out_copies(x, half):
                copy.wait()

        @pl.when(has_down)
        def _():
            m_copy(x).wait_send()

        return carry

    lax.fori_loop(0, CX, finish, 0)
    for step in range(STEPS):
        for way in range(2):
            for half in range(2):
                x_copy(step, way, half).wait_send()

    @pl.when(has_up)
    def _():
        for group in range(GROUPS):
            z_copy(group, 0).wait_send()

    @pl.when(has_down)
    def _():
        for group in range(GROUPS):
            z_copy(group, 1).wait_send()
        c_copy().wait_send()
        d_copy(0).wait_send()
        d_copy(1).wait_send()


def local(phase, solute, grain_map, frame_steps):
    hbm = pl.BlockSpec(memory_space=pltpu.HBM)
    dma = pltpu.SemaphoreType.DMA
    return pl.pallas_call(
        kernel,
        out_shape=(
            jax.ShapeDtypeStruct(phase.shape, jnp.float32),
            jax.ShapeDtypeStruct(solute.shape, jnp.float32),
        ),
        in_specs=[pl.BlockSpec(memory_space=pltpu.SMEM), hbm, hbm, hbm],
        out_specs=(hbm, hbm),
        scratch_shapes=[
            pltpu.VMEM((FIELDS, CX + 2, YT, 32, LANES), jnp.float32),
            pltpu.VMEM((FIELDS, CX + 2, YT, 24, LANES), jnp.float32),
            pltpu.VMEM((ORDERS, CX, YT, CZ, LANES), jnp.int32),
            pltpu.VMEM((2, ORDERS, CX, YT, 24, LANES), jnp.float32),
            pltpu.VMEM((FIELDS, CX, CZ, NY), jnp.float32),
            pltpu.VMEM((STEPS, 2, 1, 8, LANES), jnp.float32),
            dma((3, YT)),
            dma((2, CX, 2)),
            dma((STEPS, 2, 2)),
            dma((STEPS, 2, 2)),
            dma((2, GROUPS)),
            dma((2, GROUPS)),
            dma((CX,)),
            dma((CX,)),
            dma,
            dma,
            dma((2,)),
            dma((2,)),
        ],
        compiler_params=pltpu.CompilerParams(
            collective_id=0, has_side_effects=True, vmem_limit_bytes=48 * 1024 * 1024
        ),
        name="grow",
    )(frame_steps, phase, solute, grain_map)


def solution(mesh):
    in_specs = (P(None, "gx", "gz", None), P("gx", "gz", None), P(None, "gx", "gz", None), P())
    out_specs = (P(None, "gx", "gz", None), P("gx", "gz", None))
    return jax.shard_map(local, mesh=mesh, in_specs=in_specs, out_specs=out_specs, check_vma=False)
```

```python
import math

import jax
import jax.numpy as jnp
import numpy as np
from jax import lax
from jax.experimental import pallas as pl
from jax.experimental.pallas import tpu as pltpu
from jax.sharding import PartitionSpec as P

ORDERS = 4
FIELDS = 5
STEPS = 2
NGRAIN = 1024
NZ = 256
CX = 16
CZ = 16
NY = 512
LANES = 128
YT = NY // LANES
GROUP = 4
GROUPS = CX // GROUP
MESH = pl.DeviceIdType.MESH

BASE0 = 8


def sine_coefficients():
    nodes = np.cos(np.pi * (np.arange(400) + 0.5) / 400)
    theta = nodes * np.pi / 2
    even = np.polynomial.chebyshev.Chebyshev.fit(nodes, np.cos(theta), 8, domain=[-1, 1])
    odd = np.polynomial.chebyshev.Chebyshev.fit(nodes, np.sin(theta), 9, domain=[-1, 1])
    even = even.convert(kind=np.polynomial.Polynomial).coef
    odd = odd.convert(kind=np.polynomial.Polynomial).coef
    cos_c = [float(even[i] * math.sqrt(0.5) / 128.0**i) for i in (0, 2, 4, 6, 8)]
    sin_c = [float(odd[i] * math.sqrt(2.0) / 128.0**i) for i in (1, 3, 5, 7, 9)]
    return sin_c, cos_c


SIN_C, COS_C = sine_coefficients()


def horner(x, coefficients):
    value = coefficients[-1]
    for c in coefficients[-2::-1]:
        value = value * x + c
    return value


def next_y(rolled, offset):
    if offset > 0:
        return jnp.concatenate([rolled[1:], rolled[:1]], axis=0)
    return jnp.concatenate([rolled[-1:], rolled[:-1]], axis=0)


def neighbours(s, f, xi, row):
    at = pl.ds(row, 8)
    c = s[f, xi, :, at, :]
    xl = s[f, xi - 1, :, at, :]
    xh = s[f, xi + 1, :, at, :]
    zl = s[f, xi, :, pl.ds(row - 1, 8), :]
    zh = s[f, xi, :, pl.ds(row + 1, 8), :]
    lane = lax.broadcasted_iota(jnp.int32, c.shape, 2)
    right = pltpu.roll(c, 1, axis=2)
    left = pltpu.roll(c, LANES - 1, axis=2)
    yl = jnp.where(lane == 0, next_y(right, -1), right)
    yh = jnp.where(lane == LANES - 1, next_y(left, 1), left)
    return c, xl, xh, yl, yh, zl, zh


def advance(s, cs, x, row, cs_row, thermal, put):
    xi = x + 1
    u = s[ORDERS, xi, :, pl.ds(row, 8), :]
    drive = thermal - 2.4 * u
    q = None
    for k in range(ORDERS):
        p = s[k, xi, :, pl.ds(row, 8), :]
        q = p * p if q is None else q + p * p
    well = 0.64 - 0.16 * q
    total = None
    for k in range(ORDERS):
        p, xl, xh, yl, yh, zl, zh = neighbours(s, k, xi, row)
        gx, gy, gz = xh - xl, yh - yl, zh - zl
        lap = (xl + xh) + (yl + yh) + (zl + zh) - 6.0 * p
        x2, y2, z2 = gx * gx, gy * gy, gz * gz
        r = x2 + y2
        at = pl.ds(cs_row, 8)
        t = cs[0, k, x, :, at, :] * (gx * gy) + cs[1, k, x, :, at, :] * (x2 - y2)
        quartic = r * r + z2 * z2 - t * t
        d = (r + z2) + 0.2
        ratio = quartic * pl.reciprocal(d * d, approx=True)
        w = p - p * p
        delta = (
            lap * (0.08 + 0.04 * ratio)
            + p * (well + p * (1.44 * p - 1.92))
            + (w * w) * drive
        )
        put(k, p + delta)
        total = delta if total is None else total + delta
    c, xl, xh, yl, yh, zl, zh = neighbours(s, ORDERS, xi, row)
    near = (xl + xh) + (yl + yh) + (zl + zh)
    put(ORDERS, 0.52 * c + 0.08 * near + 0.5 * total)


def kernel(
    frames_in, phase, solute, grain, o,
    s0, s1, g, cs, heat, frames,
    load_sem, frame_sem, x_send, x_recv, z_send, z_recv, m_send, m_recv, c_send, c_recv, d_send, d_recv,
):
    gx, gz = lax.axis_index("gx"), lax.axis_index("gz")
    n_gx, n_gz = lax.axis_size("gx"), lax.axis_size("gz")
    right, left = lax.rem(gx + 1, n_gx), lax.rem(gx + n_gx - 1, n_gx)
    has_up, has_down = gz < n_gz - 1, gz > 0

    loads = []
    for k in range(YT):
        lanes = pl.ds(k * LANES, LANES)
        rows = pl.ds(BASE0, CZ)
        loads.append(
            (
                pltpu.make_async_copy(
                    phase.at[:, :, :, lanes], s0.at[pl.ds(0, ORDERS), pl.ds(1, CX), k, rows, :], load_sem.at[0, k]
                ),
                pltpu.make_async_copy(
                    solute.at[:, :, lanes], s0.at[ORDERS, pl.ds(1, CX), k, rows, :], load_sem.at[1, k]
                ),
                pltpu.make_async_copy(grain.at[:, :, :, lanes], g.at[:, :, k, :, :], load_sem.at[2, k]),
            )
        )
    frame_load = pltpu.make_async_copy(frames_in, frames, frame_sem)
    barrier = pltpu.get_barrier_semaphore()

    def greet(ix, iz):
        pl.semaphore_signal(barrier, inc=1, device_id=(ix, iz), device_id_type=MESH)

    greet(left, gz)
    greet(right, gz)

    @pl.when(has_up)
    def _():
        greet(gx, gz + 1)

    @pl.when(has_down)
    def _():
        greet(gx, gz - 1)

    for which in range(3):
        for k in range(YT):
            loads[k][which].start()

    frame_load.start()

    @pl.when(jnp.logical_not(has_down))
    def _():
        def clear(x, carry):
            s0[:, x, :, pl.ds(BASE0 - 1, 1), :] = jnp.zeros((FIELDS, YT, 1, LANES), jnp.float32)
            return carry

        lax.fori_loop(0, CX + 2, clear, 0)

    @pl.when(jnp.logical_not(has_up))
    def _():
        def clear(x, carry):
            s0[:, x, :, pl.ds(BASE0 + CZ, 1), :] = jnp.zeros((FIELDS, YT, 1, LANES), jnp.float32)
            s1[:, x, :, pl.ds(CZ, 2), :] = jnp.zeros((FIELDS, YT, 2, LANES), jnp.float32)
            return carry

        lax.fori_loop(0, CX + 2, clear, 0)

        def clear_cs(x, carry):
            cs[:, :, x, :, pl.ds(CZ, 1), :] = jnp.zeros((2, ORDERS, YT, 1, LANES), jnp.float32)
            return carry

        lax.fori_loop(0, CX, clear_cs, 0)

    def remote(src, dst, send, recv, ix, iz):
        return pltpu.make_async_remote_copy(
            src_ref=src, dst_ref=dst, send_sem=send, recv_sem=recv, device_id=(ix, iz), device_id_type=MESH
        )

    def x_copy(step, way, half):
        s, base = (s0, BASE0) if step == 0 else (s1, 0)
        rows = pl.ds(base + 8 * half, 8)
        src, dst, to = (CX, 0, right) if way == 0 else (1, CX + 1, left)
        return remote(
            s.at[:, src, :, rows, :],
            s.at[:, dst, :, rows, :],
            x_send.at[step, way, half],
            x_recv.at[step, way, half],
            to,
            gz,
        )

    def z_copy(group, way):
        planes = pl.ds(1 + group * GROUP, GROUP)
        src, dst, to = (BASE0 + CZ - 1, BASE0 - 1, gz + 1) if way == 0 else (BASE0, BASE0 + CZ, gz - 1)
        return remote(
            s0.at[:, planes, :, pl.ds(src, 1), :],
            s0.at[:, planes, :, pl.ds(dst, 1), :],
            z_send.at[way, group],
            z_recv.at[way, group],
            gx,
            to,
        )

    def m_copy(x):
        return remote(
            s1.at[:, x + 1, :, pl.ds(0, 2), :],
            s1.at[:, x + 1, :, pl.ds(CZ, 2), :],
            m_send.at[x],
            m_recv.at[x],
            gx,
            gz - 1,
        )

    def d_copy(way):
        src, dst, to = (CX, 0, right) if way == 0 else (1, CX + 1, left)
        return remote(
            s1.at[:, src, :, pl.ds(0, 1), :],
            s1.at[:, dst, :, pl.ds(CZ, 1), :],
            d_send.at[way],
            d_recv.at[way],
            to,
            gz - 1,
        )

    def c_copy():
        return remote(
            cs.at[:, :, :, :, pl.ds(0, 1), :], cs.at[:, :, :, :, pl.ds(CZ, 1), :], c_send, c_recv, gx, gz - 1
        )

    for which in range(2):
        for k in range(YT):
            loads[k][which].wait()

    pl.semaphore_wait(barrier, 2 + has_up.astype(jnp.int32) + has_down.astype(jnp.int32))

    for half in range(2):
        x_copy(0, 0, half).start()
        x_copy(0, 1, half).start()
    for group in (1, 2, 3, 0):

        @pl.when(has_up)
        def _(group=group):
            z_copy(group, 0).start()

        @pl.when(has_down)
        def _(group=group):
            z_copy(group, 1).start()

    for k in range(YT):
        loads[k][2].wait()

    def trig(x, carry):
        for k in range(ORDERS):
            for half in range(2):
                at = pl.ds(8 * half, 8)
                h = ((g[k, x, :, at, :] & 255) - 128).astype(jnp.float32)
                h2 = h * h
                cs[0, k, x, :, at, :] = h * horner(h2, SIN_C)
                cs[1, k, x, :, at, :] = horner(h2, COS_C)
        return carry

    lax.fori_loop(0, CX, trig, 0)

    @pl.when(has_down)
    def _():
        c_copy().start()

    frame_load.wait()
    for step in range(STEPS):
        for half in range(2):
            z = gz * CZ + 8 * half + step + lax.broadcasted_iota(jnp.int32, (1, 8, LANES), 1)
            height = (NZ // 2 - z - frames[step]).astype(jnp.float32)
            heat[step, half] = 2.4 * jnp.tanh(height * 0.125)

    def first_step(i, carry):
        m, half = lax.div(i, 2), lax.rem(i, 2)
        xa = jnp.where(m < 5, 4 + 2 * m, jnp.where(m == 5, 2, 21 - m))
        xb = jnp.where(m < 6, xa + 1, m - 6)

        @pl.when(jnp.logical_or(i == 0, jnp.logical_or(i == 4, jnp.logical_or(i == 8, i == 10))))
        def _():
            group = lax.div(xa, GROUP)

            @pl.when(has_down)
            def _():
                z_copy(group, 0).wait_recv()

            @pl.when(has_up)
            def _():
                z_copy(group, 1).wait_recv()

        @pl.when(m == 6)
        def _():
            x_copy(0, 0, half).wait_recv()
            x_copy(0, 1, half).wait_recv()

        for x in (xa, xb):

            def put(f, value, x=x):
                s1[f, x + 1, :, pl.ds(8 * half, 8), :] = value

            advance(s0, cs, x, BASE0 + 8 * half, 8 * half, heat[0, half], put)

        @pl.when(m == 6)
        def _():
            x_copy(1, 0, half).start()
            x_copy(1, 1, half).start()

        @pl.when(jnp.logical_and(half == 0, has_down))
        def _():
            m_copy(xa).start()
            m_copy(xb).start()

            @pl.when(m == 6)
            def _():
                d_copy(0).start()
                d_copy(1).start()

        return carry

    lax.fori_loop(0, CX, first_step, 0)

    def second_step(i, carry):
        rim = i >= 14
        half = jnp.where(rim, i - 14, lax.div(i, 7))
        m = lax.rem(i, 7)
        xa = jnp.where(rim, 0, jnp.where(m < 5, 5 + 2 * m, 13 - 2 * m))
        xb = jnp.where(rim, CX - 1, xa + 1)

        @pl.when(jnp.logical_and(has_up, i == 7))
        def _():
            c_copy().wait_recv()
            m_copy(4).wait_recv()
            m_copy(5).wait_recv()

        @pl.when(jnp.logical_and(has_up, jnp.logical_and(i >= 7, i < 14)))
        def _():
            first = jnp.where(m < 5, xa + 1, xa - 1)
            m_copy(first).wait_recv()
            m_copy(first + 1).wait_recv()

        @pl.when(i == 14)
        def _():
            for part in range(2):
                x_copy(1, 0, part).wait_recv()
                x_copy(1, 1, part).wait_recv()

        @pl.when(jnp.logical_and(i == 15, has_up))
        def _():
            d_copy(0).wait_recv()
            d_copy(1).wait_recv()

        for x in (xa, xb):

            def put(f, value, x=x):
                for k in range(YT):
                    o[f, x, pl.ds(pl.multiple_of(8 * half, 8), 8), pl.ds(k * LANES, LANES)] = value[k]

            advance(s1, cs, x, 1 + 8 * half, 1 + 8 * half, heat[1, half], put)

        @pl.when(jnp.logical_and(half == 1, jnp.logical_not(has_up)))
        def _():
            for x in (xa, xb):
                o[:, x, pl.ds(CZ - 1, 1), :] = jnp.zeros((FIELDS, 1, NY), jnp.float32)

        return carry

    lax.fori_loop(0, CX, second_step, 0)

    for step in range(STEPS):
        for way in range(2):
            for half in range(2):
                x_copy(step, way, half).wait_send()

    @pl.when(has_up)
    def _():
        for group in range(GROUPS):
            z_copy(group, 0).wait_send()

    @pl.when(has_down)
    def _():
        for group in range(GROUPS):
            z_copy(group, 1).wait_send()
        for x in range(CX):
            m_copy(x).wait_send()
        c_copy().wait_send()
        d_copy(0).wait_send()
        d_copy(1).wait_send()


def flush(o, phase_out, solute_out, sem):
    copies = (
        pltpu.make_async_copy(o.at[pl.ds(0, ORDERS)], phase_out, sem.at[0]),
        pltpu.make_async_copy(o.at[ORDERS], solute_out, sem.at[1]),
    )
    for copy in copies:
        copy.start()
    for copy in copies:
        copy.wait()


def local(phase, solute, grain_map, frame_steps):
    hbm, vmem = pl.BlockSpec(memory_space=pltpu.HBM), pl.BlockSpec(memory_space=pltpu.VMEM)
    dma = pltpu.SemaphoreType.DMA
    args = [pltpu.with_memory_space_constraint(a, pltpu.HBM) for a in (frame_steps, phase, solute, grain_map)]
    result = pl.pallas_call(
        kernel,
        out_shape=pltpu.VMEM((FIELDS, CX, CZ, NY), jnp.float32),
        in_specs=[hbm] * 4,
        out_specs=vmem,
        scratch_shapes=[
            pltpu.VMEM((FIELDS, CX + 2, YT, 32, LANES), jnp.float32),
            pltpu.VMEM((FIELDS, CX + 2, YT, 24, LANES), jnp.float32),
            pltpu.VMEM((ORDERS, CX, YT, CZ, LANES), jnp.int32),
            pltpu.VMEM((2, ORDERS, CX, YT, 24, LANES), jnp.float32),
            pltpu.VMEM((STEPS, 2, 1, 8, LANES), jnp.float32),
            pltpu.SMEM((STEPS,), jnp.int32),
            dma((3, YT)),
            dma,
            dma((STEPS, 2, 2)),
            dma((STEPS, 2, 2)),
            dma((2, GROUPS)),
            dma((2, GROUPS)),
            dma((CX,)),
            dma((CX,)),
            dma,
            dma,
            dma((2,)),
            dma((2,)),
        ],
        compiler_params=pltpu.CompilerParams(
            collective_id=0, has_side_effects=True, vmem_limit_bytes=32 * 1024 * 1024
        ),
        name="grow",
    )(*args)
    return pl.pallas_call(
        flush,
        out_shape=(
            pltpu.HBM(phase.shape, jnp.float32),
            pltpu.HBM(solute.shape, jnp.float32),
        ),
        in_specs=[vmem],
        out_specs=(hbm, hbm),
        scratch_shapes=[dma((2,))],
        compiler_params=pltpu.CompilerParams(vmem_limit_bytes=4 * 1024 * 1024),
        name="flush",
    )(result)


def solution(mesh):
    in_specs = (P(None, "gx", "gz", None), P("gx", "gz", None), P(None, "gx", "gz", None), P())
    out_specs = (P(None, "gx", "gz", None), P("gx", "gz", None))
    return jax.shard_map(local, mesh=mesh, in_specs=in_specs, out_specs=out_specs, check_vma=False)
```

```python
import math

import jax
import jax.numpy as jnp
import numpy as np
from jax import lax
from jax.experimental import pallas as pl
from jax.experimental.pallas import tpu as pltpu
from jax.sharding import PartitionSpec as P

ORDERS = 4
FIELDS = 5
STEPS = 2
NGRAIN = 1024
NZ = 256
CX = 16
CZ = 16
NY = 512
LANES = 128
YT = NY // LANES
GROUP = 4
GROUPS = CX // GROUP
MESH = pl.DeviceIdType.MESH

BASE0 = 8


def sine_coefficients():
    nodes = np.cos(np.pi * (np.arange(400) + 0.5) / 400)
    theta = nodes * np.pi / 2
    even = np.polynomial.chebyshev.Chebyshev.fit(nodes, np.cos(theta), 8, domain=[-1, 1])
    odd = np.polynomial.chebyshev.Chebyshev.fit(nodes, np.sin(theta), 9, domain=[-1, 1])
    even = even.convert(kind=np.polynomial.Polynomial).coef
    odd = odd.convert(kind=np.polynomial.Polynomial).coef
    cos_c = [float(even[i] * math.sqrt(0.5) / 128.0**i) for i in (0, 2, 4, 6, 8)]
    sin_c = [float(odd[i] * math.sqrt(2.0) / 128.0**i) for i in (1, 3, 5, 7, 9)]
    return sin_c, cos_c


SIN_C, COS_C = sine_coefficients()


def horner(x, coefficients):
    value = coefficients[-1]
    for c in coefficients[-2::-1]:
        value = value * x + c
    return value


def next_y(rolled, offset):
    if offset > 0:
        return jnp.concatenate([rolled[1:], rolled[:1]], axis=0)
    return jnp.concatenate([rolled[-1:], rolled[:-1]], axis=0)


def neighbours(s, f, xi, row):
    at = pl.ds(row, 8)
    c = s[f, xi, :, at, :]
    xl = s[f, xi - 1, :, at, :]
    xh = s[f, xi + 1, :, at, :]
    zl = s[f, xi, :, pl.ds(row - 1, 8), :]
    zh = s[f, xi, :, pl.ds(row + 1, 8), :]
    lane = lax.broadcasted_iota(jnp.int32, c.shape, 2)
    right = pltpu.roll(c, 1, axis=2)
    left = pltpu.roll(c, LANES - 1, axis=2)
    yl = jnp.where(lane == 0, next_y(right, -1), right)
    yh = jnp.where(lane == LANES - 1, next_y(left, 1), left)
    return c, xl, xh, yl, yh, zl, zh


def advance(s, cs, x, row, cs_row, thermal, put):
    xi = x + 1
    u = s[ORDERS, xi, :, pl.ds(row, 8), :]
    drive = thermal - 2.4 * u
    q = None
    for k in range(ORDERS):
        p = s[k, xi, :, pl.ds(row, 8), :]
        q = p * p if q is None else q + p * p
    well = 0.64 - 0.16 * q
    total = None
    for k in range(ORDERS):
        p, xl, xh, yl, yh, zl, zh = neighbours(s, k, xi, row)
        gx, gy, gz = xh - xl, yh - yl, zh - zl
        lap = (xl + xh) + (yl + yh) + (zl + zh) - 6.0 * p
        x2, y2, z2 = gx * gx, gy * gy, gz * gz
        r = x2 + y2
        at = pl.ds(cs_row, 8)
        t = cs[0, k, x, :, at, :] * (gx * gy) + cs[1, k, x, :, at, :] * (x2 - y2)
        quartic = r * r + z2 * z2 - t * t
        d = (r + z2) + 0.2
        ratio = quartic * pl.reciprocal(d * d, approx=True)
        w = p - p * p
        delta = (
            lap * (0.08 + 0.04 * ratio)
            + p * (well + p * (1.44 * p - 1.92))
            + (w * w) * drive
        )
        put(k, p + delta)
        total = delta if total is None else total + delta
    c, xl, xh, yl, yh, zl, zh = neighbours(s, ORDERS, xi, row)
    near = (xl + xh) + (yl + yh) + (zl + zh)
    put(ORDERS, 0.52 * c + 0.08 * near + 0.5 * total)


def kernel(
    frames_in, phase, solute, grain, o,
    s0, s1, g, cs, heat, frames,
    load_sem, frame_sem, x_send, x_recv, z_send, z_recv, m_send, m_recv, c_send, c_recv, d_send, d_recv,
):
    gx, gz = lax.axis_index("gx"), lax.axis_index("gz")
    n_gx, n_gz = lax.axis_size("gx"), lax.axis_size("gz")
    right, left = lax.rem(gx + 1, n_gx), lax.rem(gx + n_gx - 1, n_gx)
    has_up, has_down = gz < n_gz - 1, gz > 0

    loads = []
    for k in range(YT):
        lanes = pl.ds(k * LANES, LANES)
        rows = pl.ds(BASE0, CZ)
        loads.append(
            (
                pltpu.make_async_copy(
                    phase.at[:, :, :, lanes], s0.at[pl.ds(0, ORDERS), pl.ds(1, CX), k, rows, :], load_sem.at[0, k]
                ),
                pltpu.make_async_copy(
                    solute.at[:, :, lanes], s0.at[ORDERS, pl.ds(1, CX), k, rows, :], load_sem.at[1, k]
                ),
                pltpu.make_async_copy(grain.at[:, :, :, lanes], g.at[:, :, k, :, :], load_sem.at[2, k]),
            )
        )
    frame_load = pltpu.make_async_copy(frames_in, frames, frame_sem)
    barrier = pltpu.get_barrier_semaphore()

    def greet(ix, iz):
        pl.semaphore_signal(barrier, inc=1, device_id=(ix, iz), device_id_type=MESH)

    greet(left, gz)
    greet(right, gz)

    @pl.when(has_up)
    def _():
        greet(gx, gz + 1)

    @pl.when(has_down)
    def _():
        greet(gx, gz - 1)

    for which in range(3):
        for k in range(YT):
            loads[k][which].start()

    frame_load.start()

    @pl.when(jnp.logical_not(has_down))
    def _():
        def clear(x, carry):
            s0[:, x, :, pl.ds(BASE0 - 1, 1), :] = jnp.zeros((FIELDS, YT, 1, LANES), jnp.float32)
            return carry

        lax.fori_loop(0, CX + 2, clear, 0)

    @pl.when(jnp.logical_not(has_up))
    def _():
        def clear(x, carry):
            s0[:, x, :, pl.ds(BASE0 + CZ, 1), :] = jnp.zeros((FIELDS, YT, 1, LANES), jnp.float32)
            s1[:, x, :, pl.ds(CZ, 2), :] = jnp.zeros((FIELDS, YT, 2, LANES), jnp.float32)
            return carry

        lax.fori_loop(0, CX + 2, clear, 0)

        def clear_cs(x, carry):
            cs[:, :, x, :, pl.ds(CZ, 1), :] = jnp.zeros((2, ORDERS, YT, 1, LANES), jnp.float32)
            return carry

        lax.fori_loop(0, CX, clear_cs, 0)

    def remote(src, dst, send, recv, ix, iz):
        return pltpu.make_async_remote_copy(
            src_ref=src, dst_ref=dst, send_sem=send, recv_sem=recv, device_id=(ix, iz), device_id_type=MESH
        )

    def x_copy(step, way, half):
        s, base = (s0, BASE0) if step == 0 else (s1, 0)
        rows = pl.ds(base + 8 * half, 8)
        src, dst, to = (CX, 0, right) if way == 0 else (1, CX + 1, left)
        return remote(
            s.at[:, src, :, rows, :],
            s.at[:, dst, :, rows, :],
            x_send.at[step, way, half],
            x_recv.at[step, way, half],
            to,
            gz,
        )

    def z_copy(group, way):
        planes = pl.ds(1 + group * GROUP, GROUP)
        src, dst, to = (BASE0 + CZ - 1, BASE0 - 1, gz + 1) if way == 0 else (BASE0, BASE0 + CZ, gz - 1)
        return remote(
            s0.at[:, planes, :, pl.ds(src, 1), :],
            s0.at[:, planes, :, pl.ds(dst, 1), :],
            z_send.at[way, group],
            z_recv.at[way, group],
            gx,
            to,
        )

    def m_copy(x):
        return remote(
            s1.at[:, x + 1, :, pl.ds(0, 2), :],
            s1.at[:, x + 1, :, pl.ds(CZ, 2), :],
            m_send.at[x],
            m_recv.at[x],
            gx,
            gz - 1,
        )

    def d_copy(way):
        src, dst, to = (CX, 0, right) if way == 0 else (1, CX + 1, left)
        return remote(
            s1.at[:, src, :, pl.ds(0, 1), :],
            s1.at[:, dst, :, pl.ds(CZ, 1), :],
            d_send.at[way],
            d_recv.at[way],
            to,
            gz - 1,
        )

    def c_copy():
        return remote(
            cs.at[:, :, :, :, pl.ds(0, 1), :], cs.at[:, :, :, :, pl.ds(CZ, 1), :], c_send, c_recv, gx, gz - 1
        )

    for which in range(2):
        for k in range(YT):
            loads[k][which].wait()

    pl.semaphore_wait(barrier, 2 + has_up.astype(jnp.int32) + has_down.astype(jnp.int32))

    for half in range(2):
        x_copy(0, 0, half).start()
        x_copy(0, 1, half).start()
    for group in (1, 2, 3, 0):

        @pl.when(has_up)
        def _(group=group):
            z_copy(group, 0).start()

        @pl.when(has_down)
        def _(group=group):
            z_copy(group, 1).start()

    for k in range(YT):
        loads[k][2].wait()

    def trig(x, carry):
        for k in range(ORDERS):
            for half in range(2):
                at = pl.ds(8 * half, 8)
                h = ((g[k, x, :, at, :] & 255) - 128).astype(jnp.float32)
                h2 = h * h
                cs[0, k, x, :, at, :] = h * horner(h2, SIN_C)
                cs[1, k, x, :, at, :] = horner(h2, COS_C)
        return carry

    lax.fori_loop(0, CX, trig, 0)

    @pl.when(has_down)
    def _():
        c_copy().start()

    frame_load.wait()
    for step in range(STEPS):
        for half in range(2):
            z = gz * CZ + 8 * half + step + lax.broadcasted_iota(jnp.int32, (1, 8, LANES), 1)
            height = (NZ // 2 - z - frames[step]).astype(jnp.float32)
            heat[step, half] = 2.4 * jnp.tanh(height * 0.125)

    def first_units(planes, halves):
        for x in planes:
            for half in halves:

                def put(f, value, x=x, half=half):
                    s1[f, x + 1, :, pl.ds(8 * half, 8), :] = value

                advance(s0, cs, x, BASE0 + 8 * half, 8 * half, heat[0, half], put)

    def z_arrived(group):
        @pl.when(has_down)
        def _():
            z_copy(group, 0).wait_recv()

        @pl.when(has_up)
        def _():
            z_copy(group, 1).wait_recv()

    def first_rims(half, carry):
        x_copy(0, 0, half).wait_recv()
        x_copy(0, 1, half).wait_recv()
        first_units((CX - 1, 0), (half,))
        x_copy(1, 0, half).start()
        x_copy(1, 1, half).start()

        @pl.when(jnp.logical_and(half == 0, has_down))
        def _():
            for way, x in ((0, CX - 1), (1, 0)):
                m_copy(x).start()
                d_copy(way).start()

        return carry

    def first_step(m, carry):
        xa = jnp.where(m < 5, 4 + 2 * m, jnp.where(m == 5, 2, 14))
        xb = jnp.where(m < 6, xa + 1, 1)

        @pl.when(jnp.logical_and(m < 5, lax.rem(m, 2) == 0))
        def _():
            z_arrived(1 + lax.div(m, 2))

        @pl.when(m == 5)
        def _():
            z_arrived(0)
            lax.fori_loop(0, 2, first_rims, 0)

        first_units((xa, xb), (0, 1))

        @pl.when(has_down)
        def _():
            m_copy(xa).start()
            m_copy(xb).start()

        return carry

    lax.fori_loop(0, 7, first_step, 0)

    def second_step(i, carry):
        xa = jnp.where(i < 4, 5 + 2 * i, jnp.where(i < 6, 11 - 2 * i, jnp.where(i == 6, 13, 0)))
        xb = jnp.where(i < 7, xa + 1, CX - 1)

        @pl.when(jnp.logical_and(has_up, i == 0))
        def _():
            c_copy().wait_recv()
            for x in range(4, 8):
                m_copy(x).wait_recv()

        @pl.when(jnp.logical_and(has_up, jnp.logical_and(i > 0, i < 7)))
        def _():
            first = jnp.where(jnp.logical_or(i < 4, i == 6), xa + 1, xa - 1)
            m_copy(first).wait_recv()
            m_copy(first + 1).wait_recv()

        @pl.when(i == 7)
        def _():
            for half in range(2):
                x_copy(1, 0, half).wait_recv()
                x_copy(1, 1, half).wait_recv()

            @pl.when(has_up)
            def _():
                d_copy(0).wait_recv()
                d_copy(1).wait_recv()

        for x in (xa, xb):
            for half in range(2):

                def put(f, value, x=x, half=half):
                    for k in range(YT):
                        o[f, x, pl.ds(8 * half, 8), pl.ds(k * LANES, LANES)] = value[k]

                advance(s1, cs, x, 1 + 8 * half, 1 + 8 * half, heat[1, half], put)
        return carry

    lax.fori_loop(0, 8, second_step, 0)

    @pl.when(jnp.logical_not(has_up))
    def _():
        def clear_top(x, carry):
            o[:, x, pl.ds(CZ - 1, 1), :] = jnp.zeros((FIELDS, 1, NY), jnp.float32)
            return carry

        lax.fori_loop(0, CX, clear_top, 0)

    for step in range(STEPS):
        for way in range(2):
            for half in range(2):
                x_copy(step, way, half).wait_send()

    @pl.when(has_up)
    def _():
        for group in range(GROUPS):
            z_copy(group, 0).wait_send()

    @pl.when(has_down)
    def _():
        for group in range(GROUPS):
            z_copy(group, 1).wait_send()
        for x in range(CX):
            m_copy(x).wait_send()
        c_copy().wait_send()
        d_copy(0).wait_send()
        d_copy(1).wait_send()


def flush(o, phase_out, solute_out, sem):
    copies = (
        pltpu.make_async_copy(o.at[pl.ds(0, ORDERS)], phase_out, sem.at[0]),
        pltpu.make_async_copy(o.at[ORDERS], solute_out, sem.at[1]),
    )
    for copy in copies:
        copy.start()
    for copy in copies:
        copy.wait()


def local(phase, solute, grain_map, frame_steps):
    hbm, vmem = pl.BlockSpec(memory_space=pltpu.HBM), pl.BlockSpec(memory_space=pltpu.VMEM)
    dma = pltpu.SemaphoreType.DMA
    args = [pltpu.with_memory_space_constraint(a, pltpu.HBM) for a in (frame_steps, phase, solute, grain_map)]
    result = pl.pallas_call(
        kernel,
        out_shape=pltpu.VMEM((FIELDS, CX, CZ, NY), jnp.float32),
        in_specs=[hbm] * 4,
        out_specs=vmem,
        scratch_shapes=[
            pltpu.VMEM((FIELDS, CX + 2, YT, 32, LANES), jnp.float32),
            pltpu.VMEM((FIELDS, CX + 2, YT, 24, LANES), jnp.float32),
            pltpu.VMEM((ORDERS, CX, YT, CZ, LANES), jnp.int32),
            pltpu.VMEM((2, ORDERS, CX, YT, 24, LANES), jnp.float32),
            pltpu.VMEM((STEPS, 2, 1, 8, LANES), jnp.float32),
            pltpu.SMEM((STEPS,), jnp.int32),
            dma((3, YT)),
            dma,
            dma((STEPS, 2, 2)),
            dma((STEPS, 2, 2)),
            dma((2, GROUPS)),
            dma((2, GROUPS)),
            dma((CX,)),
            dma((CX,)),
            dma,
            dma,
            dma((2,)),
            dma((2,)),
        ],
        compiler_params=pltpu.CompilerParams(
            collective_id=0, has_side_effects=True, vmem_limit_bytes=32 * 1024 * 1024
        ),
        name="grow",
    )(*args)
    return pl.pallas_call(
        flush,
        out_shape=(
            pltpu.HBM(phase.shape, jnp.float32),
            pltpu.HBM(solute.shape, jnp.float32),
        ),
        in_specs=[vmem],
        out_specs=(hbm, hbm),
        scratch_shapes=[dma((2,))],
        compiler_params=pltpu.CompilerParams(vmem_limit_bytes=4 * 1024 * 1024),
        name="flush",
    )(result)


def solution(mesh):
    in_specs = (P(None, "gx", "gz", None), P("gx", "gz", None), P(None, "gx", "gz", None), P())
    out_specs = (P(None, "gx", "gz", None), P("gx", "gz", None))
    return jax.shard_map(local, mesh=mesh, in_specs=in_specs, out_specs=out_specs, check_vma=False)
```

```python
import math

import jax
import jax.numpy as jnp
import numpy as np
from jax import lax
from jax.experimental import pallas as pl
from jax.experimental.pallas import tpu as pltpu
from jax.sharding import PartitionSpec as P

ORDERS = 4
FIELDS = 5
STEPS = 2
NGRAIN = 1024
NZ = 256
CX = 16
CZ = 16
NY = 512
LANES = 128
YT = NY // LANES
GROUP = 4
GROUPS = CX // GROUP
MESH = pl.DeviceIdType.MESH

BASE0 = 8


def sine_coefficients():
    nodes = np.cos(np.pi * (np.arange(400) + 0.5) / 400)
    theta = nodes * np.pi / 2
    even = np.polynomial.chebyshev.Chebyshev.fit(nodes, np.cos(theta), 8, domain=[-1, 1])
    odd = np.polynomial.chebyshev.Chebyshev.fit(nodes, np.sin(theta), 9, domain=[-1, 1])
    even = even.convert(kind=np.polynomial.Polynomial).coef
    odd = odd.convert(kind=np.polynomial.Polynomial).coef
    cos_c = [float(even[i] * math.sqrt(0.5) / 128.0**i) for i in (0, 2, 4, 6, 8)]
    sin_c = [float(odd[i] * math.sqrt(2.0) / 128.0**i) for i in (1, 3, 5, 7, 9)]
    return sin_c, cos_c


SIN_C, COS_C = sine_coefficients()


def horner(x, coefficients):
    value = coefficients[-1]
    for c in coefficients[-2::-1]:
        value = value * x + c
    return value


def next_y(rolled, offset):
    if offset > 0:
        return jnp.concatenate([rolled[1:], rolled[:1]], axis=0)
    return jnp.concatenate([rolled[-1:], rolled[:-1]], axis=0)


def neighbours(s, f, xi, row, part):
    at = pl.ds(row, 8)
    ys = slice(None) if part is None else pl.ds(2 * part, 2)
    c = s[f, xi, ys, at, :]
    xl = s[f, xi - 1, ys, at, :]
    xh = s[f, xi + 1, ys, at, :]
    zl = s[f, xi, ys, pl.ds(row - 1, 8), :]
    zh = s[f, xi, ys, pl.ds(row + 1, 8), :]
    lane = lax.broadcasted_iota(jnp.int32, c.shape, 2)
    right = pltpu.roll(c, 1, axis=2)
    left = pltpu.roll(c, LANES - 1, axis=2)
    if part is None:
        before, after = next_y(right, -1), next_y(left, 1)
    else:
        before = s[f, xi, pl.ds(lax.rem(2 * part + YT - 1, YT), 1), at, :]
        after = s[f, xi, pl.ds(lax.rem(2 * part + 2, YT), 1), at, :]
        before = jnp.concatenate([pltpu.roll(before, 1, axis=2), right[:1]], axis=0)
        after = jnp.concatenate([left[1:], pltpu.roll(after, LANES - 1, axis=2)], axis=0)
    yl = jnp.where(lane == 0, before, right)
    yh = jnp.where(lane == LANES - 1, after, left)
    return c, xl, xh, yl, yh, zl, zh


def advance(s, cs, x, row, cs_row, thermal, put, part=None):
    xi = x + 1
    ys = slice(None) if part is None else pl.ds(2 * part, 2)
    u = s[ORDERS, xi, ys, pl.ds(row, 8), :]
    drive = thermal - 2.4 * u
    q = None
    for k in range(ORDERS):
        p = s[k, xi, ys, pl.ds(row, 8), :]
        q = p * p if q is None else q + p * p
    well = 0.64 - 0.16 * q
    total = None
    for k in range(ORDERS):
        p, xl, xh, yl, yh, zl, zh = neighbours(s, k, xi, row, part)
        gx, gy, gz = xh - xl, yh - yl, zh - zl
        lap = (xl + xh) + (yl + yh) + (zl + zh) - 6.0 * p
        x2, y2, z2 = gx * gx, gy * gy, gz * gz
        r = x2 + y2
        at = pl.ds(cs_row, 8)
        t = cs[0, k, x, ys, at, :] * (gx * gy) + cs[1, k, x, ys, at, :] * (x2 - y2)
        quartic = r * r + z2 * z2 - t * t
        d = (r + z2) + 0.2
        ratio = quartic * pl.reciprocal(d * d, approx=True)
        w = p - p * p
        delta = (
            lap * (0.08 + 0.04 * ratio)
            + p * (well + p * (1.44 * p - 1.92))
            + (w * w) * drive
        )
        put(k, p + delta)
        total = delta if total is None else total + delta
    c, xl, xh, yl, yh, zl, zh = neighbours(s, ORDERS, xi, row, part)
    near = (xl + xh) + (yl + yh) + (zl + zh)
    put(ORDERS, 0.52 * c + 0.08 * near + 0.5 * total)


def second_units(o, s1, cs, heat, planes, first):
    for x in planes:
        for half in range(2):

            def put(f, value, x=x, half=half):
                for k in range(YT):
                    o[f, x - first, pl.ds(8 * half, 8), pl.ds(k * LANES, LANES)] = value[k]

            advance(s1, cs, x, 1 + 8 * half, 1 + 8 * half, heat[1, half], put)


def clear_top(o, has_up):
    @pl.when(jnp.logical_not(has_up))
    def _():
        def clear(x, carry):
            o[:, x, pl.ds(CZ - 1, 1), :] = jnp.zeros((FIELDS, 1, NY), jnp.float32)
            return carry

        lax.fori_loop(0, o.shape[1], clear, 0)


def kernel(
    frames_in, phase, solute, grain, o, s1, cs, heat,
    s0, g, frames,
    load_sem, frame_sem, x_send, x_recv, z_send, z_recv, m_send, m_recv, c_send, c_recv, d_send, d_recv,
):
    gx, gz = lax.axis_index("gx"), lax.axis_index("gz")
    n_gx, n_gz = lax.axis_size("gx"), lax.axis_size("gz")
    right, left = lax.rem(gx + 1, n_gx), lax.rem(gx + n_gx - 1, n_gx)
    has_up, has_down = gz < n_gz - 1, gz > 0

    loads = []
    for k in range(YT):
        lanes = pl.ds(k * LANES, LANES)
        rows = pl.ds(BASE0, CZ)
        loads.append(
            (
                pltpu.make_async_copy(
                    phase.at[:, :, :, lanes], s0.at[pl.ds(0, ORDERS), pl.ds(1, CX), k, rows, :], load_sem.at[0, k]
                ),
                pltpu.make_async_copy(
                    solute.at[:, :, lanes], s0.at[ORDERS, pl.ds(1, CX), k, rows, :], load_sem.at[1, k]
                ),
                pltpu.make_async_copy(grain.at[:, :, :, lanes], g.at[:, :, k, :, :], load_sem.at[2, k]),
            )
        )
    frame_load = pltpu.make_async_copy(frames_in, frames, frame_sem)
    barrier = pltpu.get_barrier_semaphore()

    def greet(ix, iz):
        pl.semaphore_signal(barrier, inc=1, device_id=(ix, iz), device_id_type=MESH)

    greet(left, gz)
    greet(right, gz)

    @pl.when(has_up)
    def _():
        greet(gx, gz + 1)

    @pl.when(has_down)
    def _():
        greet(gx, gz - 1)

    for which in range(3):
        for k in range(YT):
            loads[k][which].start()

    frame_load.start()

    @pl.when(jnp.logical_not(has_down))
    def _():
        def clear(x, carry):
            s0[:, x, :, pl.ds(BASE0 - 1, 1), :] = jnp.zeros((FIELDS, YT, 1, LANES), jnp.float32)
            return carry

        lax.fori_loop(0, CX + 2, clear, 0)

    @pl.when(jnp.logical_not(has_up))
    def _():
        def clear(x, carry):
            s0[:, x, :, pl.ds(BASE0 + CZ, 1), :] = jnp.zeros((FIELDS, YT, 1, LANES), jnp.float32)
            s1[:, x, :, pl.ds(CZ, 2), :] = jnp.zeros((FIELDS, YT, 2, LANES), jnp.float32)
            return carry

        lax.fori_loop(0, CX + 2, clear, 0)

        def clear_cs(x, carry):
            cs[:, :, x, :, pl.ds(CZ, 1), :] = jnp.zeros((2, ORDERS, YT, 1, LANES), jnp.float32)
            return carry

        lax.fori_loop(0, CX, clear_cs, 0)

    def remote(src, dst, send, recv, ix, iz):
        return pltpu.make_async_remote_copy(
            src_ref=src, dst_ref=dst, send_sem=send, recv_sem=recv, device_id=(ix, iz), device_id_type=MESH
        )

    def x_copy(step, way, piece):
        s, base = (s0, BASE0) if step == 0 else (s1, 0)
        half, part = lax.div(piece, 2), lax.rem(piece, 2)
        ys, rows = pl.ds(2 * part, 2), pl.ds(base + 8 * half, 8)
        src, dst, to = (CX, 0, right) if way == 0 else (1, CX + 1, left)
        return remote(
            s.at[:, src, ys, rows, :],
            s.at[:, dst, ys, rows, :],
            x_send.at[step, way, piece],
            x_recv.at[step, way, piece],
            to,
            gz,
        )

    def z_copy(group, way):
        planes = pl.ds(1 + group * GROUP, GROUP)
        src, dst, to = (BASE0 + CZ - 1, BASE0 - 1, gz + 1) if way == 0 else (BASE0, BASE0 + CZ, gz - 1)
        return remote(
            s0.at[:, planes, :, pl.ds(src, 1), :],
            s0.at[:, planes, :, pl.ds(dst, 1), :],
            z_send.at[way, group],
            z_recv.at[way, group],
            gx,
            to,
        )

    def m_copy(x):
        return remote(
            s1.at[:, x + 1, :, pl.ds(0, 2), :],
            s1.at[:, x + 1, :, pl.ds(CZ, 2), :],
            m_send.at[x],
            m_recv.at[x],
            gx,
            gz - 1,
        )

    def d_copy(way):
        src, dst, to = (CX, 0, right) if way == 0 else (1, CX + 1, left)
        return remote(
            s1.at[:, src, :, pl.ds(0, 1), :],
            s1.at[:, dst, :, pl.ds(CZ, 1), :],
            d_send.at[way],
            d_recv.at[way],
            to,
            gz - 1,
        )

    def c_copy():
        return remote(
            cs.at[:, :, :, :, pl.ds(0, 1), :], cs.at[:, :, :, :, pl.ds(CZ, 1), :], c_send, c_recv, gx, gz - 1
        )

    for which in range(2):
        for k in range(YT):
            loads[k][which].wait()

    pl.semaphore_wait(barrier, 2 + has_up.astype(jnp.int32) + has_down.astype(jnp.int32))

    for piece in range(4):
        x_copy(0, 0, piece).start()
        x_copy(0, 1, piece).start()
    for group in (1, 2, 3, 0):

        @pl.when(has_up)
        def _(group=group):
            z_copy(group, 0).start()

        @pl.when(has_down)
        def _(group=group):
            z_copy(group, 1).start()

    for k in range(YT):
        loads[k][2].wait()

    def trig(x, carry):
        for k in range(ORDERS):
            for half in range(2):
                at = pl.ds(8 * half, 8)
                h = ((g[k, x, :, at, :] & 255) - 128).astype(jnp.float32)
                h2 = h * h
                cs[0, k, x, :, at, :] = h * horner(h2, SIN_C)
                cs[1, k, x, :, at, :] = horner(h2, COS_C)
        return carry

    lax.fori_loop(0, CX, trig, 0)

    @pl.when(has_down)
    def _():
        c_copy().start()

    frame_load.wait()
    for step in range(STEPS):
        for half in range(2):
            z = gz * CZ + 8 * half + step + lax.broadcasted_iota(jnp.int32, (1, 8, LANES), 1)
            height = (NZ // 2 - z - frames[step]).astype(jnp.float32)
            heat[step, half] = 2.4 * jnp.tanh(height * 0.125)

    def first_units(planes, halves):
        for x in planes:
            for half in halves:

                def put(f, value, x=x, half=half):
                    s1[f, x + 1, :, pl.ds(8 * half, 8), :] = value

                advance(s0, cs, x, BASE0 + 8 * half, 8 * half, heat[0, half], put)

    def z_arrived(group):
        @pl.when(has_down)
        def _():
            z_copy(group, 0).wait_recv()

        @pl.when(has_up)
        def _():
            z_copy(group, 1).wait_recv()

    def first_rims(piece, carry):
        half, part = lax.div(piece, 2), lax.rem(piece, 2)
        x_copy(0, 0, piece).wait_recv()
        x_copy(0, 1, piece).wait_recv()
        for x in (CX - 1, 0):

            def put(f, value, x=x):
                s1[f, x + 1, pl.ds(2 * part, 2), pl.ds(pl.multiple_of(8 * half, 8), 8), :] = value

            advance(s0, cs, x, BASE0 + 8 * half, 8 * half, heat[0, half], put, part)
        x_copy(1, 0, piece).start()
        x_copy(1, 1, piece).start()

        @pl.when(jnp.logical_and(piece == 1, has_down))
        def _():
            for way, x in ((0, CX - 1), (1, 0)):
                m_copy(x).start()
                d_copy(way).start()

        return carry

    def first_step(m, carry):
        xa = jnp.where(m < 5, 4 + 2 * m, jnp.where(m == 5, 2, 14))
        xb = jnp.where(m < 6, xa + 1, 1)

        @pl.when(jnp.logical_and(m < 5, lax.rem(m, 2) == 0))
        def _():
            z_arrived(1 + lax.div(m, 2))

        @pl.when(m == 5)
        def _():
            z_arrived(0)
            lax.fori_loop(0, 4, first_rims, 0)

        first_units((xa, xb), (0, 1))

        @pl.when(has_down)
        def _():
            m_copy(xa).start()
            m_copy(xb).start()

        return carry

    lax.fori_loop(0, 7, first_step, 0)

    def second_step(i, carry):
        xa = jnp.where(i < 4, 5 + 2 * i, jnp.where(i < 6, 11 - 2 * i, 13))

        @pl.when(jnp.logical_and(has_up, i == 0))
        def _():
            c_copy().wait_recv()
            for x in range(4, 8):
                m_copy(x).wait_recv()

        @pl.when(jnp.logical_and(has_up, i > 0))
        def _():
            first = jnp.where(jnp.logical_or(i < 4, i == 6), xa + 1, xa - 1)
            m_copy(first).wait_recv()
            m_copy(first + 1).wait_recv()

        second_units(o, s1, cs, heat, (xa, xa + 1), 0)
        return carry

    lax.fori_loop(0, 7, second_step, 0)
    clear_top(o, has_up)

    for way in range(2):
        for piece in range(4):
            x_copy(0, way, piece).wait_send()

    @pl.when(has_up)
    def _():
        for group in range(GROUPS):
            z_copy(group, 0).wait_send()

    @pl.when(has_down)
    def _():
        for group in range(GROUPS):
            z_copy(group, 1).wait_send()
        for x in range(CX):
            m_copy(x).wait_send()
        c_copy().wait_send()
        d_copy(0).wait_send()
        d_copy(1).wait_send()

    @pl.when(has_up)
    def _():
        d_copy(0).wait_recv()
        d_copy(1).wait_recv()

    for way in range(2):
        for piece in range(4):
            x_copy(1, way, piece).wait()


def finish(o, s1, cs, heat, phase_out, solute_out, rims, sem):
    inner = pl.ds(1, CX - 2)
    copies = [
        pltpu.make_async_copy(o.at[pl.ds(0, ORDERS), inner], phase_out.at[:, inner], sem.at[0]),
        pltpu.make_async_copy(o.at[ORDERS, inner], solute_out.at[inner], sem.at[1]),
    ]
    for copy in copies:
        copy.start()
    for i, x in enumerate((0, CX - 1)):
        second_units(rims.at[:, pl.ds(i, 1)], s1, cs, heat, (x,), x)
    clear_top(rims, lax.axis_index("gz") < lax.axis_size("gz") - 1)
    for i, x in enumerate((0, CX - 1)):
        ends = [
            pltpu.make_async_copy(rims.at[pl.ds(0, ORDERS), i], phase_out.at[:, x], sem.at[2 + 2 * i]),
            pltpu.make_async_copy(rims.at[ORDERS, i], solute_out.at[x], sem.at[3 + 2 * i]),
        ]
        for copy in ends:
            copy.start()
        copies += ends
    for copy in copies:
        copy.wait()


def local(phase, solute, grain_map, frame_steps):
    hbm, vmem = pl.BlockSpec(memory_space=pltpu.HBM), pl.BlockSpec(memory_space=pltpu.VMEM)
    dma = pltpu.SemaphoreType.DMA
    args = [pltpu.with_memory_space_constraint(a, pltpu.HBM) for a in (frame_steps, phase, solute, grain_map)]
    results = pl.pallas_call(
        kernel,
        out_shape=(
            pltpu.VMEM((FIELDS, CX, CZ, NY), jnp.float32),
            pltpu.VMEM((FIELDS, CX + 2, YT, 24, LANES), jnp.float32),
            pltpu.VMEM((2, ORDERS, CX, YT, 24, LANES), jnp.float32),
            pltpu.VMEM((STEPS, 2, 1, 8, LANES), jnp.float32),
        ),
        in_specs=[hbm] * 4,
        out_specs=(vmem,) * 4,
        scratch_shapes=[
            pltpu.VMEM((FIELDS, CX + 2, YT, 32, LANES), jnp.float32),
            pltpu.VMEM((ORDERS, CX, YT, CZ, LANES), jnp.int32),
            pltpu.SMEM((STEPS,), jnp.int32),
            dma((3, YT)),
            dma,
            dma((STEPS, 2, 4)),
            dma((STEPS, 2, 4)),
            dma((2, GROUPS)),
            dma((2, GROUPS)),
            dma((CX,)),
            dma((CX,)),
            dma,
            dma,
            dma((2,)),
            dma((2,)),
        ],
        compiler_params=pltpu.CompilerParams(
            collective_id=0, has_side_effects=True, vmem_limit_bytes=32 * 1024 * 1024
        ),
        name="grow",
    )(*args)
    return pl.pallas_call(
        finish,
        out_shape=(
            pltpu.HBM(phase.shape, jnp.float32),
            pltpu.HBM(solute.shape, jnp.float32),
        ),
        in_specs=[vmem] * 4,
        out_specs=(hbm, hbm),
        scratch_shapes=[pltpu.VMEM((FIELDS, 2, CZ, NY), jnp.float32), dma((6,))],
        compiler_params=pltpu.CompilerParams(vmem_limit_bytes=16 * 1024 * 1024),
        name="finish",
    )(*results)


def solution(mesh):
    in_specs = (P(None, "gx", "gz", None), P("gx", "gz", None), P(None, "gx", "gz", None), P())
    out_specs = (P(None, "gx", "gz", None), P("gx", "gz", None))
    return jax.shard_map(local, mesh=mesh, in_specs=in_specs, out_specs=out_specs, check_vma=False)
```

```python
import math

import jax
import jax.numpy as jnp
import numpy as np
from jax import lax
from jax.experimental import pallas as pl
from jax.experimental.pallas import tpu as pltpu
from jax.sharding import PartitionSpec as P

ORDERS = 4
FIELDS = 5
STEPS = 2
NGRAIN = 1024
NZ = 256
CX = 16
CZ = 16
NY = 512
LANES = 128
YT = NY // LANES
GROUP = 4
GROUPS = CX // GROUP
MESH = pl.DeviceIdType.MESH

BASE0 = 8

RIMS_AT = 5


def sine_coefficients():
    nodes = np.cos(np.pi * (np.arange(400) + 0.5) / 400)
    theta = nodes * np.pi / 2
    even = np.polynomial.chebyshev.Chebyshev.fit(nodes, np.cos(theta), 8, domain=[-1, 1])
    odd = np.polynomial.chebyshev.Chebyshev.fit(nodes, np.sin(theta), 9, domain=[-1, 1])
    even = even.convert(kind=np.polynomial.Polynomial).coef
    odd = odd.convert(kind=np.polynomial.Polynomial).coef
    cos_c = [float(even[i] * math.sqrt(0.5) / 128.0**i) for i in (0, 2, 4, 6, 8)]
    sin_c = [float(odd[i] * math.sqrt(2.0) / 128.0**i) for i in (1, 3, 5, 7, 9)]
    return sin_c, cos_c


SIN_C, COS_C = sine_coefficients()


def horner(x, coefficients):
    value = coefficients[-1]
    for c in coefficients[-2::-1]:
        value = value * x + c
    return value


def next_y(rolled, offset):
    if offset > 0:
        return jnp.concatenate([rolled[1:], rolled[:1]], axis=0)
    return jnp.concatenate([rolled[-1:], rolled[:-1]], axis=0)


def neighbours(s, f, xi, row, part):
    at = pl.ds(row, 8)
    ys = slice(None) if part is None else pl.ds(2 * part, 2)
    c = s[f, xi, ys, at, :]
    xl = s[f, xi - 1, ys, at, :]
    xh = s[f, xi + 1, ys, at, :]
    zl = s[f, xi, ys, pl.ds(row - 1, 8), :]
    zh = s[f, xi, ys, pl.ds(row + 1, 8), :]
    lane = lax.broadcasted_iota(jnp.int32, c.shape, 2)
    right = pltpu.roll(c, 1, axis=2)
    left = pltpu.roll(c, LANES - 1, axis=2)
    if part is None:
        before, after = next_y(right, -1), next_y(left, 1)
    else:
        before = s[f, xi, pl.ds(lax.rem(2 * part + YT - 1, YT), 1), at, :]
        after = s[f, xi, pl.ds(lax.rem(2 * part + 2, YT), 1), at, :]
        before = jnp.concatenate([pltpu.roll(before, 1, axis=2), right[:1]], axis=0)
        after = jnp.concatenate([left[1:], pltpu.roll(after, LANES - 1, axis=2)], axis=0)
    yl = jnp.where(lane == 0, before, right)
    yh = jnp.where(lane == LANES - 1, after, left)
    return c, xl, xh, yl, yh, zl, zh


def advance(s, cs, x, row, cs_row, thermal, put, part=None):
    xi = x + 1
    ys = slice(None) if part is None else pl.ds(2 * part, 2)
    u = s[ORDERS, xi, ys, pl.ds(row, 8), :]
    drive = thermal - 2.4 * u
    q = None
    for k in range(ORDERS):
        p = s[k, xi, ys, pl.ds(row, 8), :]
        q = p * p if q is None else q + p * p
    well = 0.64 - 0.16 * q
    total = None
    for k in range(ORDERS):
        p, xl, xh, yl, yh, zl, zh = neighbours(s, k, xi, row, part)
        gx, gy, gz = xh - xl, yh - yl, zh - zl
        lap = (xl + xh) + (yl + yh) + (zl + zh) - 6.0 * p
        x2, y2, z2 = gx * gx, gy * gy, gz * gz
        r = x2 + y2
        at = pl.ds(cs_row, 8)
        t = cs[0, k, x, ys, at, :] * (gx * gy) + cs[1, k, x, ys, at, :] * (x2 - y2)
        quartic = r * r + z2 * z2 - t * t
        d = (r + z2) + 0.2
        ratio = quartic * pl.reciprocal(d * d, approx=True)
        w = p - p * p
        delta = (
            lap * (0.08 + 0.04 * ratio)
            + p * (well + p * (1.44 * p - 1.92))
            + (w * w) * drive
        )
        put(k, p + delta)
        total = delta if total is None else total + delta
    c, xl, xh, yl, yh, zl, zh = neighbours(s, ORDERS, xi, row, part)
    near = (xl + xh) + (yl + yh) + (zl + zh)
    put(ORDERS, 0.52 * c + 0.08 * near + 0.5 * total)


def tile(half):
    return pl.ds(8 * half if isinstance(half, int) else pl.multiple_of(8 * half, 8), 8)


def second_units(o, s1, cs, heat, units, first):
    for x, half in units:

        def put(f, value, x=x, half=half):
            for k in range(YT):
                o[f, x - first, tile(half), pl.ds(k * LANES, LANES)] = value[k]

        advance(s1, cs, x, 1 + 8 * half, 1 + 8 * half, heat[1, half], put)


def clear_top(o, has_up):
    @pl.when(jnp.logical_not(has_up))
    def _():
        def clear(x, carry):
            o[:, x, pl.ds(CZ - 1, 1), :] = jnp.zeros((FIELDS, 1, NY), jnp.float32)
            return carry

        lax.fori_loop(0, o.shape[1], clear, 0)


def kernel(
    frames_in, phase, solute, grain, o, s1, cs, heat,
    s0, g, frames,
    load_sem, frame_sem, x_send, x_recv, z_send, z_recv, m_send, m_recv, c_send, c_recv, d_send, d_recv,
):
    gx, gz = lax.axis_index("gx"), lax.axis_index("gz")
    n_gx, n_gz = lax.axis_size("gx"), lax.axis_size("gz")
    right, left = lax.rem(gx + 1, n_gx), lax.rem(gx + n_gx - 1, n_gx)
    has_up, has_down = gz < n_gz - 1, gz > 0

    loads = []
    for k in range(YT):
        lanes = pl.ds(k * LANES, LANES)
        rows = pl.ds(BASE0, CZ)
        loads.append(
            (
                pltpu.make_async_copy(
                    phase.at[:, :, :, lanes], s0.at[pl.ds(0, ORDERS), pl.ds(1, CX), k, rows, :], load_sem.at[0, k]
                ),
                pltpu.make_async_copy(
                    solute.at[:, :, lanes], s0.at[ORDERS, pl.ds(1, CX), k, rows, :], load_sem.at[1, k]
                ),
                pltpu.make_async_copy(grain.at[:, :, :, lanes], g.at[:, :, k, :, :], load_sem.at[2, k]),
            )
        )
    frame_load = pltpu.make_async_copy(frames_in, frames, frame_sem)
    barrier = pltpu.get_barrier_semaphore()

    def greet(ix, iz):
        pl.semaphore_signal(barrier, inc=1, device_id=(ix, iz), device_id_type=MESH)

    greet(left, gz)
    greet(right, gz)

    @pl.when(has_up)
    def _():
        greet(gx, gz + 1)

    @pl.when(has_down)
    def _():
        greet(gx, gz - 1)

    for which in range(3):
        for k in range(YT):
            loads[k][which].start()

    frame_load.start()

    @pl.when(jnp.logical_not(has_down))
    def _():
        def clear(x, carry):
            s0[:, x, :, pl.ds(BASE0 - 1, 1), :] = jnp.zeros((FIELDS, YT, 1, LANES), jnp.float32)
            return carry

        lax.fori_loop(0, CX + 2, clear, 0)

    @pl.when(jnp.logical_not(has_up))
    def _():
        def clear(x, carry):
            s0[:, x, :, pl.ds(BASE0 + CZ, 1), :] = jnp.zeros((FIELDS, YT, 1, LANES), jnp.float32)
            s1[:, x, :, pl.ds(CZ, 2), :] = jnp.zeros((FIELDS, YT, 2, LANES), jnp.float32)
            return carry

        lax.fori_loop(0, CX + 2, clear, 0)

        def clear_cs(x, carry):
            cs[:, :, x, :, pl.ds(CZ, 1), :] = jnp.zeros((2, ORDERS, YT, 1, LANES), jnp.float32)
            return carry

        lax.fori_loop(0, CX, clear_cs, 0)

    def remote(src, dst, send, recv, ix, iz):
        return pltpu.make_async_remote_copy(
            src_ref=src, dst_ref=dst, send_sem=send, recv_sem=recv, device_id=(ix, iz), device_id_type=MESH
        )

    def x_copy(step, way, piece):
        s, base = (s0, BASE0) if step == 0 else (s1, 0)
        half, part = lax.div(piece, 2), lax.rem(piece, 2)
        ys, rows = pl.ds(2 * part, 2), pl.ds(base + 8 * half, 8)
        src, dst, to = (CX, 0, right) if way == 0 else (1, CX + 1, left)
        return remote(
            s.at[:, src, ys, rows, :],
            s.at[:, dst, ys, rows, :],
            x_send.at[step, way, piece],
            x_recv.at[step, way, piece],
            to,
            gz,
        )

    def z_copy(group, way):
        planes = pl.ds(1 + group * GROUP, GROUP)
        src, dst, to = (BASE0 + CZ - 1, BASE0 - 1, gz + 1) if way == 0 else (BASE0, BASE0 + CZ, gz - 1)
        return remote(
            s0.at[:, planes, :, pl.ds(src, 1), :],
            s0.at[:, planes, :, pl.ds(dst, 1), :],
            z_send.at[way, group],
            z_recv.at[way, group],
            gx,
            to,
        )

    def m_copy(x):
        return remote(
            s1.at[:, x + 1, :, pl.ds(0, 2), :],
            s1.at[:, x + 1, :, pl.ds(CZ, 2), :],
            m_send.at[x],
            m_recv.at[x],
            gx,
            gz - 1,
        )

    def d_copy(way):
        src, dst, to = (CX, 0, right) if way == 0 else (1, CX + 1, left)
        return remote(
            s1.at[:, src, :, pl.ds(0, 1), :],
            s1.at[:, dst, :, pl.ds(CZ, 1), :],
            d_send.at[way],
            d_recv.at[way],
            to,
            gz - 1,
        )

    def c_copy():
        return remote(
            cs.at[:, :, :, :, pl.ds(0, 1), :], cs.at[:, :, :, :, pl.ds(CZ, 1), :], c_send, c_recv, gx, gz - 1
        )

    for which in range(2):
        for k in range(YT):
            loads[k][which].wait()

    pl.semaphore_wait(barrier, 2 + has_up.astype(jnp.int32) + has_down.astype(jnp.int32))

    for piece in range(4):
        x_copy(0, 0, piece).start()
        x_copy(0, 1, piece).start()
    for group in (1, 2, 3, 0):

        @pl.when(has_up)
        def _(group=group):
            z_copy(group, 0).start()

        @pl.when(has_down)
        def _(group=group):
            z_copy(group, 1).start()

    for k in range(YT):
        loads[k][2].wait()

    def trig(x, carry):
        for k in range(ORDERS):
            for half in range(2):
                at = pl.ds(8 * half, 8)
                h = ((g[k, x, :, at, :] & 255) - 128).astype(jnp.float32)
                h2 = h * h
                cs[0, k, x, :, at, :] = h * horner(h2, SIN_C)
                cs[1, k, x, :, at, :] = horner(h2, COS_C)
        return carry

    lax.fori_loop(0, CX, trig, 0)

    @pl.when(has_down)
    def _():
        c_copy().start()

    frame_load.wait()
    for step in range(STEPS):
        for half in range(2):
            z = gz * CZ + 8 * half + step + lax.broadcasted_iota(jnp.int32, (1, 8, LANES), 1)
            height = (NZ // 2 - z - frames[step]).astype(jnp.float32)
            heat[step, half] = 2.4 * jnp.tanh(height * 0.125)

    def first_units(units):
        for x, half in units:

            def put(f, value, x=x, half=half):
                s1[f, x + 1, :, tile(half), :] = value

            advance(s0, cs, x, BASE0 + 8 * half, 8 * half, heat[0, half], put)

    def units_of(group, lower, upper):
        xa = jnp.where(group < 3, 4 + 4 * group, 14)
        xb = jnp.where(group < 3, xa + 1, 1)
        xc = jnp.where(group < 2, xa + 2, jnp.where(group == 2, 2, 14))
        xd = jnp.where(group < 3, xc + 1, 1)
        return ((xa, lower), (xb, lower), (xc, upper), (xd, upper))

    def first_rims(piece, carry):
        half, part = lax.div(piece, 2), lax.rem(piece, 2)
        x_copy(0, 0, piece).wait_recv()
        x_copy(0, 1, piece).wait_recv()
        for x in (CX - 1, 0):

            def put(f, value, x=x):
                s1[f, x + 1, pl.ds(2 * part, 2), tile(half), :] = value

            advance(s0, cs, x, BASE0 + 8 * half, 8 * half, heat[0, half], put, part)
        x_copy(1, 0, piece).start()
        x_copy(1, 1, piece).start()

        @pl.when(jnp.logical_and(piece == 1, has_down))
        def _():
            for way, x in ((0, CX - 1), (1, 0)):
                m_copy(x).start()
                d_copy(way).start()

        return carry

    def first_step(i, carry):
        group = jnp.where(i < 4, i, i - 4)

        @pl.when(jnp.logical_and(has_down, i < 3))
        def _():
            z_copy(i + 1, 0).wait_recv()

        @pl.when(jnp.logical_and(has_down, i == 2))
        def _():
            z_copy(0, 0).wait_recv()

        @pl.when(jnp.logical_and(has_up, i == 3))
        def _():
            for every in (1, 2, 3, 0):
                z_copy(every, 1).wait_recv()

        @pl.when(i == RIMS_AT)
        def _():
            lax.fori_loop(0, 4, first_rims, 0)

        units = units_of(group, lax.div(i, 4), jnp.where(i < 3, 0, 1))
        first_units(units)

        @pl.when(jnp.logical_and(has_down, i < 4))
        def _():
            m_copy(units[0][0]).start()
            m_copy(units[1][0]).start()

            @pl.when(i < 3)
            def _():
                m_copy(units[2][0]).start()
                m_copy(units[3][0]).start()

        return carry

    lax.fori_loop(0, 7, first_step, 0)

    def second_step(i, carry):
        @pl.when(jnp.logical_and(has_up, i == 3))
        def _():
            c_copy().wait_recv()
            for x in range(3, 9):
                m_copy(x).wait_recv()

        @pl.when(jnp.logical_and(has_up, i == 4))
        def _():
            for x in range(9, 13):
                m_copy(x).wait_recv()

        @pl.when(jnp.logical_and(has_up, i == 5))
        def _():
            for x in (13, 14, 1, 2):
                m_copy(x).wait_recv()

        @pl.when(jnp.logical_and(has_up, i == 6))
        def _():
            m_copy(CX - 1).wait_recv()
            m_copy(0).wait_recv()

        group = jnp.where(i < 3, i, i - 3)
        second_units(o, s1, cs, heat, units_of(group, jnp.where(jnp.logical_and(i >= 3, i < 6), 1, 0), jnp.where(i < 3, 0, 1)), 0)
        return carry

    lax.fori_loop(0, 7, second_step, 0)
    clear_top(o, has_up)

    for way in range(2):
        for piece in range(4):
            x_copy(0, way, piece).wait_send()

    @pl.when(has_up)
    def _():
        for group in range(GROUPS):
            z_copy(group, 0).wait_send()

    @pl.when(has_down)
    def _():
        for group in range(GROUPS):
            z_copy(group, 1).wait_send()
        for x in range(CX):
            m_copy(x).wait_send()
        c_copy().wait_send()
        d_copy(0).wait_send()
        d_copy(1).wait_send()

    @pl.when(has_up)
    def _():
        d_copy(0).wait_recv()
        d_copy(1).wait_recv()

    for way in range(2):
        for piece in range(4):
            x_copy(1, way, piece).wait()


def finish(o, s1, cs, heat, phase_out, solute_out, rims, sem):
    inner = pl.ds(1, CX - 2)
    copies = [
        pltpu.make_async_copy(o.at[pl.ds(0, ORDERS), inner], phase_out.at[:, inner], sem.at[0]),
        pltpu.make_async_copy(o.at[ORDERS, inner], solute_out.at[inner], sem.at[1]),
    ]
    for copy in copies:
        copy.start()
    for i, x in enumerate((0, CX - 1)):
        second_units(rims.at[:, pl.ds(i, 1)], s1, cs, heat, ((x, 0), (x, 1)), x)
    clear_top(rims, lax.axis_index("gz") < lax.axis_size("gz") - 1)
    for i, x in enumerate((0, CX - 1)):
        ends = [
            pltpu.make_async_copy(rims.at[pl.ds(0, ORDERS), i], phase_out.at[:, x], sem.at[2 + 2 * i]),
            pltpu.make_async_copy(rims.at[ORDERS, i], solute_out.at[x], sem.at[3 + 2 * i]),
        ]
        for copy in ends:
            copy.start()
        copies += ends
    for copy in copies:
        copy.wait()


def local(phase, solute, grain_map, frame_steps):
    hbm, vmem = pl.BlockSpec(memory_space=pltpu.HBM), pl.BlockSpec(memory_space=pltpu.VMEM)
    dma = pltpu.SemaphoreType.DMA
    args = [pltpu.with_memory_space_constraint(a, pltpu.HBM) for a in (frame_steps, phase, solute, grain_map)]
    results = pl.pallas_call(
        kernel,
        out_shape=(
            pltpu.VMEM((FIELDS, CX, CZ, NY), jnp.float32),
            pltpu.VMEM((FIELDS, CX + 2, YT, 24, LANES), jnp.float32),
            pltpu.VMEM((2, ORDERS, CX, YT, 24, LANES), jnp.float32),
            pltpu.VMEM((STEPS, 2, 1, 8, LANES), jnp.float32),
        ),
        in_specs=[hbm] * 4,
        out_specs=(vmem,) * 4,
        scratch_shapes=[
            pltpu.VMEM((FIELDS, CX + 2, YT, 32, LANES), jnp.float32),
            pltpu.VMEM((ORDERS, CX, YT, CZ, LANES), jnp.int32),
            pltpu.SMEM((STEPS,), jnp.int32),
            dma((3, YT)),
            dma,
            dma((STEPS, 2, 4)),
            dma((STEPS, 2, 4)),
            dma((2, GROUPS)),
            dma((2, GROUPS)),
            dma((CX,)),
            dma((CX,)),
            dma,
            dma,
            dma((2,)),
            dma((2,)),
        ],
        compiler_params=pltpu.CompilerParams(
            collective_id=0, has_side_effects=True, vmem_limit_bytes=32 * 1024 * 1024
        ),
        name="grow",
    )(*args)
    return pl.pallas_call(
        finish,
        out_shape=(
            pltpu.HBM(phase.shape, jnp.float32),
            pltpu.HBM(solute.shape, jnp.float32),
        ),
        in_specs=[vmem] * 4,
        out_specs=(hbm, hbm),
        scratch_shapes=[pltpu.VMEM((FIELDS, 2, CZ, NY), jnp.float32), dma((6,))],
        compiler_params=pltpu.CompilerParams(vmem_limit_bytes=16 * 1024 * 1024),
        name="finish",
    )(*results)


def solution(mesh):
    in_specs = (P(None, "gx", "gz", None), P("gx", "gz", None), P(None, "gx", "gz", None), P())
    out_specs = (P(None, "gx", "gz", None), P("gx", "gz", None))
    return jax.shard_map(local, mesh=mesh, in_specs=in_specs, out_specs=out_specs, check_vma=False)
```

```python
import math

import jax
import jax.numpy as jnp
import numpy as np
from jax import lax
from jax.experimental import pallas as pl
from jax.experimental.pallas import tpu as pltpu
from jax.sharding import PartitionSpec as P

ORDERS = 4
FIELDS = 5
STEPS = 2
NGRAIN = 1024
NZ = 256
CX = 16
CZ = 16
NY = 512
LANES = 128
YT = NY // LANES
GROUP = 4
GROUPS = CX // GROUP
MESH = pl.DeviceIdType.MESH

BASE0 = 8

RIMS_AT = 5


def sine_coefficients():
    nodes = np.cos(np.pi * (np.arange(400) + 0.5) / 400)
    theta = nodes * np.pi / 2
    even = np.polynomial.chebyshev.Chebyshev.fit(nodes, np.cos(theta), 8, domain=[-1, 1])
    odd = np.polynomial.chebyshev.Chebyshev.fit(nodes, np.sin(theta), 9, domain=[-1, 1])
    even = even.convert(kind=np.polynomial.Polynomial).coef
    odd = odd.convert(kind=np.polynomial.Polynomial).coef
    cos_c = [float(even[i] * math.sqrt(0.5) / 128.0**i) for i in (0, 2, 4, 6, 8)]
    sin_c = [float(odd[i] * math.sqrt(2.0) / 128.0**i) for i in (1, 3, 5, 7, 9)]
    return sin_c, cos_c


SIN_C, COS_C = sine_coefficients()


def horner(x, coefficients):
    value = coefficients[-1]
    for c in coefficients[-2::-1]:
        value = value * x + c
    return value


def next_y(rolled, offset):
    if offset > 0:
        return jnp.concatenate([rolled[1:], rolled[:1]], axis=0)
    return jnp.concatenate([rolled[-1:], rolled[:-1]], axis=0)


def neighbours(s, f, xi, row):
    at = pl.ds(row, 8)
    c = s[f, xi, :, at, :]
    xl = s[f, xi - 1, :, at, :]
    xh = s[f, xi + 1, :, at, :]
    zl = s[f, xi, :, pl.ds(row - 1, 8), :]
    zh = s[f, xi, :, pl.ds(row + 1, 8), :]
    lane = lax.broadcasted_iota(jnp.int32, c.shape, 2)
    right = pltpu.roll(c, 1, axis=2)
    left = pltpu.roll(c, LANES - 1, axis=2)
    yl = jnp.where(lane == 0, next_y(right, -1), right)
    yh = jnp.where(lane == LANES - 1, next_y(left, 1), left)
    return c, xl, xh, yl, yh, zl, zh


def advance(s, xi, row, cs, ci, cs_row, thermal, put):
    u = s[ORDERS, xi, :, pl.ds(row, 8), :]
    drive = thermal - 2.4 * u
    q = None
    for k in range(ORDERS):
        p = s[k, xi, :, pl.ds(row, 8), :]
        q = p * p if q is None else q + p * p
    well = 0.64 - 0.16 * q
    total = None
    for k in range(ORDERS):
        p, xl, xh, yl, yh, zl, zh = neighbours(s, k, xi, row)
        gx, gy, gz = xh - xl, yh - yl, zh - zl
        lap = (xl + xh) + (yl + yh) + (zl + zh) - 6.0 * p
        x2, y2, z2 = gx * gx, gy * gy, gz * gz
        r = x2 + y2
        at = pl.ds(cs_row, 8)
        t = cs[0, k, ci, :, at, :] * (gx * gy) + cs[1, k, ci, :, at, :] * (x2 - y2)
        quartic = r * r + z2 * z2 - t * t
        d = (r + z2) + 0.2
        ratio = quartic * pl.reciprocal(d * d, approx=True)
        w = p - p * p
        delta = (
            lap * (0.08 + 0.04 * ratio)
            + p * (well + p * (1.44 * p - 1.92))
            + (w * w) * drive
        )
        put(k, p + delta)
        total = delta if total is None else total + delta
    c, xl, xh, yl, yh, zl, zh = neighbours(s, ORDERS, xi, row)
    near = (xl + xh) + (yl + yh) + (zl + zh)
    put(ORDERS, 0.52 * c + 0.08 * near + 0.5 * total)


def tile(half):
    return pl.ds(8 * half if isinstance(half, int) else pl.multiple_of(8 * half, 8), 8)


def first_units(s0, s1, cs, heat, units):
    for x, half in units:

        def put(f, value, x=x, half=half):
            s1[f, x + 1, :, tile(half), :] = value

        advance(s0, x + 2, BASE0 + 8 * half, cs, x + 1, 8 * half, heat[0, half], put)


def second_units(o, s1, cs, heat, units, first):
    for x, half in units:

        def put(f, value, x=x, half=half):
            for k in range(YT):
                o[f, x - first, tile(half), pl.ds(k * LANES, LANES)] = value[k]

        advance(s1, x + 1, 1 + 8 * half, cs, x + 1, 1 + 8 * half, heat[1, half], put)


def clear_top(o, has_up):
    @pl.when(jnp.logical_not(has_up))
    def _():
        def clear(x, carry):
            o[:, x, pl.ds(CZ - 1, 1), :] = jnp.zeros((FIELDS, 1, NY), jnp.float32)
            return carry

        lax.fori_loop(0, o.shape[1], clear, 0)


def store_trig(cs, k, ci, at, ys, grain):
    h = ((grain & 255) - 128).astype(jnp.float32)
    h2 = h * h
    cs[0, k, ci, ys, at, :] = h * horner(h2, SIN_C)
    cs[1, k, ci, ys, at, :] = horner(h2, COS_C)


def kernel(
    frames_in, phase, solute, grain, o, s1, cs, heat,
    s0, g, xh, gh, frames,
    load_sem, frame_sem, near_sem, x_send, x_recv, z_send, z_recv, m_send, m_recv, c_send, c_recv, f_send, f_recv,
):
    gx, gz = lax.axis_index("gx"), lax.axis_index("gz")
    n_gx, n_gz = lax.axis_size("gx"), lax.axis_size("gz")
    right, left = lax.rem(gx + 1, n_gx), lax.rem(gx + n_gx - 1, n_gx)
    has_up, has_down = gz < n_gz - 1, gz > 0

    barrier = pltpu.get_barrier_semaphore()

    def greet(ix, iz):
        pl.semaphore_signal(barrier, inc=1, device_id=(ix, iz), device_id_type=MESH)

    greet(left, gz)

    @pl.when(has_up)
    def _():
        greet(gx, gz + 1)

    @pl.when(has_down)
    def _():
        greet(gx, gz - 1)

    loads = []
    for k in range(YT):
        lanes = pl.ds(k * LANES, LANES)
        rows = pl.ds(BASE0, CZ)
        loads.append(
            (
                pltpu.make_async_copy(
                    phase.at[:, :, :, lanes], s0.at[pl.ds(0, ORDERS), pl.ds(2, CX), k, rows, :], load_sem.at[0, k]
                ),
                pltpu.make_async_copy(
                    solute.at[:, :, lanes], s0.at[ORDERS, pl.ds(2, CX), k, rows, :], load_sem.at[1, k]
                ),
                pltpu.make_async_copy(grain.at[:, :, :, lanes], g.at[:, :, k, :, :], load_sem.at[2, k]),
            )
        )
    frame_load = pltpu.make_async_copy(frames_in, frames, frame_sem)
    for which in range(3):
        for k in range(YT):
            loads[k][which].start()
    frame_load.start()

    def remote(src, dst, send, recv, ix, iz):
        return pltpu.make_async_remote_copy(
            src_ref=src, dst_ref=dst, send_sem=send, recv_sem=recv, device_id=(ix, iz), device_id_type=MESH
        )

    def x_copy(way, i):
        outer, inner, to = (CX - 1, CX - 2, right) if way == 0 else (0, 1, left)
        orders = pl.ds(0, ORDERS)
        src, dst = (
            (phase.at[:, outer], xh.at[way, 0, orders]),
            (solute.at[outer], xh.at[way, 0, ORDERS]),
            (grain.at[:, outer], gh.at[way]),
            (phase.at[:, inner], xh.at[way, 1, orders]),
            (solute.at[inner], xh.at[way, 1, ORDERS]),
        )[i]
        return remote(src, dst, x_send.at[way, i], x_recv.at[way, i], to, gz)

    def z_copy(group, way):
        planes = pl.ds(2 + group * GROUP, GROUP)
        if way == 0:
            src, dst, to = pl.ds(BASE0 + CZ - 1, 1), pl.ds(BASE0 - 1, 1), gz + 1
        else:
            deep = 2 if group in (0, GROUPS - 1) else 1
            src, dst, to = pl.ds(BASE0, deep), pl.ds(BASE0 + CZ, deep), gz - 1
        return remote(
            s0.at[:, planes, :, src, :], s0.at[:, planes, :, dst, :], z_send.at[way, group], z_recv.at[way, group], gx, to
        )

    def m_copy(x):
        return remote(
            s1.at[:, x + 1, :, pl.ds(0, 2), :],
            s1.at[:, x + 1, :, pl.ds(CZ, 2), :],
            m_send.at[x],
            m_recv.at[x],
            gx,
            gz - 1,
        )

    def c_copy(part):
        planes = (pl.ds(1, 1), pl.ds(CX, 1), pl.ds(2, CX - 2))[part]
        return remote(
            cs.at[:, :, planes, :, pl.ds(0, 1), :],
            cs.at[:, :, planes, :, pl.ds(CZ, 1), :],
            c_send.at[part],
            c_recv.at[part],
            gx,
            gz - 1,
        )

    def f_copy(what, way):
        to = right if way == 0 else left
        if what == 1:
            src, dst = (CX, 0) if way == 0 else (1, CX + 1)
            at = pl.ds(CZ, 1)
            pair = cs.at[:, :, src, :, at, :], cs.at[:, :, dst, :, at, :]
        else:
            src, dst = (CX, 0) if way == 0 else (2, CX + 2)
            at = pl.ds(BASE0 + CZ, 2) if what == 0 else pl.ds(BASE0 - 1, 1)
            pair = s0.at[:, pl.ds(src, 2), :, at, :], s0.at[:, pl.ds(dst, 2), :, at, :]
        return remote(*pair, f_send.at[what, way], f_recv.at[what, way], to, gz)

    def towards_left():
        pl.semaphore_wait(near_sem, 1)
        for i in range(5):
            x_copy(1, i).start()

    pl.semaphore_wait(barrier, 1 + has_up.astype(jnp.int32) + has_down.astype(jnp.int32))
    pl.semaphore_signal(near_sem, inc=1, device_id=(right, gz), device_id_type=MESH)
    for i in range(5):
        x_copy(0, i).start()

    @pl.when(gx > 0)
    def _():
        towards_left()

    @pl.when(jnp.logical_not(has_down))
    def _():
        def clear(x, carry):
            s0[:, x, :, pl.ds(BASE0 - 1, 1), :] = jnp.zeros((FIELDS, YT, 1, LANES), jnp.float32)
            return carry

        lax.fori_loop(0, CX + 4, clear, 0)

    @pl.when(jnp.logical_not(has_up))
    def _():
        def clear(x, carry):
            s0[:, x, :, pl.ds(BASE0 + CZ, 2), :] = jnp.zeros((FIELDS, YT, 2, LANES), jnp.float32)
            return carry

        lax.fori_loop(0, CX + 4, clear, 0)

        def clear_next(x, carry):
            s1[:, x, :, pl.ds(CZ, 2), :] = jnp.zeros((FIELDS, YT, 2, LANES), jnp.float32)
            cs[:, :, x, :, pl.ds(CZ, 1), :] = jnp.zeros((2, ORDERS, YT, 1, LANES), jnp.float32)
            return carry

        lax.fori_loop(0, CX + 2, clear_next, 0)

    for which in range(2):
        for k in range(YT):
            loads[k][which].wait()

    for group in (3, 0, 1, 2):

        @pl.when(has_up)
        def _(group=group):
            z_copy(group, 0).start()

        @pl.when(has_down)
        def _(group=group):
            z_copy(group, 1).start()

    for k in range(YT):
        loads[k][2].wait()

    def trig(x, carry):
        for k in range(ORDERS):
            for half in range(2):
                store_trig(cs, k, x + 1, pl.ds(8 * half, 8), slice(None), g[k, x, :, pl.ds(8 * half, 8), :])
        return carry

    lax.fori_loop(0, 2, lambda i, carry: trig((CX - 1) * i, carry), 0)

    @pl.when(has_down)
    def _():
        c_copy(0).start()
        c_copy(1).start()

    lax.fori_loop(1, CX - 1, trig, 0)

    @pl.when(has_down)
    def _():
        c_copy(2).start()

    frame_load.wait()
    for step in range(STEPS):
        for half in range(3):
            z = gz * CZ + 8 * half + step + lax.broadcasted_iota(jnp.int32, (1, 8, LANES), 1)
            height = (NZ // 2 - z - frames[step]).astype(jnp.float32)
            heat[step, half] = 2.4 * jnp.tanh(height * 0.125)

    def units_of(group, lower, upper):
        xa = jnp.where(group < 3, 4 + 4 * group, jnp.where(group == 3, 14, CX - 1))
        xb = jnp.where(group < 3, xa + 1, jnp.where(group == 3, 1, 0))
        xc = jnp.where(group < 2, xa + 2, jnp.where(group == 2, 2, xa))
        xd = jnp.where(group < 3, xc + 1, xb)
        return ((xa, lower), (xb, lower), (xc, upper), (xd, upper))

    def arrange(depth):
        def field(f, carry):
            for side in range(2):
                xi = 1 - depth if side == 0 else CX + 2 + depth
                for k in range(YT):
                    s0[f, xi, k, pl.ds(BASE0, CZ), :] = xh[side, depth, f, :, pl.ds(k * LANES, LANES)]
            return carry

        lax.fori_loop(0, FIELDS, field, 0)

    def both(action, which):
        for way in range(2):
            for i in which:
                copy = x_copy(way, i)
                copy.wait_send() if action == "send" else copy.wait_recv()

    def first_step(i, carry):
        group = jnp.where(i < 4, i, jnp.where(i == RIMS_AT, 4, jnp.where(i < RIMS_AT, i - 4, i - 5)))

        @pl.when(jnp.logical_and(has_down, i == 0))
        def _():
            z_copy(1, 0).wait_recv()

        @pl.when(jnp.logical_and(has_down, i == 1))
        def _():
            z_copy(2, 0).wait_recv()

        @pl.when(jnp.logical_and(has_down, i == 2))
        def _():
            z_copy(0, 0).wait_recv()
            z_copy(3, 0).wait_recv()

        @pl.when(i == 3)
        def _():
            @pl.when(has_up)
            def _():
                for every in (3, 0, 1, 2):
                    z_copy(every, 1).wait_recv()

            @pl.when(gx == 0)
            def _():
                towards_left()

            for way in range(2):

                @pl.when(has_up)
                def _(way=way):
                    f_copy(0, way).start()
                    c_copy(1 - way).wait_recv()
                    f_copy(1, way).start()

                @pl.when(has_down)
                def _(way=way):
                    f_copy(2, way).start()

        @pl.when(i == RIMS_AT)
        def _():
            both("recv", (0, 1))
            arrange(0)

        whole = jnp.logical_or(i == 3, i == RIMS_AT)
        units = units_of(group, jnp.where(jnp.logical_or(i < 4, whole), 0, 1), jnp.where(i < 3, 0, 1))
        first_units(s0, s1, cs, heat, units)

        @pl.when(jnp.logical_and(has_down, jnp.logical_or(i < 4, whole)))
        def _():
            m_copy(units[0][0]).start()
            m_copy(units[1][0]).start()

            @pl.when(i < 3)
            def _():
                m_copy(units[2][0]).start()
                m_copy(units[3][0]).start()

        return carry

    lax.fori_loop(0, 8, first_step, 0)

    def second_step(i, carry):
        @pl.when(jnp.logical_and(has_up, i == 3))
        def _():
            c_copy(2).wait_recv()
            for x in range(3, 9):
                m_copy(x).wait_recv()

        @pl.when(jnp.logical_and(has_up, i == 4))
        def _():
            for x in range(9, 13):
                m_copy(x).wait_recv()

        @pl.when(jnp.logical_and(has_up, i == 5))
        def _():
            for x in (13, 14, 1, 2):
                m_copy(x).wait_recv()

        @pl.when(jnp.logical_and(has_up, i == 6))
        def _():
            m_copy(CX - 1).wait_recv()
            m_copy(0).wait_recv()

        group = jnp.where(i < 3, i, i - 3)
        lower = jnp.where(jnp.logical_and(i >= 3, i < 6), 1, 0)
        second_units(o, s1, cs, heat, units_of(group, lower, jnp.where(i < 3, 0, 1)), 0)
        return carry

    lax.fori_loop(0, 7, second_step, 0)
    clear_top(o, has_up)

    both("recv", (2,))

    def outer_trig(k, carry):
        for side in range(2):
            for half in range(2):
                for j in range(YT):
                    part = gh[side, k, pl.ds(8 * half, 8), pl.ds(j * LANES, LANES)]
                    store_trig(cs, k, (CX + 1) * side, pl.ds(8 * half, 8), j, part)
        return carry

    lax.fori_loop(0, ORDERS, outer_trig, 0)
    both("recv", (3, 4))
    arrange(1)

    @pl.when(has_up)
    def _():
        for way in range(2):
            f_copy(0, way).wait_recv()
            f_copy(1, way).wait_recv()

    @pl.when(has_down)
    def _():
        for way in range(2):
            f_copy(2, way).wait_recv()

    def outer_step(t, carry):
        first_units(s0, s1, cs, heat, ((-1, t), (CX, t)))
        return carry

    lax.fori_loop(0, 3, outer_step, 0)

    both("send", range(5))

    @pl.when(has_up)
    def _():
        for group in range(GROUPS):
            z_copy(group, 0).wait_send()
        for way in range(2):
            f_copy(0, way).wait_send()
            f_copy(1, way).wait_send()

    @pl.when(has_down)
    def _():
        for group in range(GROUPS):
            z_copy(group, 1).wait_send()
        for x in range(CX):
            m_copy(x).wait_send()
        for part in range(3):
            c_copy(part).wait_send()
        for way in range(2):
            f_copy(2, way).wait_send()


def finish(o, s1, cs, heat, phase_out, solute_out, rims, sem):
    inner = pl.ds(1, CX - 2)
    copies = [
        pltpu.make_async_copy(o.at[pl.ds(0, ORDERS), inner], phase_out.at[:, inner], sem.at[0]),
        pltpu.make_async_copy(o.at[ORDERS, inner], solute_out.at[inner], sem.at[1]),
    ]
    for copy in copies:
        copy.start()
    for i, x in enumerate((0, CX - 1)):
        second_units(rims.at[:, pl.ds(i, 1)], s1, cs, heat, ((x, 0), (x, 1)), x)
    clear_top(rims, lax.axis_index("gz") < lax.axis_size("gz") - 1)
    for i, x in enumerate((0, CX - 1)):
        ends = [
            pltpu.make_async_copy(rims.at[pl.ds(0, ORDERS), i], phase_out.at[:, x], sem.at[2 + 2 * i]),
            pltpu.make_async_copy(rims.at[ORDERS, i], solute_out.at[x], sem.at[3 + 2 * i]),
        ]
        for copy in ends:
            copy.start()
        copies += ends
    for copy in copies:
        copy.wait()


def local(phase, solute, grain_map, frame_steps):
    hbm, vmem = pl.BlockSpec(memory_space=pltpu.HBM), pl.BlockSpec(memory_space=pltpu.VMEM)
    dma = pltpu.SemaphoreType.DMA
    args = [pltpu.with_memory_space_constraint(a, pltpu.HBM) for a in (frame_steps, phase, solute, grain_map)]
    results = pl.pallas_call(
        kernel,
        out_shape=(
            pltpu.VMEM((FIELDS, CX, CZ, NY), jnp.float32),
            pltpu.VMEM((FIELDS, CX + 2, YT, 24, LANES), jnp.float32),
            pltpu.VMEM((2, ORDERS, CX + 2, YT, 24, LANES), jnp.float32),
            pltpu.VMEM((STEPS, 3, 1, 8, LANES), jnp.float32),
        ),
        in_specs=[hbm] * 4,
        out_specs=(vmem,) * 4,
        scratch_shapes=[
            pltpu.VMEM((FIELDS, CX + 4, YT, 40, LANES), jnp.float32),
            pltpu.VMEM((ORDERS, CX, YT, CZ, LANES), jnp.int32),
            pltpu.VMEM((2, 2, FIELDS, CZ, NY), jnp.float32),
            pltpu.VMEM((2, ORDERS, CZ, NY), jnp.int32),
            pltpu.SMEM((STEPS,), jnp.int32),
            dma((3, YT)),
            dma,
            pltpu.SemaphoreType.REGULAR,
            dma((2, 5)),
            dma((2, 5)),
            dma((2, GROUPS)),
            dma((2, GROUPS)),
            dma((CX,)),
            dma((CX,)),
            dma((3,)),
            dma((3,)),
            dma((3, 2)),
            dma((3, 2)),
        ],
        compiler_params=pltpu.CompilerParams(
            collective_id=0, has_side_effects=True, vmem_limit_bytes=32 * 1024 * 1024
        ),
        name="grow",
    )(*args)
    return pl.pallas_call(
        finish,
        out_shape=(
            pltpu.HBM(phase.shape, jnp.float32),
            pltpu.HBM(solute.shape, jnp.float32),
        ),
        in_specs=[vmem] * 4,
        out_specs=(hbm, hbm),
        scratch_shapes=[pltpu.VMEM((FIELDS, 2, CZ, NY), jnp.float32), dma((6,))],
        compiler_params=pltpu.CompilerParams(vmem_limit_bytes=16 * 1024 * 1024),
        name="finish",
    )(*results)


def solution(mesh):
    in_specs = (P(None, "gx", "gz", None), P("gx", "gz", None), P(None, "gx", "gz", None), P())
    out_specs = (P(None, "gx", "gz", None), P("gx", "gz", None))
    return jax.shard_map(local, mesh=mesh, in_specs=in_specs, out_specs=out_specs, check_vma=False)
```

```python
import math

import jax
import jax.numpy as jnp
import numpy as np
from jax import lax
from jax.experimental import pallas as pl
from jax.experimental.pallas import tpu as pltpu
from jax.sharding import PartitionSpec as P

ORDERS = 4
FIELDS = 5
STEPS = 2
NGRAIN = 1024
NZ = 256
CX = 16
CZ = 16
NY = 512
LANES = 128
YT = NY // LANES
GROUP = 4
GROUPS = CX // GROUP
MESH = pl.DeviceIdType.MESH

BASE0 = 8

ABOVE = BASE0 + CZ + 2

RIMS_AT = 0


def sine_coefficients():
    nodes = np.cos(np.pi * (np.arange(400) + 0.5) / 400)
    theta = nodes * np.pi / 2
    even = np.polynomial.chebyshev.Chebyshev.fit(nodes, np.cos(theta), 8, domain=[-1, 1])
    odd = np.polynomial.chebyshev.Chebyshev.fit(nodes, np.sin(theta), 9, domain=[-1, 1])
    even = even.convert(kind=np.polynomial.Polynomial).coef
    odd = odd.convert(kind=np.polynomial.Polynomial).coef
    cos_c = [float(even[i] * math.sqrt(0.5) / 128.0**i) for i in (0, 2, 4, 6, 8)]
    sin_c = [float(odd[i] * math.sqrt(2.0) / 128.0**i) for i in (1, 3, 5, 7, 9)]
    return sin_c, cos_c


SIN_C, COS_C = sine_coefficients()


def horner(x, coefficients):
    value = coefficients[-1]
    for c in coefficients[-2::-1]:
        value = value * x + c
    return value


def next_y(rolled, offset):
    if offset > 0:
        return jnp.concatenate([rolled[1:], rolled[:1]], axis=0)
    return jnp.concatenate([rolled[-1:], rolled[:-1]], axis=0)


def neighbours(load, f, part):
    ys = slice(None) if part is None else pl.ds(2 * part, 2)
    c = load(f, 0, 0, ys)
    xl, xh = load(f, -1, 0, ys), load(f, 1, 0, ys)
    zl, zh = load(f, 0, -1, ys), load(f, 0, 1, ys)
    lane = lax.broadcasted_iota(jnp.int32, c.shape, 2)
    right = pltpu.roll(c, 1, axis=2)
    left = pltpu.roll(c, LANES - 1, axis=2)
    if part is None:
        before, after = next_y(right, -1), next_y(left, 1)
    else:
        before = load(f, 0, 0, pl.ds(lax.rem(2 * part + YT - 1, YT), 1))
        after = load(f, 0, 0, pl.ds(lax.rem(2 * part + 2, YT), 1))
        before = jnp.concatenate([pltpu.roll(before, 1, axis=2), right[:1]], axis=0)
        after = jnp.concatenate([left[1:], pltpu.roll(after, LANES - 1, axis=2)], axis=0)
    yl = jnp.where(lane == 0, before, right)
    yh = jnp.where(lane == LANES - 1, after, left)
    return c, xl, xh, yl, yh, zl, zh


def advance(load, table, thermal, put, part=None):
    ys = slice(None) if part is None else pl.ds(2 * part, 2)
    drive = thermal - 2.4 * load(ORDERS, 0, 0, ys)
    q = None
    for k in range(ORDERS):
        p = load(k, 0, 0, ys)
        q = p * p if q is None else q + p * p
    well = 0.64 - 0.16 * q
    total = None
    for k in range(ORDERS):
        p, xl, xh, yl, yh, zl, zh = neighbours(load, k, part)
        gx, gy, gz = xh - xl, yh - yl, zh - zl
        lap = (xl + xh) + (yl + yh) + (zl + zh) - 6.0 * p
        x2, y2, z2 = gx * gx, gy * gy, gz * gz
        r = x2 + y2
        t = table(0, k, ys) * (gx * gy) + table(1, k, ys) * (x2 - y2)
        quartic = r * r + z2 * z2 - t * t
        d = (r + z2) + 0.2
        ratio = quartic * pl.reciprocal(d * d, approx=True)
        w = p - p * p
        delta = (
            lap * (0.08 + 0.04 * ratio)
            + p * (well + p * (1.44 * p - 1.92))
            + (w * w) * drive
        )
        put(k, p + delta)
        total = delta if total is None else total + delta
    c, xl, xh, yl, yh, zl, zh = neighbours(load, ORDERS, part)
    near = (xl + xh) + (yl + yh) + (zl + zh)
    put(ORDERS, 0.52 * c + 0.08 * near + 0.5 * total)


def advance_tile(s, cs, x, row, cs_row, thermal, put, part=None):
    def load(f, dx, dz, ys):
        return s[f, x + 1 + dx, ys, pl.ds(row + dz, 8), :]

    def table(i, k, ys):
        return cs[i, k, x, ys, pl.ds(cs_row, 8), :]

    advance(load, table, thermal, put, part)


def advance_row(s, s_new, cs, x, row, above, z, thermal):
    def load(f, dx, dz, ys):
        flat, rows = strided(s, f, x + 1 + dx, above if dz > 0 else row + dz)
        return jnp.stack([flat[r, :] for r in rows])

    def table(i, k, ys):
        flat, rows = strided(cs, i, k, x, z)
        return jnp.stack([flat[r, :] for r in rows])

    def put(f, value):
        flat, rows = strided(s_new, f, x + 1, z)
        for k in range(YT):
            flat[rows[k], :] = value[k]

    advance(load, table, thermal, put)


def sine_cosine(grain):
    h = ((grain & 255) - 128).astype(jnp.float32)
    h2 = h * h
    return h * horner(h2, SIN_C), horner(h2, COS_C)


def strided(ref, *at):
    *outer, plane, where = at
    planes, rows = ref.shape[-4], ref.shape[-2]
    first = 0
    for size, index in zip(ref.shape, outer):
        first = first * size + index
    first = (first * planes + plane) * YT * rows + where
    flat = ref.reshape(math.prod(ref.shape[:-1]), LANES)
    return flat, [pl.ds(first + k * rows, 8, stride=YT * rows) for k in range(YT)]


def tile(half):
    return pl.ds(8 * half if isinstance(half, int) else pl.multiple_of(8 * half, 8), 8)


def second_units(o, s1, cs, heat, units, first):
    for x, half in units:

        def put(f, value, x=x, half=half):
            for k in range(YT):
                o[f, x - first, tile(half), pl.ds(k * LANES, LANES)] = value[k]

        advance_tile(s1, cs, x, 1 + 8 * half, 1 + 8 * half, heat[1, half], put)


def clear_top(o, has_up):
    @pl.when(jnp.logical_not(has_up))
    def _():
        def clear(x, carry):
            o[:, x, pl.ds(CZ - 1, 1), :] = jnp.zeros((FIELDS, 1, NY), jnp.float32)
            return carry

        lax.fori_loop(0, o.shape[1], clear, 0)


def kernel(
    frames_in, phase, solute, grain, o, s1, cs, heat,
    s0, g, low, frames,
    load_sem, frame_sem, x_send, x_recv, z_send, z_recv, m_send, m_recv, c_send, c_recv, d_send, d_recv,
):
    gx, gz = lax.axis_index("gx"), lax.axis_index("gz")
    n_gx, n_gz = lax.axis_size("gx"), lax.axis_size("gz")
    right, left = lax.rem(gx + 1, n_gx), lax.rem(gx + n_gx - 1, n_gx)
    has_up, has_down = gz < n_gz - 1, gz > 0

    loads = []
    for k in range(YT):
        lanes = pl.ds(k * LANES, LANES)
        rows = pl.ds(BASE0, CZ)
        loads.append(
            (
                pltpu.make_async_copy(
                    phase.at[:, :, :, lanes], s0.at[pl.ds(0, ORDERS), pl.ds(1, CX), k, rows, :], load_sem.at[0, k]
                ),
                pltpu.make_async_copy(
                    solute.at[:, :, lanes], s0.at[ORDERS, pl.ds(1, CX), k, rows, :], load_sem.at[1, k]
                ),
                pltpu.make_async_copy(grain.at[:, :, :, lanes], g.at[:, :, k, :, :], load_sem.at[2, k]),
            )
        )
    frame_load = pltpu.make_async_copy(frames_in, frames, frame_sem)
    barrier = pltpu.get_barrier_semaphore()

    def greet(ix, iz):
        pl.semaphore_signal(barrier, inc=1, device_id=(ix, iz), device_id_type=MESH)

    greet(left, gz)
    greet(right, gz)

    @pl.when(has_up)
    def _():
        greet(gx, gz + 1)

    @pl.when(has_down)
    def _():
        greet(gx, gz - 1)

    for which in range(3):
        for k in range(YT):
            loads[k][which].start()

    frame_load.start()

    @pl.when(jnp.logical_not(has_down))
    def _():
        def clear(x, carry):
            s0[:, x, :, pl.ds(BASE0 - 1, 1), :] = jnp.zeros((FIELDS, YT, 1, LANES), jnp.float32)
            return carry

        lax.fori_loop(0, CX + 2, clear, 0)

    @pl.when(jnp.logical_not(has_up))
    def _():
        def clear(x, carry):
            s0[:, x, :, pl.ds(ABOVE, 1), :] = jnp.zeros((FIELDS, YT, 1, LANES), jnp.float32)
            s1[:, x, :, pl.ds(CZ, 2), :] = jnp.zeros((FIELDS, YT, 2, LANES), jnp.float32)
            return carry

        lax.fori_loop(0, CX + 2, clear, 0)

        def clear_cs(x, carry):
            cs[:, :, x, :, pl.ds(CZ, 1), :] = jnp.zeros((2, ORDERS, YT, 1, LANES), jnp.float32)
            return carry

        lax.fori_loop(0, CX, clear_cs, 0)

    def remote(src, dst, send, recv, ix, iz):
        return pltpu.make_async_remote_copy(
            src_ref=src, dst_ref=dst, send_sem=send, recv_sem=recv, device_id=(ix, iz), device_id_type=MESH
        )

    def x_copy(step, way, piece):
        s, base = (s0, BASE0) if step == 0 else (s1, 0)
        half, part = lax.div(piece, 2), lax.rem(piece, 2)
        ys, rows = pl.ds(2 * part, 2), pl.ds(base + 8 * half, 8)
        src, dst, to = (CX, 0, right) if way == 0 else (1, CX + 1, left)
        return remote(
            s.at[:, src, ys, rows, :],
            s.at[:, dst, ys, rows, :],
            x_send.at[step, way, piece],
            x_recv.at[step, way, piece],
            to,
            gz,
        )

    def z_copy(group, way):
        planes = pl.ds(1 + group * GROUP, GROUP)
        src, dst, to = (BASE0 + CZ - 1, BASE0 - 1, gz + 1) if way == 0 else (BASE0, ABOVE, gz - 1)
        return remote(
            s0.at[:, planes, :, pl.ds(src, 1), :],
            s0.at[:, planes, :, pl.ds(dst, 1), :],
            z_send.at[way, group],
            z_recv.at[way, group],
            gx,
            to,
        )

    def m_copy(x):
        return remote(
            s1.at[:, x + 1, :, pl.ds(0, 2), :],
            s1.at[:, x + 1, :, pl.ds(CZ, 2), :],
            m_send.at[x],
            m_recv.at[x],
            gx,
            gz - 1,
        )

    def d_copy(way):
        src, dst, to = (CX, 0, right) if way == 0 else (1, CX + 1, left)
        return remote(
            s1.at[:, src, :, pl.ds(0, 1), :],
            s1.at[:, dst, :, pl.ds(CZ, 1), :],
            d_send.at[way],
            d_recv.at[way],
            to,
            gz - 1,
        )

    def c_copy():
        return remote(grain.at[:, :, 0, :], low, c_send, c_recv, gx, gz - 1)

    for which in range(2):
        for k in range(YT):
            loads[k][which].wait()

    pl.semaphore_wait(barrier, 2 + has_up.astype(jnp.int32) + has_down.astype(jnp.int32))

    for piece in range(4):
        x_copy(0, 0, piece).start()
        x_copy(0, 1, piece).start()
    for group in (1, 2, 3, 0):

        @pl.when(has_up)
        def _(group=group):
            z_copy(group, 0).start()

        @pl.when(has_down)
        def _(group=group):
            z_copy(group, 1).start()

    @pl.when(has_down)
    def _():
        c_copy().start()

    for k in range(YT):
        loads[k][2].wait()

    def trig(x, carry):
        for k in range(ORDERS):
            for half in range(2):
                at = pl.ds(8 * half, 8)
                cs[0, k, x, :, at, :], cs[1, k, x, :, at, :] = sine_cosine(g[k, x, :, at, :])
        return carry

    lax.fori_loop(0, CX, trig, 0)

    frame_load.wait()
    for step in range(STEPS):
        for half in range(2):
            z = gz * CZ + 8 * half + step + lax.broadcasted_iota(jnp.int32, (1, 8, LANES), 1)
            height = (NZ // 2 - z - frames[step]).astype(jnp.float32)
            heat[step, half] = 2.4 * jnp.tanh(height * 0.125)

    def first_units(units):
        for x, half in units:

            def put(f, value, x=x, half=half):
                s1[f, x + 1, :, tile(half), :] = value

            advance_tile(s0, cs, x, BASE0 + 8 * half, 8 * half, heat[0, half], put)

    def units_of(group, lower, upper):
        xa = jnp.where(group < 3, 4 + 4 * group, 14)
        xb = jnp.where(group < 3, xa + 1, 1)
        xc = jnp.where(group < 2, xa + 2, jnp.where(group == 2, 2, 14))
        xd = jnp.where(group < 3, xc + 1, 1)
        return ((xa, lower), (xb, lower), (xc, upper), (xd, upper))

    def first_rims(piece, carry):
        half, part = lax.div(piece, 2), lax.rem(piece, 2)
        @pl.when(piece == 2)
        def _():
            @pl.when(has_up)
            def _():
                z_copy(0, 1).wait_recv()
                z_copy(3, 1).wait_recv()

            for xi in (1, CX):
                s0[:, xi, :, pl.ds(BASE0 + CZ, 1), :] = s0[:, xi, :, pl.ds(ABOVE, 1), :]

        x_copy(0, 0, piece).wait_recv()
        x_copy(0, 1, piece).wait_recv()
        for x in (CX - 1, 0):

            def put(f, value, x=x):
                s1[f, x + 1, pl.ds(2 * part, 2), tile(half), :] = value

            advance_tile(s0, cs, x, BASE0 + 8 * half, 8 * half, heat[0, half], put, part)
        x_copy(1, 0, piece).start()
        x_copy(1, 1, piece).start()

        @pl.when(jnp.logical_and(piece == 1, has_down))
        def _():
            for way, x in ((0, CX - 1), (1, 0)):
                m_copy(x).start()
                d_copy(way).start()

        return carry

    def first_step(i, carry):
        group = jnp.where(i < 4, i, i - 4)

        @pl.when(jnp.logical_and(has_down, i < 3))
        def _():
            z_copy(i + 1, 0).wait_recv()

        @pl.when(jnp.logical_and(has_down, i == 2))
        def _():
            z_copy(0, 0).wait_recv()

        units = units_of(group, lax.div(i, 4), jnp.where(i < 3, 0, 1))
        first_units(units)

        @pl.when(jnp.logical_and(has_down, i < 4))
        def _():
            m_copy(units[0][0]).start()
            m_copy(units[1][0]).start()

            @pl.when(i < 3)
            def _():
                m_copy(units[2][0]).start()
                m_copy(units[3][0]).start()

        return carry

    lax.fori_loop(0, 7, first_step, 0)

    def second_step(i, carry):
        @pl.when(i == RIMS_AT)
        def _():
            lax.fori_loop(0, 4, first_rims, 0)

        @pl.when(i == 3)
        def _():
            @pl.when(has_up)
            def _():
                z_copy(1, 1).wait_recv()
                z_copy(2, 1).wait_recv()

            def top(j, carry):
                row = jnp.broadcast_to(heat[0, 1, :, pl.ds(7, 1), :], (1, 8, LANES))
                advance_row(s0, s1, cs, 1 + 6 * j, BASE0 + CZ - 1, ABOVE, CZ - 1, row)
                return carry

            lax.fori_loop(0, 2, top, 0)

        @pl.when(jnp.logical_and(has_up, i == 3))
        def _():
            c_copy().wait_recv()

            def above_trig(k, carry):
                for x in (0, 8):
                    for i in range(2):
                        flat, rows = strided(cs, i, k, x, CZ)
                        for j in range(YT):
                            part = low[k, pl.ds(x, 8), pl.ds(j * LANES, LANES)]
                            flat[rows[j], :] = sine_cosine(part)[i]
                return carry

            lax.fori_loop(0, ORDERS, above_trig, 0)
            for x in range(3, 9):
                m_copy(x).wait_recv()

        @pl.when(jnp.logical_and(has_up, i == 4))
        def _():
            for x in range(9, 13):
                m_copy(x).wait_recv()

        @pl.when(jnp.logical_and(has_up, i == 5))
        def _():
            for x in (13, 14, 1, 2):
                m_copy(x).wait_recv()

        @pl.when(jnp.logical_and(has_up, i == 6))
        def _():
            m_copy(CX - 1).wait_recv()
            m_copy(0).wait_recv()

        group = jnp.where(i < 3, i, i - 3)
        second_units(o, s1, cs, heat, units_of(group, jnp.where(jnp.logical_and(i >= 3, i < 6), 1, 0), jnp.where(i < 3, 0, 1)), 0)
        return carry

    lax.fori_loop(0, 7, second_step, 0)
    clear_top(o, has_up)

    for way in range(2):
        for piece in range(4):
            x_copy(0, way, piece).wait_send()

    @pl.when(has_up)
    def _():
        for group in range(GROUPS):
            z_copy(group, 0).wait_send()

    @pl.when(has_down)
    def _():
        for group in range(GROUPS):
            z_copy(group, 1).wait_send()
        for x in range(CX):
            m_copy(x).wait_send()
        c_copy().wait_send()
        d_copy(0).wait_send()
        d_copy(1).wait_send()

    @pl.when(has_up)
    def _():
        d_copy(0).wait_recv()
        d_copy(1).wait_recv()

    for way in range(2):
        for piece in range(4):
            x_copy(1, way, piece).wait()


def finish(o, s1, cs, heat, phase_out, solute_out, rims, sem):
    inner = pl.ds(1, CX - 2)
    copies = [
        pltpu.make_async_copy(o.at[pl.ds(0, ORDERS), inner], phase_out.at[:, inner], sem.at[0]),
        pltpu.make_async_copy(o.at[ORDERS, inner], solute_out.at[inner], sem.at[1]),
    ]
    for copy in copies:
        copy.start()
    for i, x in enumerate((0, CX - 1)):
        second_units(rims.at[:, pl.ds(i, 1)], s1, cs, heat, ((x, 0), (x, 1)), x)
    clear_top(rims, lax.axis_index("gz") < lax.axis_size("gz") - 1)
    for i, x in enumerate((0, CX - 1)):
        ends = [
            pltpu.make_async_copy(rims.at[pl.ds(0, ORDERS), i], phase_out.at[:, x], sem.at[2 + 2 * i]),
            pltpu.make_async_copy(rims.at[ORDERS, i], solute_out.at[x], sem.at[3 + 2 * i]),
        ]
        for copy in ends:
            copy.start()
        copies += ends
    for copy in copies:
        copy.wait()


def local(phase, solute, grain_map, frame_steps):
    hbm, vmem = pl.BlockSpec(memory_space=pltpu.HBM), pl.BlockSpec(memory_space=pltpu.VMEM)
    dma = pltpu.SemaphoreType.DMA
    args = [pltpu.with_memory_space_constraint(a, pltpu.HBM) for a in (frame_steps, phase, solute, grain_map)]
    results = pl.pallas_call(
        kernel,
        out_shape=(
            pltpu.VMEM((FIELDS, CX, CZ, NY), jnp.float32),
            pltpu.VMEM((FIELDS, CX + 2, YT, 24, LANES), jnp.float32),
            pltpu.VMEM((2, ORDERS, CX, YT, 24, LANES), jnp.float32),
            pltpu.VMEM((STEPS, 2, 1, 8, LANES), jnp.float32),
        ),
        in_specs=[hbm] * 4,
        out_specs=(vmem,) * 4,
        scratch_shapes=[
            pltpu.VMEM((FIELDS, CX + 2, YT, 32, LANES), jnp.float32),
            pltpu.VMEM((ORDERS, CX, YT, CZ, LANES), jnp.int32),
            pltpu.VMEM((ORDERS, CX, NY), jnp.int32),
            pltpu.SMEM((STEPS,), jnp.int32),
            dma((3, YT)),
            dma,
            dma((STEPS, 2, 4)),
            dma((STEPS, 2, 4)),
            dma((2, GROUPS)),
            dma((2, GROUPS)),
            dma((CX,)),
            dma((CX,)),
            dma,
            dma,
            dma((2,)),
            dma((2,)),
        ],
        compiler_params=pltpu.CompilerParams(
            collective_id=0, has_side_effects=True, vmem_limit_bytes=32 * 1024 * 1024
        ),
        name="grow",
    )(*args)
    return pl.pallas_call(
        finish,
        out_shape=(
            pltpu.HBM(phase.shape, jnp.float32),
            pltpu.HBM(solute.shape, jnp.float32),
        ),
        in_specs=[vmem] * 4,
        out_specs=(hbm, hbm),
        scratch_shapes=[pltpu.VMEM((FIELDS, 2, CZ, NY), jnp.float32), dma((6,))],
        compiler_params=pltpu.CompilerParams(vmem_limit_bytes=16 * 1024 * 1024),
        name="finish",
    )(*results)


def solution(mesh):
    in_specs = (P(None, "gx", "gz", None), P("gx", "gz", None), P(None, "gx", "gz", None), P())
    out_specs = (P(None, "gx", "gz", None), P("gx", "gz", None))
    return jax.shard_map(local, mesh=mesh, in_specs=in_specs, out_specs=out_specs, check_vma=False)
```

```python
import math

import jax
import jax.numpy as jnp
import numpy as np
from jax import lax
from jax.experimental import pallas as pl
from jax.experimental.pallas import tpu as pltpu
from jax.sharding import PartitionSpec as P

ORDERS = 4
FIELDS = 5
STEPS = 2
NGRAIN = 1024
NZ = 256
CX = 16
CZ = 16
NY = 512
LANES = 128
YT = NY // LANES
GROUP = 4
GROUPS = CX // GROUP
MESH = pl.DeviceIdType.MESH

BASE0 = 8

ABOVE = BASE0 + CZ + 2

RIMS_AT = 0


def sine_coefficients():
    nodes = np.cos(np.pi * (np.arange(400) + 0.5) / 400)
    theta = nodes * np.pi / 2
    even = np.polynomial.chebyshev.Chebyshev.fit(nodes, np.cos(theta), 8, domain=[-1, 1])
    odd = np.polynomial.chebyshev.Chebyshev.fit(nodes, np.sin(theta), 9, domain=[-1, 1])
    even = even.convert(kind=np.polynomial.Polynomial).coef
    odd = odd.convert(kind=np.polynomial.Polynomial).coef
    cos_c = [float(even[i] * math.sqrt(0.5) / 128.0**i) for i in (0, 2, 4, 6, 8)]
    sin_c = [float(odd[i] * math.sqrt(2.0) / 128.0**i) for i in (1, 3, 5, 7, 9)]
    return sin_c, cos_c


SIN_C, COS_C = sine_coefficients()


def horner(x, coefficients):
    value = coefficients[-1]
    for c in coefficients[-2::-1]:
        value = value * x + c
    return value


def next_y(rolled, offset):
    if offset > 0:
        return jnp.concatenate([rolled[1:], rolled[:1]], axis=0)
    return jnp.concatenate([rolled[-1:], rolled[:-1]], axis=0)


def neighbours(load, f, part):
    ys = slice(None) if part is None else pl.ds(2 * part, 2)
    c = load(f, 0, 0, ys)
    xl, xh = load(f, -1, 0, ys), load(f, 1, 0, ys)
    zl, zh = load(f, 0, -1, ys), load(f, 0, 1, ys)
    lane = lax.broadcasted_iota(jnp.int32, c.shape, 2)
    right = pltpu.roll(c, 1, axis=2)
    left = pltpu.roll(c, LANES - 1, axis=2)
    if part is None:
        before, after = next_y(right, -1), next_y(left, 1)
    else:
        before = load(f, 0, 0, pl.ds(lax.rem(2 * part + YT - 1, YT), 1))
        after = load(f, 0, 0, pl.ds(lax.rem(2 * part + 2, YT), 1))
        before = jnp.concatenate([pltpu.roll(before, 1, axis=2), right[:1]], axis=0)
        after = jnp.concatenate([left[1:], pltpu.roll(after, LANES - 1, axis=2)], axis=0)
    yl = jnp.where(lane == 0, before, right)
    yh = jnp.where(lane == LANES - 1, after, left)
    return c, xl, xh, yl, yh, zl, zh


def advance(load, table, thermal, put, part=None):
    ys = slice(None) if part is None else pl.ds(2 * part, 2)
    drive = thermal - 2.4 * load(ORDERS, 0, 0, ys)
    q = None
    for k in range(ORDERS):
        p = load(k, 0, 0, ys)
        q = p * p if q is None else q + p * p
    well = 0.64 - 0.16 * q
    total = None
    for k in range(ORDERS):
        p, xl, xh, yl, yh, zl, zh = neighbours(load, k, part)
        gx, gy, gz = xh - xl, yh - yl, zh - zl
        lap = (xl + xh) + (yl + yh) + (zl + zh) - 6.0 * p
        x2, y2, z2 = gx * gx, gy * gy, gz * gz
        r = x2 + y2
        t = table(0, k, ys) * (gx * gy) + table(1, k, ys) * (x2 - y2)
        quartic = r * r + z2 * z2 - t * t
        d = (r + z2) + 0.2
        ratio = quartic * pl.reciprocal(d * d, approx=True)
        w = p - p * p
        delta = (
            lap * (0.08 + 0.04 * ratio)
            + p * (well + p * (1.44 * p - 1.92))
            + (w * w) * drive
        )
        put(k, p + delta)
        total = delta if total is None else total + delta
    c, xl, xh, yl, yh, zl, zh = neighbours(load, ORDERS, part)
    near = (xl + xh) + (yl + yh) + (zl + zh)
    put(ORDERS, 0.52 * c + 0.08 * near + 0.5 * total)


def advance_tile(s, cs, x, row, cs_row, thermal, put, part=None):
    def load(f, dx, dz, ys):
        return s[f, x + 1 + dx, ys, pl.ds(row + dz, 8), :]

    def table(i, k, ys):
        return cs[i, k, x, ys, pl.ds(cs_row, 8), :]

    advance(load, table, thermal, put, part)


def advance_row(s, s_new, cs, x, row, above, z, thermal):
    def load(f, dx, dz, ys):
        flat, rows = strided(s, f, x + 1 + dx, above if dz > 0 else row + dz)
        return jnp.stack([flat[r, :] for r in rows])

    def table(i, k, ys):
        flat, rows = strided(cs, i, k, x, z)
        return jnp.stack([flat[r, :] for r in rows])

    def put(f, value):
        flat, rows = strided(s_new, f, x + 1, z)
        for k in range(YT):
            flat[rows[k], :] = value[k]

    advance(load, table, thermal, put)


def sine_cosine(grain):
    h = ((grain & 255) - 128).astype(jnp.float32)
    h2 = h * h
    return h * horner(h2, SIN_C), horner(h2, COS_C)


def strided(ref, *at):
    *outer, plane, where = at
    planes, rows = ref.shape[-4], ref.shape[-2]
    first = 0
    for size, index in zip(ref.shape, outer):
        first = first * size + index
    first = (first * planes + plane) * YT * rows + where
    flat = ref.reshape(math.prod(ref.shape[:-1]), LANES)
    return flat, [pl.ds(first + k * rows, 8, stride=YT * rows) for k in range(YT)]


def tile(half):
    return pl.ds(8 * half if isinstance(half, int) else pl.multiple_of(8 * half, 8), 8)


def second_units(o, s1, cs, heat, units, first):
    for x, half in units:

        def put(f, value, x=x, half=half):
            for k in range(YT):
                o[f, x - first, tile(half), pl.ds(k * LANES, LANES)] = value[k]

        advance_tile(s1, cs, x, 1 + 8 * half, 1 + 8 * half, heat[1, half], put)


def clear_top(o, has_up):
    @pl.when(jnp.logical_not(has_up))
    def _():
        def clear(x, carry):
            o[:, x, pl.ds(CZ - 1, 1), :] = jnp.zeros((FIELDS, 1, NY), jnp.float32)
            return carry

        lax.fori_loop(0, o.shape[1], clear, 0)


def kernel(
    frames_in, phase, solute, grain, o, s1, cs, heat,
    s0, g, low, frames,
    load_sem, frame_sem, x_send, x_recv, z_send, z_recv, m_send, m_recv, c_send, c_recv, d_send, d_recv,
):
    gx, gz = lax.axis_index("gx"), lax.axis_index("gz")
    n_gx, n_gz = lax.axis_size("gx"), lax.axis_size("gz")
    right, left = lax.rem(gx + 1, n_gx), lax.rem(gx + n_gx - 1, n_gx)
    has_up, has_down = gz < n_gz - 1, gz > 0

    loads = []
    for k in range(YT):
        lanes = pl.ds(k * LANES, LANES)
        rows = pl.ds(BASE0, CZ)
        loads.append(
            (
                pltpu.make_async_copy(
                    phase.at[:, :, :, lanes], s0.at[pl.ds(0, ORDERS), pl.ds(1, CX), k, rows, :], load_sem.at[0, k]
                ),
                pltpu.make_async_copy(
                    solute.at[:, :, lanes], s0.at[ORDERS, pl.ds(1, CX), k, rows, :], load_sem.at[1, k]
                ),
                pltpu.make_async_copy(grain.at[:, :, :, lanes], g.at[:, :, k, :, :], load_sem.at[2, k]),
            )
        )
    frame_load = pltpu.make_async_copy(frames_in, frames, frame_sem)
    barrier = pltpu.get_barrier_semaphore()

    def greet(ix, iz):
        pl.semaphore_signal(barrier, inc=1, device_id=(ix, iz), device_id_type=MESH)

    greet(left, gz)
    greet(right, gz)

    @pl.when(has_up)
    def _():
        greet(gx, gz + 1)

    @pl.when(has_down)
    def _():
        greet(gx, gz - 1)

    for which in range(3):
        for k in range(YT):
            loads[k][which].start()

    frame_load.start()

    @pl.when(jnp.logical_not(has_down))
    def _():
        def clear(x, carry):
            s0[:, x, :, pl.ds(BASE0 - 1, 1), :] = jnp.zeros((FIELDS, YT, 1, LANES), jnp.float32)
            return carry

        lax.fori_loop(0, CX + 2, clear, 0)

    @pl.when(jnp.logical_not(has_up))
    def _():
        def clear(x, carry):
            s0[:, x, :, pl.ds(ABOVE, 1), :] = jnp.zeros((FIELDS, YT, 1, LANES), jnp.float32)
            s1[:, x, :, pl.ds(CZ, 2), :] = jnp.zeros((FIELDS, YT, 2, LANES), jnp.float32)
            return carry

        lax.fori_loop(0, CX + 2, clear, 0)

        def clear_cs(x, carry):
            cs[:, :, x, :, pl.ds(CZ, 1), :] = jnp.zeros((2, ORDERS, YT, 1, LANES), jnp.float32)
            return carry

        lax.fori_loop(0, CX, clear_cs, 0)

    def remote(src, dst, send, recv, ix, iz):
        return pltpu.make_async_remote_copy(
            src_ref=src, dst_ref=dst, send_sem=send, recv_sem=recv, device_id=(ix, iz), device_id_type=MESH
        )

    def x_copy(step, way, piece):
        s, base = (s0, BASE0) if step == 0 else (s1, 0)
        half, part = lax.div(piece, 2), lax.rem(piece, 2)
        ys, rows = pl.ds(2 * part, 2), pl.ds(base + 8 * half, 8)
        src, dst, to = (CX, 0, right) if way == 0 else (1, CX + 1, left)
        return remote(
            s.at[:, src, ys, rows, :],
            s.at[:, dst, ys, rows, :],
            x_send.at[step, way, piece],
            x_recv.at[step, way, piece],
            to,
            gz,
        )

    def z_copy(group, way):
        planes = pl.ds(1 + group * GROUP, GROUP)
        src, dst, to = (BASE0 + CZ - 1, BASE0 - 1, gz + 1) if way == 0 else (BASE0, ABOVE, gz - 1)
        return remote(
            s0.at[:, planes, :, pl.ds(src, 1), :],
            s0.at[:, planes, :, pl.ds(dst, 1), :],
            z_send.at[way, group],
            z_recv.at[way, group],
            gx,
            to,
        )

    def m_copy(x):
        return remote(
            s1.at[:, x + 1, :, pl.ds(0, 2), :],
            s1.at[:, x + 1, :, pl.ds(CZ, 2), :],
            m_send.at[x],
            m_recv.at[x],
            gx,
            gz - 1,
        )

    def d_copy(way):
        src, dst, to = (CX, 0, right) if way == 0 else (1, CX + 1, left)
        return remote(
            s1.at[:, src, :, pl.ds(0, 1), :],
            s1.at[:, dst, :, pl.ds(CZ, 1), :],
            d_send.at[way],
            d_recv.at[way],
            to,
            gz - 1,
        )

    def c_copy():
        return remote(grain.at[:, :, 0, :], low, c_send, c_recv, gx, gz - 1)

    for which in range(2):
        for k in range(YT):
            loads[k][which].wait()

    pl.semaphore_wait(barrier, 2 + has_up.astype(jnp.int32) + has_down.astype(jnp.int32))

    for piece in range(4):
        x_copy(0, 0, piece).start()
        x_copy(0, 1, piece).start()
    @pl.when(has_down)
    def _():
        for group in (3, 0, 1, 2):
            z_copy(group, 1).start()

    @pl.when(has_up)
    def _():
        for group in (1, 2, 3, 0):
            z_copy(group, 0).start()

    @pl.when(has_down)
    def _():
        c_copy().start()

    for k in range(YT):
        loads[k][2].wait()

    def trig(x, carry):
        for k in range(ORDERS):
            for half in range(2):
                at = pl.ds(8 * half, 8)
                cs[0, k, x, :, at, :], cs[1, k, x, :, at, :] = sine_cosine(g[k, x, :, at, :])
        return carry

    lax.fori_loop(0, CX, trig, 0)

    frame_load.wait()
    for step in range(STEPS):
        for half in range(2):
            z = gz * CZ + 8 * half + step + lax.broadcasted_iota(jnp.int32, (1, 8, LANES), 1)
            height = (NZ // 2 - z - frames[step]).astype(jnp.float32)
            heat[step, half] = 2.4 * jnp.tanh(height * 0.125)

    def first_units(units):
        for x, half in units:

            def put(f, value, x=x, half=half):
                s1[f, x + 1, :, tile(half), :] = value

            advance_tile(s0, cs, x, BASE0 + 8 * half, 8 * half, heat[0, half], put)

    def units_of(group, lower, upper):
        xa = jnp.where(group < 3, 4 + 4 * group, 14)
        xb = jnp.where(group < 3, xa + 1, 1)
        xc = jnp.where(group < 2, xa + 2, jnp.where(group == 2, 2, 14))
        xd = jnp.where(group < 3, xc + 1, 1)
        return ((xa, lower), (xb, lower), (xc, upper), (xd, upper))

    def first_rims(piece, carry):
        half, part = lax.div(piece, 2), lax.rem(piece, 2)
        @pl.when(piece == 2)
        def _():
            @pl.when(has_up)
            def _():
                z_copy(0, 1).wait_recv()
                z_copy(3, 1).wait_recv()

            for xi in (1, CX):
                s0[:, xi, :, pl.ds(BASE0 + CZ, 1), :] = s0[:, xi, :, pl.ds(ABOVE, 1), :]

        x_copy(0, 0, piece).wait_recv()
        x_copy(0, 1, piece).wait_recv()
        for x in (CX - 1, 0):

            def put(f, value, x=x):
                s1[f, x + 1, pl.ds(2 * part, 2), tile(half), :] = value

            advance_tile(s0, cs, x, BASE0 + 8 * half, 8 * half, heat[0, half], put, part)
        x_copy(1, 0, piece).start()
        x_copy(1, 1, piece).start()

        @pl.when(jnp.logical_and(piece == 1, has_down))
        def _():
            for way in range(2):
                d_copy(way).start()
            m_copy(CX - 1).start()
            m_copy(0).start()

        return carry

    def first_step(i, carry):
        group = jnp.where(i < 4, i, i - 4)

        @pl.when(jnp.logical_and(has_down, i < 3))
        def _():
            z_copy(i + 1, 0).wait_recv()

        @pl.when(jnp.logical_and(has_down, i == 2))
        def _():
            z_copy(0, 0).wait_recv()

        units = units_of(group, lax.div(i, 4), jnp.where(i < 3, 0, 1))
        first_units(units)

        @pl.when(jnp.logical_and(has_down, i < 4))
        def _():
            m_copy(units[0][0]).start()
            m_copy(units[1][0]).start()

            @pl.when(i < 3)
            def _():
                m_copy(units[2][0]).start()
                m_copy(units[3][0]).start()

        return carry

    lax.fori_loop(0, 7, first_step, 0)

    def second_step(i, carry):
        @pl.when(i == RIMS_AT)
        def _():
            lax.fori_loop(0, 4, first_rims, 0)

        @pl.when(i == 3)
        def _():
            @pl.when(has_up)
            def _():
                z_copy(1, 1).wait_recv()
                z_copy(2, 1).wait_recv()

            def top(j, carry):
                row = jnp.broadcast_to(heat[0, 1, :, pl.ds(7, 1), :], (1, 8, LANES))
                advance_row(s0, s1, cs, 1 + 6 * j, BASE0 + CZ - 1, ABOVE, CZ - 1, row)
                return carry

            lax.fori_loop(0, 2, top, 0)

        @pl.when(jnp.logical_and(has_up, i == 3))
        def _():
            c_copy().wait_recv()

            def above_trig(k, carry):
                for x in (0, 8):
                    for i in range(2):
                        flat, rows = strided(cs, i, k, x, CZ)
                        for j in range(YT):
                            part = low[k, pl.ds(x, 8), pl.ds(j * LANES, LANES)]
                            flat[rows[j], :] = sine_cosine(part)[i]
                return carry

            lax.fori_loop(0, ORDERS, above_trig, 0)
            for x in range(3, 9):
                m_copy(x).wait_recv()

        @pl.when(jnp.logical_and(has_up, i == 4))
        def _():
            for x in range(9, 13):
                m_copy(x).wait_recv()

        @pl.when(jnp.logical_and(has_up, i == 5))
        def _():
            for x in (13, 14, 1, 2):
                m_copy(x).wait_recv()

        @pl.when(jnp.logical_and(has_up, i == 6))
        def _():
            m_copy(CX - 1).wait_recv()
            m_copy(0).wait_recv()

        group = jnp.where(i < 3, i, i - 3)
        second_units(o, s1, cs, heat, units_of(group, jnp.where(jnp.logical_and(i >= 3, i < 6), 1, 0), jnp.where(i < 3, 0, 1)), 0)
        return carry

    lax.fori_loop(0, 7, second_step, 0)
    clear_top(o, has_up)

    for way in range(2):
        for piece in range(4):
            x_copy(0, way, piece).wait_send()

    @pl.when(has_up)
    def _():
        for group in range(GROUPS):
            z_copy(group, 0).wait_send()

    @pl.when(has_down)
    def _():
        for group in range(GROUPS):
            z_copy(group, 1).wait_send()
        for x in range(CX):
            m_copy(x).wait_send()
        c_copy().wait_send()
        d_copy(0).wait_send()
        d_copy(1).wait_send()

    @pl.when(has_up)
    def _():
        d_copy(0).wait_recv()
        d_copy(1).wait_recv()

    for way in range(2):
        for piece in range(4):
            x_copy(1, way, piece).wait()


def finish(o, s1, cs, heat, phase_out, solute_out, rims, sem):
    inner = pl.ds(1, CX - 2)
    copies = [
        pltpu.make_async_copy(o.at[pl.ds(0, ORDERS), inner], phase_out.at[:, inner], sem.at[0]),
        pltpu.make_async_copy(o.at[ORDERS, inner], solute_out.at[inner], sem.at[1]),
    ]
    for copy in copies:
        copy.start()
    for i, x in enumerate((0, CX - 1)):
        second_units(rims.at[:, pl.ds(i, 1)], s1, cs, heat, ((x, 0), (x, 1)), x)
    clear_top(rims, lax.axis_index("gz") < lax.axis_size("gz") - 1)
    for i, x in enumerate((0, CX - 1)):
        ends = [
            pltpu.make_async_copy(rims.at[pl.ds(0, ORDERS), i], phase_out.at[:, x], sem.at[2 + 2 * i]),
            pltpu.make_async_copy(rims.at[ORDERS, i], solute_out.at[x], sem.at[3 + 2 * i]),
        ]
        for copy in ends:
            copy.start()
        copies += ends
    for copy in copies:
        copy.wait()


def local(phase, solute, grain_map, frame_steps):
    hbm, vmem = pl.BlockSpec(memory_space=pltpu.HBM), pl.BlockSpec(memory_space=pltpu.VMEM)
    dma = pltpu.SemaphoreType.DMA
    args = [pltpu.with_memory_space_constraint(a, pltpu.HBM) for a in (frame_steps, phase, solute, grain_map)]
    results = pl.pallas_call(
        kernel,
        out_shape=(
            pltpu.VMEM((FIELDS, CX, CZ, NY), jnp.float32),
            pltpu.VMEM((FIELDS, CX + 2, YT, 24, LANES), jnp.float32),
            pltpu.VMEM((2, ORDERS, CX, YT, 24, LANES), jnp.float32),
            pltpu.VMEM((STEPS, 2, 1, 8, LANES), jnp.float32),
        ),
        in_specs=[hbm] * 4,
        out_specs=(vmem,) * 4,
        scratch_shapes=[
            pltpu.VMEM((FIELDS, CX + 2, YT, 32, LANES), jnp.float32),
            pltpu.VMEM((ORDERS, CX, YT, CZ, LANES), jnp.int32),
            pltpu.VMEM((ORDERS, CX, NY), jnp.int32),
            pltpu.SMEM((STEPS,), jnp.int32),
            dma((3, YT)),
            dma,
            dma((STEPS, 2, 4)),
            dma((STEPS, 2, 4)),
            dma((2, GROUPS)),
            dma((2, GROUPS)),
            dma((CX,)),
            dma((CX,)),
            dma,
            dma,
            dma((2,)),
            dma((2,)),
        ],
        compiler_params=pltpu.CompilerParams(
            collective_id=0, has_side_effects=True, vmem_limit_bytes=32 * 1024 * 1024
        ),
        name="grow",
    )(*args)
    return pl.pallas_call(
        finish,
        out_shape=(
            pltpu.HBM(phase.shape, jnp.float32),
            pltpu.HBM(solute.shape, jnp.float32),
        ),
        in_specs=[vmem] * 4,
        out_specs=(hbm, hbm),
        scratch_shapes=[pltpu.VMEM((FIELDS, 2, CZ, NY), jnp.float32), dma((6,))],
        compiler_params=pltpu.CompilerParams(vmem_limit_bytes=16 * 1024 * 1024),
        name="finish",
    )(*results)


def solution(mesh):
    in_specs = (P(None, "gx", "gz", None), P("gx", "gz", None), P(None, "gx", "gz", None), P())
    out_specs = (P(None, "gx", "gz", None), P("gx", "gz", None))
    return jax.shard_map(local, mesh=mesh, in_specs=in_specs, out_specs=out_specs, check_vma=False)
```

```python
import math

import jax
import jax.numpy as jnp
import numpy as np
from jax import lax
from jax.experimental import pallas as pl
from jax.experimental.pallas import tpu as pltpu
from jax.sharding import PartitionSpec as P

ORDERS = 4
FIELDS = 5
STEPS = 2
NGRAIN = 1024
NZ = 256
CX = 16
CZ = 16
NY = 512
LANES = 128
YT = NY // LANES
GROUP = 4
GROUPS = CX // GROUP
MESH = pl.DeviceIdType.MESH

BASE0 = 8

ABOVE = BASE0 + CZ + 2

RIMS_AT = 0


def sine_coefficients():
    nodes = np.cos(np.pi * (np.arange(400) + 0.5) / 400)
    theta = nodes * np.pi / 2
    even = np.polynomial.chebyshev.Chebyshev.fit(nodes, np.cos(theta), 8, domain=[-1, 1])
    odd = np.polynomial.chebyshev.Chebyshev.fit(nodes, np.sin(theta), 9, domain=[-1, 1])
    even = even.convert(kind=np.polynomial.Polynomial).coef
    odd = odd.convert(kind=np.polynomial.Polynomial).coef
    cos_c = [float(even[i] * math.sqrt(0.5) / 128.0**i) for i in (0, 2, 4, 6, 8)]
    sin_c = [float(odd[i] * math.sqrt(2.0) / 128.0**i) for i in (1, 3, 5, 7, 9)]
    return sin_c, cos_c


SIN_C, COS_C = sine_coefficients()


def horner(x, coefficients):
    value = coefficients[-1]
    for c in coefficients[-2::-1]:
        value = value * x + c
    return value


def next_y(rolled, offset):
    if offset > 0:
        return jnp.concatenate([rolled[1:], rolled[:1]], axis=0)
    return jnp.concatenate([rolled[-1:], rolled[:-1]], axis=0)


def neighbours(load, f, part):
    ys = slice(None) if part is None else pl.ds(2 * part, 2)
    c = load(f, 0, 0, ys)
    xl, xh = load(f, -1, 0, ys), load(f, 1, 0, ys)
    zl, zh = load(f, 0, -1, ys), load(f, 0, 1, ys)
    lane = lax.broadcasted_iota(jnp.int32, c.shape, 2)
    right = pltpu.roll(c, 1, axis=2)
    left = pltpu.roll(c, LANES - 1, axis=2)
    if part is None:
        before, after = next_y(right, -1), next_y(left, 1)
    else:
        before = load(f, 0, 0, pl.ds(lax.rem(2 * part + YT - 1, YT), 1))
        after = load(f, 0, 0, pl.ds(lax.rem(2 * part + 2, YT), 1))
        before = jnp.concatenate([pltpu.roll(before, 1, axis=2), right[:1]], axis=0)
        after = jnp.concatenate([left[1:], pltpu.roll(after, LANES - 1, axis=2)], axis=0)
    yl = jnp.where(lane == 0, before, right)
    yh = jnp.where(lane == LANES - 1, after, left)
    return c, xl, xh, yl, yh, zl, zh


def advance(load, table, thermal, put, part=None):
    ys = slice(None) if part is None else pl.ds(2 * part, 2)
    drive = thermal - 2.4 * load(ORDERS, 0, 0, ys)
    q = None
    for k in range(ORDERS):
        p = load(k, 0, 0, ys)
        q = p * p if q is None else q + p * p
    well = 0.64 - 0.16 * q
    total = None
    for k in range(ORDERS):
        p, xl, xh, yl, yh, zl, zh = neighbours(load, k, part)
        gx, gy, gz = xh - xl, yh - yl, zh - zl
        lap = (xl + xh) + (yl + yh) + (zl + zh) - 6.0 * p
        x2, y2, z2 = gx * gx, gy * gy, gz * gz
        r = x2 + y2
        t = table(0, k, ys) * (gx * gy) + table(1, k, ys) * (x2 - y2)
        quartic = r * r + z2 * z2 - t * t
        d = (r + z2) + 0.2
        ratio = quartic * pl.reciprocal(d * d, approx=True)
        w = p - p * p
        delta = (
            lap * (0.08 + 0.04 * ratio)
            + p * (well + p * (1.44 * p - 1.92))
            + (w * w) * drive
        )
        put(k, p + delta)
        total = delta if total is None else total + delta
    c, xl, xh, yl, yh, zl, zh = neighbours(load, ORDERS, part)
    near = (xl + xh) + (yl + yh) + (zl + zh)
    put(ORDERS, 0.52 * c + 0.08 * near + 0.5 * total)


def advance_tile(s, cs, x, row, cs_row, thermal, put, part=None):
    def load(f, dx, dz, ys):
        return s[f, x + 1 + dx, ys, pl.ds(row + dz, 8), :]

    def table(i, k, ys):
        return cs[i, k, x, ys, pl.ds(cs_row, 8), :]

    advance(load, table, thermal, put, part)


def advance_row(s, s_new, cs, x, row, above, z, thermal):
    def load(f, dx, dz, ys):
        flat, rows = strided(s, f, x + 1 + dx, above if dz > 0 else row + dz)
        return jnp.stack([flat[r, :] for r in rows])

    def table(i, k, ys):
        flat, rows = strided(cs, i, k, x, z)
        return jnp.stack([flat[r, :] for r in rows])

    def put(f, value):
        flat, rows = strided(s_new, f, x + 1, z)
        for k in range(YT):
            flat[rows[k], :] = value[k]

    advance(load, table, thermal, put)


def sine_cosine(grain):
    h = ((grain & 255) - 128).astype(jnp.float32)
    h2 = h * h
    return h * horner(h2, SIN_C), horner(h2, COS_C)


def strided(ref, *at):
    *outer, plane, where = at
    planes, rows = ref.shape[-4], ref.shape[-2]
    first = 0
    for size, index in zip(ref.shape, outer):
        first = first * size + index
    first = (first * planes + plane) * YT * rows + where
    flat = ref.reshape(math.prod(ref.shape[:-1]), LANES)
    return flat, [pl.ds(first + k * rows, 8, stride=YT * rows) for k in range(YT)]


def tile(half):
    return pl.ds(8 * half if isinstance(half, int) else pl.multiple_of(8 * half, 8), 8)


def second_units(o, s1, cs, heat, units, first):
    for x, half in units:

        def put(f, value, x=x, half=half):
            for k in range(YT):
                o[f, x - first, tile(half), pl.ds(k * LANES, LANES)] = value[k]

        advance_tile(s1, cs, x, 1 + 8 * half, 1 + 8 * half, heat[1, half], put)


def clear_top(o, has_up):
    @pl.when(jnp.logical_not(has_up))
    def _():
        def clear(x, carry):
            o[:, x, pl.ds(CZ - 1, 1), :] = jnp.zeros((FIELDS, 1, NY), jnp.float32)
            return carry

        lax.fori_loop(0, o.shape[1], clear, 0)


def kernel(
    frames_in, phase, solute, grain, o, s1, cs, heat,
    s0, g, low, frames,
    load_sem, frame_sem, x_send, x_recv, z_send, z_recv, m_send, m_recv, c_send, c_recv, d_send, d_recv,
):
    gx, gz = lax.axis_index("gx"), lax.axis_index("gz")
    n_gx, n_gz = lax.axis_size("gx"), lax.axis_size("gz")
    right, left = lax.rem(gx + 1, n_gx), lax.rem(gx + n_gx - 1, n_gx)
    has_up, has_down = gz < n_gz - 1, gz > 0

    loads = []
    for k in range(YT):
        lanes = pl.ds(k * LANES, LANES)
        rows = pl.ds(BASE0, CZ)
        loads.append(
            (
                pltpu.make_async_copy(
                    phase.at[:, :, :, lanes], s0.at[pl.ds(0, ORDERS), pl.ds(1, CX), k, rows, :], load_sem.at[0, k]
                ),
                pltpu.make_async_copy(
                    solute.at[:, :, lanes], s0.at[ORDERS, pl.ds(1, CX), k, rows, :], load_sem.at[1, k]
                ),
                pltpu.make_async_copy(grain.at[:, :, :, lanes], g.at[:, :, k, :, :], load_sem.at[2, k]),
            )
        )
    frame_load = pltpu.make_async_copy(frames_in, frames, frame_sem)
    barrier = pltpu.get_barrier_semaphore()

    def greet(ix, iz):
        pl.semaphore_signal(barrier, inc=1, device_id=(ix, iz), device_id_type=MESH)

    greet(left, gz)
    greet(right, gz)

    @pl.when(has_up)
    def _():
        greet(gx, gz + 1)

    @pl.when(has_down)
    def _():
        greet(gx, gz - 1)

    for which in range(3):
        for k in range(YT):
            loads[k][which].start()

    frame_load.start()

    @pl.when(jnp.logical_not(has_down))
    def _():
        def clear(x, carry):
            s0[:, x, :, pl.ds(BASE0 - 1, 1), :] = jnp.zeros((FIELDS, YT, 1, LANES), jnp.float32)
            return carry

        lax.fori_loop(0, CX + 2, clear, 0)

    @pl.when(jnp.logical_not(has_up))
    def _():
        def clear(x, carry):
            s0[:, x, :, pl.ds(ABOVE, 1), :] = jnp.zeros((FIELDS, YT, 1, LANES), jnp.float32)
            s1[:, x, :, pl.ds(CZ, 2), :] = jnp.zeros((FIELDS, YT, 2, LANES), jnp.float32)
            return carry

        lax.fori_loop(0, CX + 2, clear, 0)

        def clear_cs(x, carry):
            cs[:, :, x, :, pl.ds(CZ, 1), :] = jnp.zeros((2, ORDERS, YT, 1, LANES), jnp.float32)
            return carry

        lax.fori_loop(0, CX, clear_cs, 0)

    def remote(src, dst, send, recv, ix, iz):
        return pltpu.make_async_remote_copy(
            src_ref=src, dst_ref=dst, send_sem=send, recv_sem=recv, device_id=(ix, iz), device_id_type=MESH
        )

    def x_copy(step, way, piece):
        s, base = (s0, BASE0) if step == 0 else (s1, 0)
        half, part = lax.div(piece, 2), lax.rem(piece, 2)
        ys, rows = pl.ds(2 * part, 2), pl.ds(base + 8 * half, 8)
        src, dst, to = (CX, 0, right) if way == 0 else (1, CX + 1, left)
        return remote(
            s.at[:, src, ys, rows, :],
            s.at[:, dst, ys, rows, :],
            x_send.at[step, way, piece],
            x_recv.at[step, way, piece],
            to,
            gz,
        )

    def z_copy(group, way):
        planes = pl.ds(1 + group * GROUP, GROUP)
        src, dst, to = (BASE0 + CZ - 1, BASE0 - 1, gz + 1) if way == 0 else (BASE0, ABOVE, gz - 1)
        return remote(
            s0.at[:, planes, :, pl.ds(src, 1), :],
            s0.at[:, planes, :, pl.ds(dst, 1), :],
            z_send.at[way, group],
            z_recv.at[way, group],
            gx,
            to,
        )

    def m_copy(x):
        return remote(
            s1.at[:, x + 1, :, pl.ds(0, 2), :],
            s1.at[:, x + 1, :, pl.ds(CZ, 2), :],
            m_send.at[x],
            m_recv.at[x],
            gx,
            gz - 1,
        )

    def d_copy(way):
        src, dst, to = (CX, 0, right) if way == 0 else (1, CX + 1, left)
        return remote(
            s1.at[:, src, :, pl.ds(0, 1), :],
            s1.at[:, dst, :, pl.ds(CZ, 1), :],
            d_send.at[way],
            d_recv.at[way],
            to,
            gz - 1,
        )

    def c_copy():
        return remote(grain.at[:, :, 0, :], low, c_send, c_recv, gx, gz - 1)

    for which in range(2):
        for k in range(YT):
            loads[k][which].wait()

    pl.semaphore_wait(barrier, 2 + has_up.astype(jnp.int32) + has_down.astype(jnp.int32))

    for piece in range(4):
        x_copy(0, 0, piece).start()
        x_copy(0, 1, piece).start()
    @pl.when(has_down)
    def _():
        for group in (3, 0, 1, 2):
            z_copy(group, 1).start()

    @pl.when(has_up)
    def _():
        for group in (1, 2, 3, 0):
            z_copy(group, 0).start()

    @pl.when(has_down)
    def _():
        c_copy().start()

    for k in range(YT):
        loads[k][2].wait()

    def trig(x, carry):
        for k in range(ORDERS):
            for half in range(2):
                at = pl.ds(8 * half, 8)
                cs[0, k, x, :, at, :], cs[1, k, x, :, at, :] = sine_cosine(g[k, x, :, at, :])
        return carry

    lax.fori_loop(0, CX, trig, 0)

    frame_load.wait()
    for step in range(STEPS):
        for half in range(2):
            z = gz * CZ + 8 * half + step + lax.broadcasted_iota(jnp.int32, (1, 8, LANES), 1)
            height = (NZ // 2 - z - frames[step]).astype(jnp.float32)
            heat[step, half] = 2.4 * jnp.tanh(height * 0.125)

    def first_units(units):
        for x, half in units:

            def put(f, value, x=x, half=half):
                s1[f, x + 1, :, tile(half), :] = value

            advance_tile(s0, cs, x, BASE0 + 8 * half, 8 * half, heat[0, half], put)

    def units_of(group, lower, upper):
        xa = jnp.where(group < 3, 4 + 4 * group, 14)
        xb = jnp.where(group < 3, xa + 1, 1)
        xc = jnp.where(group < 2, xa + 2, jnp.where(group == 2, 2, 14))
        xd = jnp.where(group < 3, xc + 1, 1)
        return ((xa, lower), (xb, lower), (xc, upper), (xd, upper))

    def first_rims(piece, carry):
        half, part = lax.div(piece, 2), lax.rem(piece, 2)
        @pl.when(piece == 2)
        def _():
            @pl.when(has_up)
            def _():
                z_copy(0, 1).wait_recv()
                z_copy(3, 1).wait_recv()

            for xi in (1, CX):
                s0[:, xi, :, pl.ds(BASE0 + CZ, 1), :] = s0[:, xi, :, pl.ds(ABOVE, 1), :]

        x_copy(0, 0, piece).wait_recv()
        x_copy(0, 1, piece).wait_recv()
        for x in (CX - 1, 0):

            def put(f, value, x=x):
                s1[f, x + 1, pl.ds(2 * part, 2), tile(half), :] = value

            advance_tile(s0, cs, x, BASE0 + 8 * half, 8 * half, heat[0, half], put, part)
        x_copy(1, 0, piece).start()
        x_copy(1, 1, piece).start()

        @pl.when(jnp.logical_and(piece == 1, has_down))
        def _():
            for way in range(2):
                d_copy(way).start()
            m_copy(CX - 1).start()
            m_copy(0).start()

        return carry

    def first_step(i, carry):
        group = jnp.where(i < 4, i, i - 4)

        @pl.when(jnp.logical_and(has_down, i < 3))
        def _():
            z_copy(i + 1, 0).wait_recv()

        @pl.when(jnp.logical_and(has_down, i == 2))
        def _():
            z_copy(0, 0).wait_recv()

        units = units_of(group, lax.div(i, 4), jnp.where(i < 3, 0, 1))
        first_units(units)

        @pl.when(jnp.logical_and(has_down, i < 4))
        def _():
            m_copy(units[0][0]).start()
            m_copy(units[1][0]).start()

            @pl.when(i < 3)
            def _():
                m_copy(units[2][0]).start()
                m_copy(units[3][0]).start()

        return carry

    lax.fori_loop(0, 7, first_step, 0)

    def second_step(i, carry):
        @pl.when(i == RIMS_AT)
        def _():
            lax.fori_loop(0, 4, first_rims, 0)

        @pl.when(i == 3)
        def _():
            @pl.when(has_up)
            def _():
                z_copy(1, 1).wait_recv()
                z_copy(2, 1).wait_recv()

            def top(j, carry):
                row = jnp.broadcast_to(heat[0, 1, :, pl.ds(7, 1), :], (1, 8, LANES))
                advance_row(s0, s1, cs, 1 + 6 * j, BASE0 + CZ - 1, ABOVE, CZ - 1, row)
                return carry

            lax.fori_loop(0, 2, top, 0)

        @pl.when(jnp.logical_and(has_up, i == 3))
        def _():
            c_copy().wait_recv()

            def above_trig(k, carry):
                for x in (0, 8):
                    for i in range(2):
                        flat, rows = strided(cs, i, k, x, CZ)
                        for j in range(YT):
                            part = low[k, pl.ds(x, 8), pl.ds(j * LANES, LANES)]
                            flat[rows[j], :] = sine_cosine(part)[i]
                return carry

            lax.fori_loop(0, ORDERS, above_trig, 0)
            for x in range(3, 9):
                m_copy(x).wait_recv()

        @pl.when(jnp.logical_and(has_up, i == 4))
        def _():
            for x in range(9, 13):
                m_copy(x).wait_recv()

        @pl.when(jnp.logical_and(has_up, i == 5))
        def _():
            for x in (13, 14, 1, 2):
                m_copy(x).wait_recv()

        @pl.when(jnp.logical_and(has_up, i == 6))
        def _():
            m_copy(CX - 1).wait_recv()
            m_copy(0).wait_recv()

        group = jnp.where(i < 3, i, i - 3)
        second_units(o, s1, cs, heat, units_of(group, jnp.where(jnp.logical_and(i >= 3, i < 6), 1, 0), jnp.where(i < 3, 0, 1)), 0)
        return carry

    lax.fori_loop(0, 7, second_step, 0)
    clear_top(o, has_up)

    for way in range(2):
        for piece in range(4):
            x_copy(0, way, piece).wait_send()

    @pl.when(has_up)
    def _():
        for group in range(GROUPS):
            z_copy(group, 0).wait_send()

    @pl.when(has_down)
    def _():
        for group in range(GROUPS):
            z_copy(group, 1).wait_send()
        for x in range(CX):
            m_copy(x).wait_send()
        c_copy().wait_send()
        d_copy(0).wait_send()
        d_copy(1).wait_send()

    @pl.when(has_up)
    def _():
        d_copy(0).wait_recv()
        d_copy(1).wait_recv()

    for way in range(2):
        for piece in range(4):
            x_copy(1, way, piece).wait()


def finish(o, s1, cs, heat, phase_out, solute_out, rims, sem):
    inner = pl.ds(1, CX - 2)
    copies = [
        pltpu.make_async_copy(o.at[pl.ds(0, ORDERS), inner], phase_out.at[:, inner], sem.at[0]),
        pltpu.make_async_copy(o.at[ORDERS, inner], solute_out.at[inner], sem.at[1]),
    ]
    for copy in copies:
        copy.start()
    has_up = lax.axis_index("gz") < lax.axis_size("gz") - 1
    for i, x in enumerate((0, CX - 1)):
        rim = rims.at[:, pl.ds(i, 1)]
        second_units(rim, s1, cs, heat, ((x, 0), (x, 1)), x)
        clear_top(rim, has_up)
        ends = [
            pltpu.make_async_copy(rims.at[pl.ds(0, ORDERS), i], phase_out.at[:, x], sem.at[2 + 2 * i]),
            pltpu.make_async_copy(rims.at[ORDERS, i], solute_out.at[x], sem.at[3 + 2 * i]),
        ]
        for copy in ends:
            copy.start()
        copies += ends
    for copy in copies:
        copy.wait()


def local(phase, solute, grain_map, frame_steps):
    hbm, vmem = pl.BlockSpec(memory_space=pltpu.HBM), pl.BlockSpec(memory_space=pltpu.VMEM)
    dma = pltpu.SemaphoreType.DMA
    args = [pltpu.with_memory_space_constraint(a, pltpu.HBM) for a in (frame_steps, phase, solute, grain_map)]
    results = pl.pallas_call(
        kernel,
        out_shape=(
            pltpu.VMEM((FIELDS, CX, CZ, NY), jnp.float32),
            pltpu.VMEM((FIELDS, CX + 2, YT, 24, LANES), jnp.float32),
            pltpu.VMEM((2, ORDERS, CX, YT, 24, LANES), jnp.float32),
            pltpu.VMEM((STEPS, 2, 1, 8, LANES), jnp.float32),
        ),
        in_specs=[hbm] * 4,
        out_specs=(vmem,) * 4,
        scratch_shapes=[
            pltpu.VMEM((FIELDS, CX + 2, YT, 32, LANES), jnp.float32),
            pltpu.VMEM((ORDERS, CX, YT, CZ, LANES), jnp.int32),
            pltpu.VMEM((ORDERS, CX, NY), jnp.int32),
            pltpu.SMEM((STEPS,), jnp.int32),
            dma((3, YT)),
            dma,
            dma((STEPS, 2, 4)),
            dma((STEPS, 2, 4)),
            dma((2, GROUPS)),
            dma((2, GROUPS)),
            dma((CX,)),
            dma((CX,)),
            dma,
            dma,
            dma((2,)),
            dma((2,)),
        ],
        compiler_params=pltpu.CompilerParams(
            collective_id=0, has_side_effects=True, vmem_limit_bytes=32 * 1024 * 1024
        ),
        name="grow",
    )(*args)
    return pl.pallas_call(
        finish,
        out_shape=(
            pltpu.HBM(phase.shape, jnp.float32),
            pltpu.HBM(solute.shape, jnp.float32),
        ),
        in_specs=[vmem] * 4,
        out_specs=(hbm, hbm),
        scratch_shapes=[pltpu.VMEM((FIELDS, 2, CZ, NY), jnp.float32), dma((6,))],
        compiler_params=pltpu.CompilerParams(vmem_limit_bytes=16 * 1024 * 1024),
        name="finish",
    )(*results)


def solution(mesh):
    in_specs = (P(None, "gx", "gz", None), P("gx", "gz", None), P(None, "gx", "gz", None), P())
    out_specs = (P(None, "gx", "gz", None), P("gx", "gz", None))
    return jax.shard_map(local, mesh=mesh, in_specs=in_specs, out_specs=out_specs, check_vma=False)
```

```python
import math

import jax
import jax.numpy as jnp
import numpy as np
from jax import lax
from jax.experimental import pallas as pl
from jax.experimental.pallas import tpu as pltpu
from jax.sharding import PartitionSpec as P

ORDERS = 4
FIELDS = 5
STEPS = 2
NGRAIN = 1024
NZ = 256
CX = 16
CZ = 16
NY = 512
LANES = 128
YT = NY // LANES
GROUP = 4
GROUPS = CX // GROUP
MESH = pl.DeviceIdType.MESH

BASE0 = 8

ABOVE = BASE0 + CZ + 2

RIMS_AT = 0


def sine_coefficients():
    nodes = np.cos(np.pi * (np.arange(400) + 0.5) / 400)
    theta = nodes * np.pi / 2
    even = np.polynomial.chebyshev.Chebyshev.fit(nodes, np.cos(theta), 8, domain=[-1, 1])
    odd = np.polynomial.chebyshev.Chebyshev.fit(nodes, np.sin(theta), 9, domain=[-1, 1])
    even = even.convert(kind=np.polynomial.Polynomial).coef
    odd = odd.convert(kind=np.polynomial.Polynomial).coef
    cos_c = [float(even[i] * math.sqrt(0.5) / 128.0**i) for i in (0, 2, 4, 6, 8)]
    sin_c = [float(odd[i] * math.sqrt(2.0) / 128.0**i) for i in (1, 3, 5, 7, 9)]
    return sin_c, cos_c


SIN_C, COS_C = sine_coefficients()


def horner(x, coefficients):
    value = coefficients[-1]
    for c in coefficients[-2::-1]:
        value = value * x + c
    return value


def next_y(rolled, offset):
    if offset > 0:
        return jnp.concatenate([rolled[1:], rolled[:1]], axis=0)
    return jnp.concatenate([rolled[-1:], rolled[:-1]], axis=0)


def neighbours(load, f, part):
    ys = slice(None) if part is None else pl.ds(2 * part, 2)
    c = load(f, 0, 0, ys)
    xl, xh = load(f, -1, 0, ys), load(f, 1, 0, ys)
    zl, zh = load(f, 0, -1, ys), load(f, 0, 1, ys)
    lane = lax.broadcasted_iota(jnp.int32, c.shape, 2)
    right = pltpu.roll(c, 1, axis=2)
    left = pltpu.roll(c, LANES - 1, axis=2)
    if part is None:
        before, after = next_y(right, -1), next_y(left, 1)
    else:
        before = load(f, 0, 0, pl.ds(lax.rem(2 * part + YT - 1, YT), 1))
        after = load(f, 0, 0, pl.ds(lax.rem(2 * part + 2, YT), 1))
        before = jnp.concatenate([pltpu.roll(before, 1, axis=2), right[:1]], axis=0)
        after = jnp.concatenate([left[1:], pltpu.roll(after, LANES - 1, axis=2)], axis=0)
    yl = jnp.where(lane == 0, before, right)
    yh = jnp.where(lane == LANES - 1, after, left)
    return c, xl, xh, yl, yh, zl, zh


def advance(load, table, thermal, put, part=None):
    ys = slice(None) if part is None else pl.ds(2 * part, 2)
    drive = thermal - 2.4 * load(ORDERS, 0, 0, ys)
    q = None
    for k in range(ORDERS):
        p = load(k, 0, 0, ys)
        q = p * p if q is None else q + p * p
    well = 0.64 - 0.16 * q
    total = None
    for k in range(ORDERS):
        p, xl, xh, yl, yh, zl, zh = neighbours(load, k, part)
        gx, gy, gz = xh - xl, yh - yl, zh - zl
        lap = (xl + xh) + (yl + yh) + (zl + zh) - 6.0 * p
        x2, y2, z2 = gx * gx, gy * gy, gz * gz
        r = x2 + y2
        t = table(0, k, ys) * (gx * gy) + table(1, k, ys) * (x2 - y2)
        quartic = r * r + z2 * z2 - t * t
        d = (r + z2) + 0.2
        ratio = quartic * pl.reciprocal(d * d, approx=True)
        w = p - p * p
        delta = (
            lap * (0.08 + 0.04 * ratio)
            + p * (well + p * (1.44 * p - 1.92))
            + (w * w) * drive
        )
        put(k, p + delta)
        total = delta if total is None else total + delta
    c, xl, xh, yl, yh, zl, zh = neighbours(load, ORDERS, part)
    near = (xl + xh) + (yl + yh) + (zl + zh)
    put(ORDERS, 0.52 * c + 0.08 * near + 0.5 * total)


def advance_tile(s, cs, x, row, cs_row, thermal, put, part=None):
    def load(f, dx, dz, ys):
        return s[f, x + 1 + dx, ys, pl.ds(row + dz, 8), :]

    def table(i, k, ys):
        return cs[i, k, x, ys, pl.ds(cs_row, 8), :]

    advance(load, table, thermal, put, part)


def advance_row(s, s_new, cs, x, row, above, z, thermal):
    def load(f, dx, dz, ys):
        flat, rows = strided(s, f, x + 1 + dx, above if dz > 0 else row + dz)
        return jnp.stack([flat[r, :] for r in rows])

    def table(i, k, ys):
        flat, rows = strided(cs, i, k, x, z)
        return jnp.stack([flat[r, :] for r in rows])

    def put(f, value):
        flat, rows = strided(s_new, f, x + 1, z)
        for k in range(YT):
            flat[rows[k], :] = value[k]

    advance(load, table, thermal, put)


def sine_cosine(grain):
    h = ((grain & 255) - 128).astype(jnp.float32)
    h2 = h * h
    return h * horner(h2, SIN_C), horner(h2, COS_C)


def strided(ref, *at):
    *outer, plane, where = at
    planes, rows = ref.shape[-4], ref.shape[-2]
    first = 0
    for size, index in zip(ref.shape, outer):
        first = first * size + index
    first = (first * planes + plane) * YT * rows + where
    flat = ref.reshape(math.prod(ref.shape[:-1]), LANES)
    return flat, [pl.ds(first + k * rows, 8, stride=YT * rows) for k in range(YT)]


def tile(half):
    return pl.ds(8 * half if isinstance(half, int) else pl.multiple_of(8 * half, 8), 8)


def second_units(o, s1, cs, heat, units, first):
    for x, half in units:

        def put(f, value, x=x, half=half):
            for k in range(YT):
                o[f, x - first, tile(half), pl.ds(k * LANES, LANES)] = value[k]

        advance_tile(s1, cs, x, 1 + 8 * half, 1 + 8 * half, heat[1, half], put)


def clear_top(o, has_up):
    @pl.when(jnp.logical_not(has_up))
    def _():
        def clear(x, carry):
            o[:, x, pl.ds(CZ - 1, 1), :] = jnp.zeros((FIELDS, 1, NY), jnp.float32)
            return carry

        lax.fori_loop(0, o.shape[1], clear, 0)


def kernel(
    frames_in, phase, solute, grain, o, s1, cs, heat,
    s0, g, low, frames,
    load_sem, frame_sem, x_send, x_recv, z_send, z_recv, m_send, m_recv, c_send, c_recv, d_send, d_recv,
):
    gx, gz = lax.axis_index("gx"), lax.axis_index("gz")
    n_gx, n_gz = lax.axis_size("gx"), lax.axis_size("gz")
    right, left = lax.rem(gx + 1, n_gx), lax.rem(gx + n_gx - 1, n_gx)
    has_up, has_down = gz < n_gz - 1, gz > 0

    loads = []
    for k in range(YT):
        lanes = pl.ds(k * LANES, LANES)
        rows = pl.ds(BASE0, CZ)
        loads.append(
            (
                pltpu.make_async_copy(
                    phase.at[:, :, :, lanes], s0.at[pl.ds(0, ORDERS), pl.ds(1, CX), k, rows, :], load_sem.at[0, k]
                ),
                pltpu.make_async_copy(
                    solute.at[:, :, lanes], s0.at[ORDERS, pl.ds(1, CX), k, rows, :], load_sem.at[1, k]
                ),
                pltpu.make_async_copy(grain.at[:, :, :, lanes], g.at[:, :, k, :, :], load_sem.at[2, k]),
            )
        )
    frame_load = pltpu.make_async_copy(frames_in, frames, frame_sem)
    barrier = pltpu.get_barrier_semaphore()

    def greet(ix, iz):
        pl.semaphore_signal(barrier, inc=1, device_id=(ix, iz), device_id_type=MESH)

    greet(left, gz)
    greet(right, gz)

    @pl.when(has_up)
    def _():
        greet(gx, gz + 1)

    @pl.when(has_down)
    def _():
        greet(gx, gz - 1)

    for which in range(3):
        for k in range(YT):
            loads[k][which].start()

    frame_load.start()

    @pl.when(jnp.logical_not(has_down))
    def _():
        def clear(x, carry):
            s0[:, x, :, pl.ds(BASE0 - 1, 1), :] = jnp.zeros((FIELDS, YT, 1, LANES), jnp.float32)
            return carry

        lax.fori_loop(0, CX + 2, clear, 0)

    @pl.when(jnp.logical_not(has_up))
    def _():
        def clear(x, carry):
            s0[:, x, :, pl.ds(ABOVE, 1), :] = jnp.zeros((FIELDS, YT, 1, LANES), jnp.float32)
            s1[:, x, :, pl.ds(CZ, 2), :] = jnp.zeros((FIELDS, YT, 2, LANES), jnp.float32)
            return carry

        lax.fori_loop(0, CX + 2, clear, 0)

        def clear_cs(x, carry):
            cs[:, :, x, :, pl.ds(CZ, 1), :] = jnp.zeros((2, ORDERS, YT, 1, LANES), jnp.float32)
            return carry

        lax.fori_loop(0, CX, clear_cs, 0)

    def remote(src, dst, send, recv, ix, iz):
        return pltpu.make_async_remote_copy(
            src_ref=src, dst_ref=dst, send_sem=send, recv_sem=recv, device_id=(ix, iz), device_id_type=MESH
        )

    def x_copy(step, way, piece):
        s, base = (s0, BASE0) if step == 0 else (s1, 0)
        half, part = lax.div(piece, 2), lax.rem(piece, 2)
        ys, rows = pl.ds(2 * part, 2), pl.ds(base + 8 * half, 8)
        src, dst, to = (CX, 0, right) if way == 0 else (1, CX + 1, left)
        return remote(
            s.at[:, src, ys, rows, :],
            s.at[:, dst, ys, rows, :],
            x_send.at[step, way, piece],
            x_recv.at[step, way, piece],
            to,
            gz,
        )

    def z_copy(group, way):
        planes = pl.ds(1 + group * GROUP, GROUP)
        src, dst, to = (BASE0 + CZ - 1, BASE0 - 1, gz + 1) if way == 0 else (BASE0, ABOVE, gz - 1)
        return remote(
            s0.at[:, planes, :, pl.ds(src, 1), :],
            s0.at[:, planes, :, pl.ds(dst, 1), :],
            z_send.at[way, group],
            z_recv.at[way, group],
            gx,
            to,
        )

    def m_copy(x):
        return remote(
            s1.at[:, x + 1, :, pl.ds(0, 2), :],
            s1.at[:, x + 1, :, pl.ds(CZ, 2), :],
            m_send.at[x],
            m_recv.at[x],
            gx,
            gz - 1,
        )

    def d_copy(way):
        src, dst, to = (CX, 0, right) if way == 0 else (1, CX + 1, left)
        return remote(
            s1.at[:, src, :, pl.ds(0, 1), :],
            s1.at[:, dst, :, pl.ds(CZ, 1), :],
            d_send.at[way],
            d_recv.at[way],
            to,
            gz - 1,
        )

    def c_copy():
        return remote(grain.at[:, :, 0, :], low, c_send, c_recv, gx, gz - 1)

    for which in range(2):
        for k in range(YT):
            loads[k][which].wait()

    pl.semaphore_wait(barrier, 2 + has_up.astype(jnp.int32) + has_down.astype(jnp.int32))

    for piece in range(4):
        x_copy(0, 0, piece).start()
        x_copy(0, 1, piece).start()
    @pl.when(has_down)
    def _():
        for group in (3, 0, 1, 2):
            z_copy(group, 1).start()

    @pl.when(has_up)
    def _():
        for group in (1, 2, 3, 0):
            z_copy(group, 0).start()

    @pl.when(has_down)
    def _():
        c_copy().start()

    for k in range(YT):
        loads[k][2].wait()

    def trig(x, carry):
        for k in range(ORDERS):
            for half in range(2):
                at = pl.ds(8 * half, 8)
                cs[0, k, x, :, at, :], cs[1, k, x, :, at, :] = sine_cosine(g[k, x, :, at, :])
        return carry

    lax.fori_loop(0, CX, trig, 0)

    frame_load.wait()
    for step in range(STEPS):
        for half in range(2):
            z = gz * CZ + 8 * half + step + lax.broadcasted_iota(jnp.int32, (1, 8, LANES), 1)
            height = (NZ // 2 - z - frames[step]).astype(jnp.float32)
            heat[step, half] = 2.4 * jnp.tanh(height * 0.125)

    def first_units(units):
        for x, half in units:

            def put(f, value, x=x, half=half):
                s1[f, x + 1, :, tile(half), :] = value

            advance_tile(s0, cs, x, BASE0 + 8 * half, 8 * half, heat[0, half], put)

    def units_of(group, lower, upper):
        xa = jnp.where(group < 3, 4 + 4 * group, 14)
        xb = jnp.where(group < 3, xa + 1, 1)
        xc = jnp.where(group < 2, xa + 2, jnp.where(group == 2, 2, 14))
        xd = jnp.where(group < 3, xc + 1, 1)
        return ((xa, lower), (xb, lower), (xc, upper), (xd, upper))

    def first_rims(piece, carry):
        half, part = lax.div(piece, 2), lax.rem(piece, 2)
        @pl.when(piece == 2)
        def _():
            @pl.when(has_up)
            def _():
                z_copy(0, 1).wait_recv()
                z_copy(3, 1).wait_recv()

            for xi in (1, CX):
                s0[:, xi, :, pl.ds(BASE0 + CZ, 1), :] = s0[:, xi, :, pl.ds(ABOVE, 1), :]

        x_copy(0, 0, piece).wait_recv()
        x_copy(0, 1, piece).wait_recv()
        for way, x in ((0, CX - 1), (1, 0)):

            def put(f, value, x=x):
                s1[f, x + 1, pl.ds(2 * part, 2), tile(half), :] = value

            advance_tile(s0, cs, x, BASE0 + 8 * half, 8 * half, heat[0, half], put, part)
            x_copy(1, way, piece).start()

        @pl.when(jnp.logical_and(piece == 1, has_down))
        def _():
            for way in range(2):
                d_copy(way).start()
            m_copy(CX - 1).start()
            m_copy(0).start()

        return carry

    def first_step(i, carry):
        group = jnp.where(i < 4, i, i - 4)

        @pl.when(jnp.logical_and(has_down, i < 3))
        def _():
            z_copy(i + 1, 0).wait_recv()

        @pl.when(jnp.logical_and(has_down, i == 2))
        def _():
            z_copy(0, 0).wait_recv()

        units = units_of(group, lax.div(i, 4), jnp.where(i < 3, 0, 1))
        first_units(units)

        @pl.when(jnp.logical_and(has_down, i < 4))
        def _():
            m_copy(units[0][0]).start()
            m_copy(units[1][0]).start()

            @pl.when(i < 3)
            def _():
                m_copy(units[2][0]).start()
                m_copy(units[3][0]).start()

        return carry

    lax.fori_loop(0, 7, first_step, 0)

    def second_step(i, carry):
        @pl.when(i == RIMS_AT)
        def _():
            lax.fori_loop(0, 4, first_rims, 0)

        @pl.when(i == 3)
        def _():
            @pl.when(has_up)
            def _():
                z_copy(1, 1).wait_recv()
                z_copy(2, 1).wait_recv()

            def top(j, carry):
                row = jnp.broadcast_to(heat[0, 1, :, pl.ds(7, 1), :], (1, 8, LANES))
                advance_row(s0, s1, cs, 1 + 6 * j, BASE0 + CZ - 1, ABOVE, CZ - 1, row)
                return carry

            lax.fori_loop(0, 2, top, 0)

        @pl.when(jnp.logical_and(has_up, i == 3))
        def _():
            c_copy().wait_recv()

            def above_trig(k, carry):
                for x in (0, 8):
                    for i in range(2):
                        flat, rows = strided(cs, i, k, x, CZ)
                        for j in range(YT):
                            part = low[k, pl.ds(x, 8), pl.ds(j * LANES, LANES)]
                            flat[rows[j], :] = sine_cosine(part)[i]
                return carry

            lax.fori_loop(0, ORDERS, above_trig, 0)
            for x in range(3, 9):
                m_copy(x).wait_recv()

        @pl.when(jnp.logical_and(has_up, i == 4))
        def _():
            for x in range(9, 13):
                m_copy(x).wait_recv()

        @pl.when(jnp.logical_and(has_up, i == 5))
        def _():
            for x in (13, 14, 1, 2):
                m_copy(x).wait_recv()

        @pl.when(jnp.logical_and(has_up, i == 6))
        def _():
            m_copy(CX - 1).wait_recv()
            m_copy(0).wait_recv()

        group = jnp.where(i < 3, i, i - 3)
        second_units(o, s1, cs, heat, units_of(group, jnp.where(jnp.logical_and(i >= 3, i < 6), 1, 0), jnp.where(i < 3, 0, 1)), 0)
        return carry

    lax.fori_loop(0, 7, second_step, 0)
    clear_top(o, has_up)

    for way in range(2):
        for piece in range(4):
            x_copy(0, way, piece).wait_send()

    @pl.when(has_up)
    def _():
        for group in range(GROUPS):
            z_copy(group, 0).wait_send()

    @pl.when(has_down)
    def _():
        for group in range(GROUPS):
            z_copy(group, 1).wait_send()
        for x in range(CX):
            m_copy(x).wait_send()
        c_copy().wait_send()
        d_copy(0).wait_send()
        d_copy(1).wait_send()

    @pl.when(has_up)
    def _():
        d_copy(0).wait_recv()
        d_copy(1).wait_recv()

    for way in range(2):
        for piece in range(4):
            x_copy(1, way, piece).wait()


def finish(o, s1, cs, heat, phase_out, solute_out, rims, sem):
    inner = pl.ds(1, CX - 2)
    copies = [
        pltpu.make_async_copy(o.at[pl.ds(0, ORDERS), inner], phase_out.at[:, inner], sem.at[0]),
        pltpu.make_async_copy(o.at[ORDERS, inner], solute_out.at[inner], sem.at[1]),
    ]
    for copy in copies:
        copy.start()
    has_up = lax.axis_index("gz") < lax.axis_size("gz") - 1
    for i, x in enumerate((0, CX - 1)):
        rim = rims.at[:, pl.ds(i, 1)]
        second_units(rim, s1, cs, heat, ((x, 0), (x, 1)), x)
        clear_top(rim, has_up)
        ends = [
            pltpu.make_async_copy(rims.at[pl.ds(0, ORDERS), i], phase_out.at[:, x], sem.at[2 + 2 * i]),
            pltpu.make_async_copy(rims.at[ORDERS, i], solute_out.at[x], sem.at[3 + 2 * i]),
        ]
        for copy in ends:
            copy.start()
        copies += ends
    for copy in copies:
        copy.wait()


def local(phase, solute, grain_map, frame_steps):
    hbm, vmem = pl.BlockSpec(memory_space=pltpu.HBM), pl.BlockSpec(memory_space=pltpu.VMEM)
    dma = pltpu.SemaphoreType.DMA
    args = [pltpu.with_memory_space_constraint(a, pltpu.HBM) for a in (frame_steps, phase, solute, grain_map)]
    results = pl.pallas_call(
        kernel,
        out_shape=(
            pltpu.VMEM((FIELDS, CX, CZ, NY), jnp.float32),
            pltpu.VMEM((FIELDS, CX + 2, YT, 24, LANES), jnp.float32),
            pltpu.VMEM((2, ORDERS, CX, YT, 24, LANES), jnp.float32),
            pltpu.VMEM((STEPS, 2, 1, 8, LANES), jnp.float32),
        ),
        in_specs=[hbm] * 4,
        out_specs=(vmem,) * 4,
        scratch_shapes=[
            pltpu.VMEM((FIELDS, CX + 2, YT, 32, LANES), jnp.float32),
            pltpu.VMEM((ORDERS, CX, YT, CZ, LANES), jnp.int32),
            pltpu.VMEM((ORDERS, CX, NY), jnp.int32),
            pltpu.SMEM((STEPS,), jnp.int32),
            dma((3, YT)),
            dma,
            dma((STEPS, 2, 4)),
            dma((STEPS, 2, 4)),
            dma((2, GROUPS)),
            dma((2, GROUPS)),
            dma((CX,)),
            dma((CX,)),
            dma,
            dma,
            dma((2,)),
            dma((2,)),
        ],
        compiler_params=pltpu.CompilerParams(
            collective_id=0, has_side_effects=True, vmem_limit_bytes=32 * 1024 * 1024
        ),
        name="grow",
    )(*args)
    return pl.pallas_call(
        finish,
        out_shape=(
            pltpu.HBM(phase.shape, jnp.float32),
            pltpu.HBM(solute.shape, jnp.float32),
        ),
        in_specs=[vmem] * 4,
        out_specs=(hbm, hbm),
        scratch_shapes=[pltpu.VMEM((FIELDS, 2, CZ, NY), jnp.float32), dma((6,))],
        compiler_params=pltpu.CompilerParams(vmem_limit_bytes=16 * 1024 * 1024),
        name="finish",
    )(*results)


def solution(mesh):
    in_specs = (P(None, "gx", "gz", None), P("gx", "gz", None), P(None, "gx", "gz", None), P())
    out_specs = (P(None, "gx", "gz", None), P("gx", "gz", None))
    return jax.shard_map(local, mesh=mesh, in_specs=in_specs, out_specs=out_specs, check_vma=False)
```
